128 devices in a mesh: gx: 16 (over y, z), gy: 8 (over x, core).
Axes of the slice: x: 4, y: 4, z: 4, core: 2. Of those that a mesh axis runs over, the one named last changes fastest.
Arguments:
- starting_wetness: float32 [32, 1024, 1024], P(None, 'gx', 'gy'), may hold values from 0.05 to 0.95
- surface_inflow: float32 [1024, 1024], P('gx', 'gy'), may hold values from 0 to 0.2
- category_permeability: float32 [12], replicated, may hold values from 0.01 to 0.09
- earth_category: int32 [1024, 1024], P('gx', 'gy'), may hold values from 0 to 11
- thermal_state: float32 [1024, 1024], P('gx', 'gy'), may hold values from 0.8 to 1.2
- sensor_patch_coefficients: bfloat16 [4096, 4, 128, 128], P(('gx', 'gy')), may hold values from -0.25 to 0.25
- patch_device_slot: int32 [4096, 4], P(('gx', 'gy')), may hold values from 0 to 127, all different within a row; in each aligned block of 32 rows (0 to 31, 32 to 63, ...) at most 4 rows name the same one
- patch_strip_number: int32 [4096, 4], P(('gx', 'gy')), may hold values from 0 to 63
- measured_radiance: float32 [4096, 128], P(('gx', 'gy')), may hold values from -6 to 6
Outputs:
- moisture: float32 [32, 1024, 1024], P(None, 'gx', 'gy')
- brightness: float32 [4096, 128], P(('gx', 'gy'))
- grad_top: float32 [2, 1024, 1024], P(None, 'gx', 'gy')
The draws below stay inside these ranges and needn't reach their ends.
Inputs may be any that keep to these rules, and one draw needn't show every extreme that they name: `patch_device_slot`: each footprint block names 4 different tiles; the footprint blocks of one device name one tile at most 4 times, and exactly 4 times on some device.
All inputs are finite; a program needn't handle non-finite values.
Results may differ from the reference program's by a relative error of at most 0.0032.
Values may be sent and summed in bfloat16 or wider, within the bound.
No kernel may reach another device: no remote copies, remote signals or barrier semaphores. Data moves between devices by JAX's collectives and lax.ppermute only.
A program may use at most 64 MiB of HBM per device.

```python
import math
import jax
import jax.numpy as jnp
import numpy as np
from jax import lax

L = 32
CX = 64
CY = 128
FOOT = 128
NNZ = 4
CAP = 4
FB_DEV = 32
NCLASS = 12
STEPS = 4
LATTICE_HEIGHT = 1024
LATTICE_WIDTH = 1024
NFB = 4096
N_GX = 16
N_GY = 8
DEVICES = 128


def place_ends(values, stream_key, low, high):
    longest = values.shape.index(max(values.shape))
    spots = []
    for shift in (0, 1):
        where = [jax.random.randint(jax.random.fold_in(stream_key, axis), (), 0, length) for axis, length in enumerate(values.shape)]
        where[longest] = (where[longest] + shift) % values.shape[longest]
        spots.append(tuple(where))
    return values.at[spots[0]].set(low).at[spots[1]].set(high)


def level_of(key, extent, split, smallest, largest):
    loudness = 1.0
    for axis_at, parts in split:
        draws = jax.random.uniform(jax.random.fold_in(jax.random.fold_in(key, 6), axis_at), (parts,), jnp.float32, smallest / len(split), largest / len(split))
        loudness = loudness * jnp.repeat(jnp.exp(draws), extent[axis_at] // parts).reshape((-1,) + (1,) * (len(extent) - 1 - axis_at))
    return loudness


def assign_block(key, own, number, rows, number_of, top, reach, slope):
    sequence = jax.random.permutation(key, number_of)
    crowded, common = shares(number_of, rows * top, reach, slope, True), shares(number_of, rows * top, reach, slope, False)
    places = jnp.arange(number_of)

    def named(tallies, turn):
        used = int((tallies > 0).sum())
        fixed = max(1, used // 4)
        passed = fixed + (places - fixed + turn * (used - fixed)) % max(1, number_of - fixed)
        return jnp.zeros((number_of,), jnp.int32).at[sequence[jnp.where(places < fixed, places, passed)]].set(jnp.asarray(tallies, jnp.int32))

    tallies = jnp.where(number % 4 == 0, named(crowded, number // 4), named(common, number - number // 4 - 1))
    mixed = jax.random.permutation(jax.random.fold_in(own, 3), number_of)
    source_of, sink = mixed[0:number_of // 2 * 2:2], mixed[1:number_of // 2 * 2:2]
    room = jnp.minimum(tallies[source_of] - 1, reach - tallies[sink]) // 2
    room = jnp.where((source_of == sequence[0]) | (sink == sequence[0]) | (tallies[sink] == 0), 0, jnp.maximum(room, 0))
    passed = jax.random.randint(jax.random.fold_in(own, 4), (number_of // 2,), 0, 1 << 20) % (room + 1)
    tallies = tallies.at[source_of].add(-passed).at[sink].add(passed)
    members = jnp.searchsorted(jnp.cumsum(tallies), jnp.arange(rows * top), side="right").astype(jnp.int32)
    listing = members.reshape(top, rows).T
    listing = listing[jax.random.permutation(jax.random.fold_in(own, 1), rows)]
    turn = jax.random.randint(jax.random.fold_in(own, 2), (rows, 1), 0, top)
    return jnp.take_along_axis(listing, (jnp.arange(top)[None, :] + turn) % top, axis=1)


def shares(number_of, total, reach, lean, full):
    portions = [(1 << 20) // math.isqrt(standing ** lean) + 1 for standing in range(1, number_of + 1)]
    largest = reach if full else min(reach, max(-(-total // number_of), total * portions[0] // sum(portions)))
    least = 1 if total - largest >= number_of - 1 else 0
    counts, surplus = [largest] + [least] * (number_of - 1), total - largest - least * (number_of - 1)
    while surplus > 0:
        free = [i for i in range(1, number_of) if counts[i] < largest] or [i for i in range(1, number_of) if counts[i] < reach]
        pool, left = sum([portions[i] for i in free]), surplus
        for i in free:
            extra = min(reach - counts[i], max(1, left * portions[i] // pool), surplus)
            counts[i] = counts[i] + extra
            surplus = surplus - extra
    return np.array(counts)


def noise(own_key, extent, spread, reach, shards=(), kind=jnp.bfloat16):
    entries = jax.random.normal(own_key, extent, jnp.float32) * spread
    if len(shards) > 0:
        entries = level_of(own_key, extent, shards, -0.22, 0.18) * entries
    return jnp.clip(entries, min=-reach, max=reach).astype(kind)


def setup_inputs(seed: int = 0) -> dict:
    splits = jax.random.split(jax.random.key(seed), 10)
    starting_wetness = jnp.clip(0.05 + 0.9 * jax.random.uniform(splits[0], (L, LATTICE_HEIGHT, LATTICE_WIDTH), jnp.float32) ** level_of(splits[0], (L, LATTICE_HEIGHT, LATTICE_WIDTH), ((1, 16), (2, 8)), -0.2, 0.2), 0.05, 0.95)
    surface_inflow = jnp.clip(0.2 * jax.random.uniform(splits[1], (LATTICE_HEIGHT, LATTICE_WIDTH), jnp.float32) ** level_of(splits[1], (LATTICE_HEIGHT, LATTICE_WIDTH), ((0, 16), (1, 8)), -0.2, 0.2), 0.0, 0.2)
    category_permeability = jnp.clip(jnp.exp(jax.random.uniform(splits[2], (NCLASS,), jnp.float32, math.log(0.01), math.log(0.09))), 0.01, 0.09)
    earth_category = place_ends(jax.random.randint(splits[3], (LATTICE_HEIGHT, LATTICE_WIDTH), 0, NCLASS), jax.random.fold_in(splits[3], 1), 0, NCLASS - 1).astype(jnp.int32)
    thermal_state = jnp.clip(0.8 + 0.40000004 * jax.random.uniform(splits[4], (LATTICE_HEIGHT, LATTICE_WIDTH), jnp.float32) ** level_of(splits[4], (LATTICE_HEIGHT, LATTICE_WIDTH), ((0, 16), (1, 8)), -0.2, 0.2), 0.8, 1.2)
    sensor_patch_coefficients = noise(splits[5], (NFB, NNZ, FOOT, CY), (NNZ * CY) ** -0.5, 0.25, ((0, 128),))
    patch_device_slot_keys = jax.random.split(jax.random.fold_in(splits[6], 1), NFB // FB_DEV)
    patch_device_slot_turns = jax.random.permutation(jax.random.fold_in(splits[6], 3), NFB // FB_DEV)
    patch_device_slot = jax.vmap(lambda own, number: assign_block(jax.random.fold_in(splits[6], 2), own, number, FB_DEV, DEVICES, NNZ, CAP, 2))(patch_device_slot_keys, patch_device_slot_turns).reshape((NFB, NNZ))
    patch_strip_number = place_ends(jax.random.randint(splits[7], (NFB, NNZ), 0, CX), jax.random.fold_in(splits[7], 1), 0, CX - 1).astype(jnp.int32)
    measured_radiance = noise(splits[8], (NFB, FOOT), 1.0, 6.0, ((0, 128),), jnp.float32)
    return {"starting_wetness": starting_wetness, "surface_inflow": surface_inflow, "category_permeability": category_permeability, "earth_category": earth_category, "thermal_state": thermal_state, "sensor_patch_coefficients": sensor_patch_coefficients, "patch_device_slot": patch_device_slot, "patch_strip_number": patch_strip_number, "measured_radiance": measured_radiance}


def substep(state, conduct_col):
    conduct = conduct_col[None] * (0.5 + state)
    padded = jnp.pad(state, ((0, 0), (1, 1), (1, 1)))
    kpadded = jnp.pad(conduct, ((0, 0), (1, 1), (1, 1)))
    change = jnp.zeros_like(state)
    for near_s, near_k in ((padded[:, 2:, 1:-1], kpadded[:, 2:, 1:-1]), (padded[:, :-2, 1:-1], kpadded[:, :-2, 1:-1]), (padded[:, 1:-1, 2:], kpadded[:, 1:-1, 2:]), (padded[:, 1:-1, :-2], kpadded[:, 1:-1, :-2])):
        change = change + 0.5 * (conduct + near_k) * (near_s - state)
    flux_down = 0.5 * (conduct[:-1] + conduct[1:]) * (state[:-1] - state[1:] + 0.3)
    change = change + jnp.pad(-flux_down, ((0, 1), (0, 0), (0, 0))) + jnp.pad(flux_down, ((1, 0), (0, 0), (0, 0)))
    return state + change


def reference(starting_wetness, surface_inflow, category_permeability, earth_category, thermal_state, sensor_patch_coefficients, patch_device_slot, patch_strip_number, measured_radiance):
    classes = jnp.arange(NCLASS, dtype=jnp.int32)
    conduct_col = jnp.sum(jnp.where(earth_category[None] == classes[:, None, None], category_permeability[:, None, None], jnp.float32(0.0)), axis=0)
    state = starting_wetness.at[0].add(surface_inflow)
    for step in range(STEPS):
        state = substep(state, conduct_col)
    combined_average = 0.6 * state[0] + 0.4 * state[1]
    radiance_map = (thermal_state * (1.0 - 0.4 * combined_average * combined_average)).astype(jnp.bfloat16)
    blocks = radiance_map.reshape(N_GX, CX, N_GY, CY).transpose(0, 2, 1, 3).reshape(N_GX * N_GY * CX, CY)
    block_ids = (patch_device_slot * CX + patch_strip_number).astype(jnp.int32)
    touched = blocks[block_ids]
    ndev = N_GX * N_GY
    weights_own = sensor_patch_coefficients.reshape(ndev, FB_DEV, NNZ, FOOT, CY)
    touched_own = touched.reshape(ndev, FB_DEV, NNZ, CY)
    observed_own = measured_radiance.reshape(ndev, FB_DEV, FOOT)

    def owner_work(items):
        weights, cells, seen = items
        wf = weights.astype(jnp.float32)
        evolved = jnp.einsum('bnfc,bnc->bf', wf, cells.astype(jnp.float32))
        misfit = (evolved - seen).astype(jnp.bfloat16)
        contrib = jnp.einsum('bnfc,bf->bnc', wf, misfit.astype(jnp.float32))
        return evolved, contrib

    evolved, contrib = lax.map(owner_work, (weights_own, touched_own, observed_own))
    brightness = evolved.reshape(NFB, FOOT)
    grad_blocks = jnp.zeros((ndev * CX, CY), jnp.float32).at[block_ids.reshape(-1)].add(contrib.reshape(-1, CY))
    sensitivity_by_location = grad_blocks.reshape(N_GX, N_GY, CX, CY).transpose(0, 2, 1, 3).reshape(N_GX * CX, N_GY * CY)
    common_portion = sensitivity_by_location * thermal_state * (-0.8 * combined_average)
    grad_top = jnp.stack([0.6 * common_portion, 0.4 * common_portion])
    return state, brightness, grad_top
```

```python
import jax
import jax.numpy as jnp
from jax import lax
from jax.experimental import pallas as pl
from jax.experimental.pallas import tpu as pltpu
from jax.sharding import PartitionSpec as P

CAP = 4
STEPS = 4
L = 32
ROWS = 64
COLS = 128
WIDE = ROWS + 8
TILES = 128
SLOTS = TILES * CAP
OWN = 32
TOUCH = 4
REFS = OWN * TOUCH
FOOT = 128
F32 = jnp.float32
BF16 = jnp.bfloat16
VMEM = pl.BlockSpec(memory_space=pltpu.VMEM)
SMEM = pl.BlockSpec(memory_space=pltpu.SMEM)
ANY = pl.BlockSpec(memory_space=pl.ANY)
HBM = pl.BlockSpec(memory_space=pltpu.HBM)
LIMIT = 32 * 1024 * 1024


def call(body, outs, in_specs, name, scratch=(), out_specs=None, aliases=None, flops=0, moved=0):
    return pl.pallas_call(
        body,
        out_shape=outs,
        in_specs=in_specs,
        out_specs=out_specs or jax.tree.map(lambda _: VMEM, outs),
        input_output_aliases=aliases or {},
        scratch_shapes=list(scratch),
        name=name,
        compiler_params=pltpu.CompilerParams(vmem_limit_bytes=LIMIT),
        cost_estimate=pl.CostEstimate(flops=flops, bytes_accessed=moved, transcendentals=0),
    )


def iota(shape, dim):
    return lax.broadcasted_iota(jnp.int32, shape, dim)


def dot(a, b, ca, cb):
    return lax.dot_general(a, b, (((ca,), (cb,)), ((), ())), preferred_element_type=F32)


def prep_body(
    classes_ref, inflow_hbm, category_hbm, state_hbm,
    state_ref, conduct_ref, edge_ref, inflow_ref, category_ref, sems,
):
    copies = [
        pltpu.make_async_copy(category_hbm, category_ref, sems.at[0]),
        pltpu.make_async_copy(inflow_hbm, inflow_ref, sems.at[1]),
        pltpu.make_async_copy(state_hbm, state_ref, sems.at[2]),
    ]
    for copy in copies:
        copy.start()
    copies[0].wait()
    category = category_ref[...]
    conduct = jnp.zeros((ROWS, COLS), F32)
    for i in range(classes_ref.shape[0]):
        conduct = jnp.where(category == i, classes_ref[i], conduct)
    conduct_ref[...] = conduct
    copies[1].wait()
    copies[2].wait()
    state_ref[0] = state_ref[0] + inflow_ref[...]
    upper = iota((8, COLS), 0) < 4
    edges = jnp.where(upper[None], state_ref[:, 0:8, :], state_ref[:, ROWS - 8 : ROWS, :])
    ends = jnp.where(upper, conduct[0:8], conduct[ROWS - 8 : ROWS])[None]
    whole = jnp.concatenate([edges, ends, jnp.zeros((1, 8, COLS), F32)], axis=0)
    edge_ref[...] = whole.reshape((L + 2) * 8, COLS).astype(BF16)


def request_body(slot_hbm, strip_hbm, after_ref, placing_ref, request_ref, slot_ref, strip_ref, sems):
    copies = [
        pltpu.make_async_copy(slot_hbm, slot_ref, sems.at[0]),
        pltpu.make_async_copy(strip_hbm, strip_ref, sems.at[1]),
    ]
    for copy in copies:
        copy.start()
    for copy in copies:
        copy.wait()
    tile = jnp.concatenate([slot_ref[k : k + 1, :] for k in range(TOUCH)], axis=1)
    row = jnp.concatenate([strip_ref[k : k + 1, :] for k in range(TOUCH)], axis=1)
    sub = iota((TILES, REFS), 0)
    named = (sub == tile).astype(F32)
    before = (sub < iota((REFS, REFS), 1)).astype(F32).astype(BF16)
    rank = jnp.sum(dot(named.astype(BF16), before, 1, 0) * named, axis=0, keepdims=True)
    place = tile * CAP + rank.astype(jnp.int32)
    placing = (iota((SLOTS, REFS), 0) == place).astype(F32).astype(BF16)
    placing_ref[...] = placing
    wanted = (sub == row).astype(F32).astype(BF16)
    request_ref[...] = dot(placing, wanted, 1, 1).astype(BF16)


def row_halo(a_ref, b_ref, levels=L + 1):
    odd = lax.rem(lax.axis_index("gx"), 2)
    a = a_ref[...].astype(F32).reshape(L + 2, 8, COLS)
    b = b_ref[...].astype(F32).reshape(L + 2, 8, COLS)
    half = lax.div(iota((8, COLS), 0), 4)
    return jnp.where((half == odd)[None], a, b)


def halo_rows_inside():
    gx = lax.axis_index("gx")
    sub = iota((8, COLS), 0)
    below = (gx < lax.axis_size("gx") - 1).astype(jnp.int32)
    above = (gx > 0).astype(jnp.int32)
    return jnp.where(sub < 4, below, above) > 0


def held(new, inside):
    return jnp.concatenate([new[:ROWS], jnp.where(inside, new[ROWS:], 0.5)], axis=0)


def rows_change(u, k, cd):
    ud = pltpu.roll(u, WIDE - 1, 0)
    f = (k + cd * ud) * (ud - u)
    return f - pltpu.roll(f, 1, 0)


def lanes_change(u, k, cr):
    ur = pltpu.roll(u, COLS - 1, 1)
    f = (k + cr * ur) * (ur - u)
    return f - pltpu.roll(f, 1, 1)


def pack_body(state_ref, conduct_ref, a_ref, b_ref, own_ref, cond_ref, pa_ref, pb_ref):
    halo = row_halo(a_ref, b_ref)
    lane64 = iota((ROWS, COLS), 1)
    lane8 = iota((8, COLS), 1)
    shifts = (0, -4, 4, 8)

    def pack(levels_of, lane):
        acc = [jnp.zeros(lane.shape, F32) for _ in range(4)]
        for l in range(L):
            turned = levels_of(l)
            if l:
                turned = pltpu.roll(turned, 4 * l, 1)
            group = lane // 4
            for i, at in enumerate((l, (l + 1) % L, (l - 1) % L, (l - 2) % L)):
                acc[i] = jnp.where(group == at, turned, acc[i])
        return [pltpu.roll(x, s % COLS, 1) if s else x for x, s in zip(acc, shifts)]

    def spread(x, lane):
        out = []
        for s in (0, COLS - 4, 4, 8):
            y = jnp.where(lane < 4, pltpu.roll(x, s, 1) if s else x, 0.0)
            for d in (4, 8, 16, 32, 64):
                y = y + pltpu.roll(y, d, 1)
            out.append(y)
        return out

    main = pack(lambda l: state_ref[l], lane64)
    ends = pack(lambda l: halo[l], lane8)
    cmain = spread(conduct_ref[...], lane64)
    cends = spread(halo[L], lane8)
    packs = [jnp.concatenate([m, e], axis=0) for m, e in zip(main, ends)]
    conds = [jnp.concatenate([m, e], axis=0) for m, e in zip(cmain, cends)]
    for i in range(4):
        own_ref[i] = packs[i]
        cond_ref[i] = conds[i]
    odd = lax.rem(lax.axis_index("gy"), 2)
    left = jnp.concatenate([packs[0], conds[0]], axis=0)
    right = jnp.concatenate([packs[2], conds[2]], axis=0)
    is_odd = (jnp.zeros((2 * WIDE, COLS), jnp.int32) + odd) > 0
    pa_ref[...] = jnp.where(is_odd, left, right).astype(BF16)
    pb_ref[...] = jnp.where(is_odd, right, left).astype(BF16)


def strip_body(
    own_ref, cond_ref, pa_ref, pb_ref, tops_ref, thermal_ref, picker_ref,
    left_ref, right_ref, adjoint_ref, served_ref, u_ref, c_ref, cd_ref, cr_ref,
):
    gy = lax.axis_index("gy")
    odd = lax.rem(gy, 2)
    a = pa_ref[...].astype(F32)
    b = pb_ref[...].astype(F32)
    is_odd = (jnp.zeros((2 * WIDE, COLS), jnp.int32) + odd) > 0
    from_right = jnp.where(is_odd, b, a)
    from_left = jnp.where(is_odd, a, b)
    lane = iota((WIDE, COLS), 1)
    last = lax.rem(lane, 4) == 3
    first = lax.rem(lane, 4) == 0
    lowest = lane >= COLS - 4
    inside = halo_rows_inside()
    in_left = (jnp.zeros((WIDE, COLS), jnp.int32) + gy) > 0
    in_right = (jnp.zeros((WIDE, COLS), jnp.int32) + gy) < lax.axis_size("gy") - 1
    sources = (
        (from_left[:WIDE], from_left[WIDE:]),
        (own_ref[0], cond_ref[0]),
        (own_ref[1], cond_ref[1]),
        (own_ref[3], cond_ref[3]),
        (own_ref[2], cond_ref[2]),
        (from_right[:WIDE], from_right[WIDE:]),
    )
    for i, (s, c) in enumerate(sources):
        u_ref[i] = s + 0.5
        c_ref[i] = 0.5 * c

    def next_of(ref, i):
        x = pltpu.roll(ref[i], COLS - 1, 1)
        y = pltpu.roll(ref[min(i + 1, i // 3 * 3 + 2)], 3, 1)
        return jnp.where(last, y, x)

    for i in range(6):
        cd_ref[i] = pltpu.roll(c_ref[i], WIDE - 1, 0)
        cr_ref[i] = next_of(c_ref, i)

    for step in range(STEPS):
        fresh = []
        flux = None
        for i in range(6):
            u, c = u_ref[i], c_ref[i]
            k = c * u
            change = rows_change(u, k, cd_ref[i])
            ur = next_of(u_ref, i)
            f = (k + cr_ref[i] * ur) * (ur - u)
            before = pltpu.roll(f, 1, 1)
            if i % 3:
                before = jnp.where(first, pltpu.roll(flux, COLS - 3, 1), before)
            flux = f
            change = change + (f - before)
            uz = pltpu.roll(u, COLS - 4, 1)
            down = jnp.where(lowest, 0.0, (k + c * uz) * ((u - uz) + 0.3))
            change = change + (pltpu.roll(down, 4, 1) - down)
            new = held(u + change, inside)
            if i == 0:
                new = jnp.where(in_left, new, 0.5)
            if i == 5:
                new = jnp.where(in_right, new, 0.5)
            fresh.append(new)
        for i in range(6):
            u_ref[i] = fresh[i]
    left = u_ref[1][:ROWS] - 0.5
    right = u_ref[4][:ROWS] - 0.5
    left_ref[...] = left
    right_ref[...] = right
    lane = iota((ROWS, COLS), 1)

    def joined(l):
        lhs = pltpu.roll(left, COLS - 4 * l, 1) if l else left
        rhs = pltpu.roll(right, COLS - 4 - 4 * l, 1)
        return jnp.where(lane < 4, lhs, jnp.where(lane >= COLS - 4, rhs, tops_ref[l]))

    mix = 0.6 * joined(0) + 0.4 * joined(1)
    thermal = thermal_ref[...]
    bright = (thermal * (1.0 - 0.4 * mix * mix)).astype(BF16)
    adjoint_ref[...] = thermal * (-0.8 * mix)
    bright = jnp.concatenate([bright, jnp.zeros((COLS - ROWS, COLS), BF16)], axis=0)
    served_ref[...] = dot(picker_ref[...], bright, 1, 0).astype(BF16)


def wide_conduct(conduct_ref, halo):
    return 0.5 * jnp.concatenate([conduct_ref[...], halo[L]], axis=0)


def evolve(state_ref, conduct_ref, a_ref, b_ref, u_ref, c_ref, low, high, finish):
    halo = row_halo(a_ref, b_ref)
    c = wide_conduct(conduct_ref, halo)
    c_ref[0] = c
    c_ref[1] = pltpu.roll(c, WIDE - 1, 0)
    c_ref[2] = pltpu.roll(c, COLS - 1, 1)
    inside = halo_rows_inside()
    start, stop = max(0, low - STEPS), min(L, high + STEPS)
    for l in range(start, stop):
        u_ref[l - start] = jnp.concatenate([state_ref[l], halo[l]], axis=0) + 0.5
    for step in range(STEPS):
        top = max(0, low - (STEPS - 1 - step))
        end = min(L, high + (STEPS - 1 - step))
        above = None
        if top > 0:
            u, uz = u_ref[top - 1 - start], u_ref[top - start]
            above = c_ref[0] * (u + uz) * ((u - uz) + 0.3)
        u = u_ref[top - start]
        k = c_ref[0] * u
        for l in range(top, end):
            change = rows_change(u, k, c_ref[1]) + lanes_change(u, k, c_ref[2])
            if above is not None:
                change = change + above
            if l < L - 1:
                uz = u_ref[l + 1 - start]
                kz = c_ref[0] * uz
                above = (k + kz) * ((u - uz) + 0.3)
                change = change - above
            new = u + change
            if step < STEPS - 1:
                u_ref[l - start] = held(new, inside)
            else:
                finish(l, new[:ROWS] - 0.5)
            u, k = uz, kz


def tops_body(state_ref, conduct_ref, a_ref, b_ref, tops_ref, u_ref, c_ref):
    def finish(l, new):
        tops_ref[l] = new

    evolve(state_ref, conduct_ref, a_ref, b_ref, u_ref, c_ref, 0, 2, finish)


HALF = L // 2
PIECE = 4


def half_body(low, state_ref, conduct_ref, a_ref, b_ref, left_ref, right_ref, out_hbm, done_ref, u_ref, c_ref, own_ref, sems):
    lane = iota((ROWS, COLS), 1)
    copies = []

    def finish(l, new):
        lhs = pltpu.roll(left_ref[...], (COLS - 4 * l) % COLS, 1) if l else left_ref[...]
        turn = (COLS - 4 - 4 * l) % COLS
        rhs = pltpu.roll(right_ref[...], turn, 1) if turn else right_ref[...]
        own_ref[l - low] = jnp.where(lane < 4, lhs, jnp.where(lane >= COLS - 4, rhs, new))
        if (l + 1) % PIECE == 0:
            at = l + 1 - PIECE
            copy = pltpu.make_async_copy(
                own_ref.at[pl.ds(at - low, PIECE)], out_hbm.at[pl.ds(at, PIECE)], sems.at[len(copies)]
            )
            copy.start()
            copies.append(copy)

    evolve(state_ref, conduct_ref, a_ref, b_ref, u_ref, c_ref, low, low + HALF, finish)
    if done_ref is not None:
        done_ref[...] = jnp.zeros(done_ref.shape, F32)
    for copy in copies:
        copy.wait()


def upper_body(state_ref, conduct_ref, a_ref, b_ref, left_ref, right_ref, out_hbm, done_ref, *scratch):
    half_body(0, state_ref, conduct_ref, a_ref, b_ref, left_ref, right_ref, out_hbm, done_ref, *scratch)


def lower_body(state_ref, conduct_ref, a_ref, b_ref, left_ref, right_ref, begun_hbm, out_hbm, *scratch):
    half_body(HALF, state_ref, conduct_ref, a_ref, b_ref, left_ref, right_ref, out_hbm, None, *scratch)


def foot_body(
    returned_ref, placing_ref, after_ref, measured_hbm, weights_ref,
    bright_ref, outgoing_ref, measured_ref, held_ref, cells_ref, seen_ref, misfit_ref, contrib_ref, sems,
):
    parts = 8
    each = OWN // parts
    seen_copy = pltpu.make_async_copy(measured_hbm, measured_ref, sems.at[parts])
    seen_copy.start()
    copies = [
        pltpu.make_async_copy(
            weights_ref.at[pl.ds(p * each, each)], held_ref.at[pl.ds(p * each, each)], sems.at[p]
        )
        for p in range(parts)
    ]
    for copy in copies:
        copy.start()
    placing = placing_ref[...]
    cells_ref[...] = dot(placing, returned_ref[...], 0, 0)
    seen_copy.wait()
    seen = jnp.concatenate([measured_ref[...], jnp.zeros((COLS - OWN, FOOT), F32)], axis=0)
    seen_ref[...] = jnp.transpose(seen)
    misfit_ref[...] = jnp.zeros((FOOT, COLS), F32)
    lane = iota((FOOT, COLS), 1)

    def block(b, carry):
        total = jnp.where(lane == b, -seen_ref[...], 0.0)
        for k in range(TOUCH):
            total = total + held_ref[b, k].astype(F32) * cells_ref[pl.ds(k * OWN + b, 1), :]
        misfit = jnp.sum(total, axis=1, keepdims=True)
        misfit_ref[...] = jnp.where(lane == b, misfit, misfit_ref[...])
        rounded = misfit.astype(BF16).astype(F32)
        for k in range(TOUCH):
            contrib_ref[pl.ds(k * OWN + b, 1), :] = jnp.sum(
                held_ref[b, k].astype(F32) * rounded, axis=0, keepdims=True
            )
        return carry

    for p in range(parts):
        copies[p].wait()
        for b in range(p * each, (p + 1) * each):
            block(b, 0)
    evolved = jnp.transpose(misfit_ref[...] + seen_ref[...])
    bright_ref[...] = evolved[:OWN]
    outgoing_ref[...] = dot(placing, contrib_ref[...].astype(BF16), 1, 0).astype(BF16)


def gradient_body(grads_ref, picker_ref, adjoint_ref, out_ref):
    summed = dot(picker_ref[...], grads_ref[...], 0, 0)[:ROWS]
    common = summed * adjoint_ref[...]
    out_ref[0] = 0.6 * common
    out_ref[1] = 0.4 * common


def swapped(x, axis):
    n = lax.axis_size(axis)
    one = [(i, i ^ 1) for i in range(n)]
    two = [(i, i + 1) for i in range(1, n - 1, 2)] + [(i + 1, i) for i in range(1, n - 1, 2)]
    return lax.ppermute(x[0], axis, one), lax.ppermute(x[1], axis, two)


def exchange(x):
    return lax.all_to_all(
        x.reshape(TILES, CAP, COLS), ("gx", "gy"), split_axis=0, concat_axis=0, tiled=True
    ).reshape(SLOTS, COLS)


def on_device(state, inflow, classes, category, thermal, weights, slots, strips, measured):
    def sds(*shape, dtype=F32):
        return jax.ShapeDtypeStruct(shape, dtype)

    held_state, conduct, edge = call(
        prep_body,
        (sds(L, ROWS, COLS), sds(ROWS, COLS), sds((L + 2) * 8, COLS, dtype=BF16)),
        [SMEM, HBM, HBM, HBM],
        "prep",
        [pltpu.VMEM((ROWS, COLS), F32), pltpu.VMEM((ROWS, COLS), jnp.int32), pltpu.SemaphoreType.DMA((3,))],
        flops=1_000_000, moved=2_000_000,
    )(classes, inflow, category, state)
    xa, xb = swapped((edge, edge), "gx")
    placing, request = call(
        request_body,
        (sds(SLOTS, REFS, dtype=BF16), sds(SLOTS, COLS, dtype=BF16)),
        [HBM, HBM, ANY],
        "requests",
        [pltpu.VMEM((TOUCH, OWN), jnp.int32), pltpu.VMEM((TOUCH, OWN), jnp.int32), pltpu.SemaphoreType.DMA((2,))],
        flops=20_000_000, moved=500_000,
    )(slots.T, strips.T, conduct)
    picker = exchange(request)
    own, cond, pa, pb = call(
        pack_body,
        (sds(4, WIDE, COLS), sds(4, WIDE, COLS), sds(2 * WIDE, COLS, dtype=BF16), sds(2 * WIDE, COLS, dtype=BF16)),
        [VMEM] * 4,
        "pack",
        flops=2_000_000, moved=1_500_000,
    )(held_state, conduct, xa, xb)
    ya, yb = swapped((pa, pb), "gy")
    tops = call(
        tops_body,
        sds(2, ROWS, COLS),
        [VMEM] * 4,
        "tops",
        [pltpu.VMEM((STEPS + 2, WIDE, COLS), F32), pltpu.VMEM((3, WIDE, COLS), F32)],
        flops=4_000_000, moved=1_000_000,
    )(held_state, conduct, xa, xb)
    left, right, adjoint, served = call(
        strip_body,
        (sds(ROWS, COLS), sds(ROWS, COLS), sds(ROWS, COLS), sds(SLOTS, COLS, dtype=BF16)),
        [VMEM] * 7,
        "strips",
        [pltpu.VMEM((6, WIDE, COLS), F32)] * 4,
        flops=20_000_000, moved=1_000_000,
    )(own, cond, ya, yb, tops, thermal, picker)
    returned = exchange(served)
    scratch = [
        pltpu.VMEM((HALF + STEPS, WIDE, COLS), F32),
        pltpu.VMEM((3, WIDE, COLS), F32),
        pltpu.VMEM((HALF, ROWS, COLS), F32),
        pltpu.SemaphoreType.DMA((HALF // PIECE,)),
    ]
    begun, done = call(
        upper_body,
        (sds(L, ROWS, COLS), sds(8, COLS)),
        [VMEM] * 6,
        "upper",
        scratch,
        out_specs=(HBM, VMEM),
        flops=500_000_000, moved=3_000_000,
    )(held_state, conduct, xa, xb, left, right)
    brightness, outgoing = call(
        foot_body,
        (sds(OWN, FOOT), sds(SLOTS, COLS, dtype=BF16)),
        [VMEM, VMEM, ANY, HBM, HBM],
        "footprints",
        [
            pltpu.VMEM((OWN, FOOT), F32),
            pltpu.VMEM((OWN, TOUCH, FOOT, COLS), BF16),
            pltpu.VMEM((REFS, COLS), F32),
            pltpu.VMEM((FOOT, COLS), F32),
            pltpu.VMEM((FOOT, COLS), F32),
            pltpu.VMEM((REFS, COLS), F32),
            pltpu.SemaphoreType.DMA((9,)),
        ],
        flops=20_000_000, moved=5_000_000,
    )(returned, placing, done, measured, weights)
    moisture = call(
        lower_body,
        sds(L, ROWS, COLS),
        [VMEM] * 6 + [HBM],
        "lower",
        scratch,
        out_specs=HBM,
        aliases={6: 0},
        flops=500_000_000, moved=3_000_000,
    )(held_state, conduct, xa, xb, left, right, begun)
    grads = exchange(outgoing)
    grad_top = call(
        gradient_body, sds(2, ROWS, COLS), [VMEM] * 3, "gradient", flops=20_000_000, moved=400_000
    )(grads, picker, adjoint)
    return moisture, brightness, grad_top


def solution(mesh):
    placed = (
        P(None, "gx", "gy"),
        P("gx", "gy"),
        P(),
        P("gx", "gy"),
        P("gx", "gy"),
        P(("gx", "gy"), None, None, None),
        P(("gx", "gy"), None),
        P(("gx", "gy"), None),
        P(("gx", "gy"), None),
    )
    return jax.shard_map(
        on_device,
        mesh=mesh,
        in_specs=placed,
        out_specs=(P(None, "gx", "gy"), P(("gx", "gy"), None), P(None, "gx", "gy")),
        check_vma=False,
    )
```

```python
import jax
import jax.numpy as jnp
from jax import lax
from jax.experimental import pallas as pl
from jax.experimental.pallas import tpu as pltpu
from jax.sharding import PartitionSpec as P

CAP = 4
STEPS = 4
L = 32
ROWS = 64
COLS = 128
WIDE = ROWS + 8
TILES = 128
SLOTS = TILES * CAP
OWN = 32
TOUCH = 4
REFS = OWN * TOUCH
FOOT = 128
F32 = jnp.float32
BF16 = jnp.bfloat16
VMEM = pl.BlockSpec(memory_space=pltpu.VMEM)
SMEM = pl.BlockSpec(memory_space=pltpu.SMEM)
ANY = pl.BlockSpec(memory_space=pl.ANY)
HBM = pl.BlockSpec(memory_space=pltpu.HBM)
LIMIT = 32 * 1024 * 1024


def call(body, outs, in_specs, name, scratch=(), out_specs=None, aliases=None, flops=0, moved=0):
    return pl.pallas_call(
        body,
        out_shape=outs,
        in_specs=in_specs,
        out_specs=out_specs or jax.tree.map(lambda _: VMEM, outs),
        input_output_aliases=aliases or {},
        scratch_shapes=list(scratch),
        name=name,
        compiler_params=pltpu.CompilerParams(vmem_limit_bytes=LIMIT),
        cost_estimate=pl.CostEstimate(flops=flops, bytes_accessed=moved, transcendentals=0),
    )


def iota(shape, dim):
    return lax.broadcasted_iota(jnp.int32, shape, dim)


def far(x):
    return pltpu.with_memory_space_constraint(x, pltpu.HBM)


def dot(a, b, ca, cb):
    return lax.dot_general(a, b, (((ca,), (cb,)), ((), ())), preferred_element_type=F32)


def prep_body(
    classes_ref, inflow_hbm, category_hbm, state_hbm, thermal_hbm,
    state_ref, conduct_ref, edge_ref, thermal_ref, inflow_ref, category_ref, sems,
):
    copies = [
        pltpu.make_async_copy(category_hbm, category_ref, sems.at[0]),
        pltpu.make_async_copy(inflow_hbm, inflow_ref, sems.at[1]),
        pltpu.make_async_copy(state_hbm, state_ref, sems.at[2]),
        pltpu.make_async_copy(thermal_hbm, thermal_ref, sems.at[3]),
    ]
    for copy in copies:
        copy.start()
    copies[0].wait()
    category = category_ref[...]
    conduct = jnp.zeros((ROWS, COLS), F32)
    for i in range(classes_ref.shape[0]):
        conduct = jnp.where(category == i, classes_ref[i], conduct)
    conduct_ref[...] = conduct
    copies[1].wait()
    copies[2].wait()
    state_ref[0] = state_ref[0] + inflow_ref[...]
    upper = iota((8, COLS), 0) < 4
    edges = jnp.where(upper[None], state_ref[:, 0:8, :], state_ref[:, ROWS - 8 : ROWS, :])
    ends = jnp.where(upper, conduct[0:8], conduct[ROWS - 8 : ROWS])[None]
    whole = jnp.concatenate([edges, ends, jnp.zeros((1, 8, COLS), F32)], axis=0)
    edge_ref[...] = whole.reshape((L + 2) * 8, COLS).astype(BF16)
    copies[3].wait()


def request_body(slot_hbm, strip_hbm, after_ref, placing_ref, request_ref, slot_ref, strip_ref, sems):
    copies = [
        pltpu.make_async_copy(slot_hbm, slot_ref, sems.at[0]),
        pltpu.make_async_copy(strip_hbm, strip_ref, sems.at[1]),
    ]
    for copy in copies:
        copy.start()
    for copy in copies:
        copy.wait()
    tile = jnp.concatenate([slot_ref[k : k + 1, :] for k in range(TOUCH)], axis=1)
    row = jnp.concatenate([strip_ref[k : k + 1, :] for k in range(TOUCH)], axis=1)
    sub = iota((TILES, REFS), 0)
    named = (sub == tile).astype(F32)
    before = (sub < iota((REFS, REFS), 1)).astype(F32).astype(BF16)
    rank = jnp.sum(dot(named.astype(BF16), before, 1, 0) * named, axis=0, keepdims=True)
    place = tile * CAP + rank.astype(jnp.int32)
    placing = (iota((SLOTS, REFS), 0) == place).astype(F32).astype(BF16)
    placing_ref[...] = placing
    wanted = (sub == row).astype(F32).astype(BF16)
    request_ref[...] = dot(placing, wanted, 1, 1).astype(BF16)


def row_halo(a_ref, b_ref, levels=L + 1):
    odd = lax.rem(lax.axis_index("gx"), 2)
    a = a_ref[...].astype(F32).reshape(L + 2, 8, COLS)
    b = b_ref[...].astype(F32).reshape(L + 2, 8, COLS)
    half = lax.div(iota((8, COLS), 0), 4)
    return jnp.where((half == odd)[None], a, b)


def halo_rows_inside():
    gx = lax.axis_index("gx")
    sub = iota((8, COLS), 0)
    below = (gx < lax.axis_size("gx") - 1).astype(jnp.int32)
    above = (gx > 0).astype(jnp.int32)
    return jnp.where(sub < 4, below, above) > 0


def held(new, inside):
    return jnp.concatenate([new[:ROWS], jnp.where(inside, new[ROWS:], 0.5)], axis=0)


def rows_change(u, k, cd):
    ud = pltpu.roll(u, WIDE - 1, 0)
    f = (k + cd * ud) * (ud - u)
    return f - pltpu.roll(f, 1, 0)


def lanes_change(u, k, cr):
    ur = pltpu.roll(u, COLS - 1, 1)
    f = (k + cr * ur) * (ur - u)
    return f - pltpu.roll(f, 1, 1)


def pack_body(state_ref, conduct_ref, a_ref, b_ref, own_ref, cond_ref, pa_ref, pb_ref):
    halo = row_halo(a_ref, b_ref)
    lane64 = iota((ROWS, COLS), 1)
    lane8 = iota((8, COLS), 1)
    shifts = (0, -4, 4, 8)

    def pack(levels_of, lane):
        acc = [jnp.zeros(lane.shape, F32) for _ in range(4)]
        for l in range(L):
            turned = levels_of(l)
            if l:
                turned = pltpu.roll(turned, 4 * l, 1)
            group = lane // 4
            for i, at in enumerate((l, (l + 1) % L, (l - 1) % L, (l - 2) % L)):
                acc[i] = jnp.where(group == at, turned, acc[i])
        return [pltpu.roll(x, s % COLS, 1) if s else x for x, s in zip(acc, shifts)]

    def spread(x, lane):
        out = []
        for s in (0, COLS - 4, 4, 8):
            y = jnp.where(lane < 4, pltpu.roll(x, s, 1) if s else x, 0.0)
            for d in (4, 8, 16, 32, 64):
                y = y + pltpu.roll(y, d, 1)
            out.append(y)
        return out

    main = pack(lambda l: state_ref[l], lane64)
    ends = pack(lambda l: halo[l], lane8)
    cmain = spread(conduct_ref[...], lane64)
    cends = spread(halo[L], lane8)
    packs = [jnp.concatenate([m, e], axis=0) for m, e in zip(main, ends)]
    conds = [jnp.concatenate([m, e], axis=0) for m, e in zip(cmain, cends)]
    for i in range(4):
        own_ref[i] = packs[i]
        cond_ref[i] = conds[i]
    odd = lax.rem(lax.axis_index("gy"), 2)
    left = jnp.concatenate([packs[0], conds[0]], axis=0)
    right = jnp.concatenate([packs[2], conds[2]], axis=0)
    is_odd = (jnp.zeros((2 * WIDE, COLS), jnp.int32) + odd) > 0
    pa_ref[...] = jnp.where(is_odd, left, right).astype(BF16)
    pb_ref[...] = jnp.where(is_odd, right, left).astype(BF16)


def strip_body(
    own_ref, cond_ref, pa_ref, pb_ref, tops_ref, thermal_ref, picker_ref,
    left_ref, right_ref, adjoint_ref, served_ref, u_ref, c_ref, cd_ref, cr_ref,
):
    gy = lax.axis_index("gy")
    odd = lax.rem(gy, 2)
    a = pa_ref[...].astype(F32)
    b = pb_ref[...].astype(F32)
    is_odd = (jnp.zeros((2 * WIDE, COLS), jnp.int32) + odd) > 0
    from_right = jnp.where(is_odd, b, a)
    from_left = jnp.where(is_odd, a, b)
    lane = iota((WIDE, COLS), 1)
    last = lax.rem(lane, 4) == 3
    first = lax.rem(lane, 4) == 0
    lowest = lane >= COLS - 4
    inside = halo_rows_inside()
    in_left = (jnp.zeros((WIDE, COLS), jnp.int32) + gy) > 0
    in_right = (jnp.zeros((WIDE, COLS), jnp.int32) + gy) < lax.axis_size("gy") - 1
    sources = (
        (from_left[:WIDE], from_left[WIDE:]),
        (own_ref[0], cond_ref[0]),
        (own_ref[1], cond_ref[1]),
        (own_ref[3], cond_ref[3]),
        (own_ref[2], cond_ref[2]),
        (from_right[:WIDE], from_right[WIDE:]),
    )
    for i, (s, c) in enumerate(sources):
        u_ref[i] = s + 0.5
        c_ref[i] = 0.5 * c

    def next_of(ref, i):
        x = pltpu.roll(ref[i], COLS - 1, 1)
        y = pltpu.roll(ref[min(i + 1, i // 3 * 3 + 2)], 3, 1)
        return jnp.where(last, y, x)

    for i in range(6):
        cd_ref[i] = pltpu.roll(c_ref[i], WIDE - 1, 0)
        cr_ref[i] = next_of(c_ref, i)

    for step in range(STEPS):
        fresh = []
        flux = None
        for i in range(6):
            u, c = u_ref[i], c_ref[i]
            k = c * u
            change = rows_change(u, k, cd_ref[i])
            ur = next_of(u_ref, i)
            f = (k + cr_ref[i] * ur) * (ur - u)
            before = pltpu.roll(f, 1, 1)
            if i % 3:
                before = jnp.where(first, pltpu.roll(flux, COLS - 3, 1), before)
            flux = f
            change = change + (f - before)
            uz = pltpu.roll(u, COLS - 4, 1)
            down = jnp.where(lowest, 0.0, (k + c * uz) * ((u - uz) + 0.3))
            change = change + (pltpu.roll(down, 4, 1) - down)
            new = held(u + change, inside)
            if i == 0:
                new = jnp.where(in_left, new, 0.5)
            if i == 5:
                new = jnp.where(in_right, new, 0.5)
            fresh.append(new)
        for i in range(6):
            u_ref[i] = fresh[i]
    left = u_ref[1][:ROWS] - 0.5
    right = u_ref[4][:ROWS] - 0.5
    left_ref[...] = left
    right_ref[...] = right
    lane = iota((ROWS, COLS), 1)

    def joined(l):
        lhs = pltpu.roll(left, COLS - 4 * l, 1) if l else left
        rhs = pltpu.roll(right, COLS - 4 - 4 * l, 1)
        return jnp.where(lane < 4, lhs, jnp.where(lane >= COLS - 4, rhs, tops_ref[l]))

    mix = 0.6 * joined(0) + 0.4 * joined(1)
    thermal = thermal_ref[...]
    bright = (thermal * (1.0 - 0.4 * mix * mix)).astype(BF16)
    adjoint_ref[...] = thermal * (-0.8 * mix)
    bright = jnp.concatenate([bright, jnp.zeros((COLS - ROWS, COLS), BF16)], axis=0)
    served_ref[...] = dot(picker_ref[...], bright, 1, 0).astype(BF16)


def wide_conduct(conduct_ref, halo):
    return 0.5 * jnp.concatenate([conduct_ref[...], halo[L]], axis=0)


def evolve(state_ref, conduct_ref, a_ref, b_ref, u_ref, c_ref, low, high, finish):
    halo = row_halo(a_ref, b_ref)
    c = wide_conduct(conduct_ref, halo)
    c_ref[0] = c
    c_ref[1] = pltpu.roll(c, WIDE - 1, 0)
    c_ref[2] = pltpu.roll(c, COLS - 1, 1)
    inside = halo_rows_inside()
    start, stop = max(0, low - STEPS), min(L, high + STEPS)
    for l in range(start, stop):
        u_ref[l - start] = jnp.concatenate([state_ref[l], halo[l]], axis=0) + 0.5
    for step in range(STEPS):
        top = max(0, low - (STEPS - 1 - step))
        end = min(L, high + (STEPS - 1 - step))
        above = None
        if top > 0:
            u, uz = u_ref[top - 1 - start], u_ref[top - start]
            above = c_ref[0] * (u + uz) * ((u - uz) + 0.3)
        u = u_ref[top - start]
        k = c_ref[0] * u
        for l in range(top, end):
            change = rows_change(u, k, c_ref[1]) + lanes_change(u, k, c_ref[2])
            if above is not None:
                change = change + above
            if l < L - 1:
                uz = u_ref[l + 1 - start]
                kz = c_ref[0] * uz
                above = (k + kz) * ((u - uz) + 0.3)
                change = change - above
            new = u + change
            if step < STEPS - 1:
                u_ref[l - start] = held(new, inside)
            else:
                finish(l, new[:ROWS] - 0.5)
            u, k = uz, kz


def tops_body(state_ref, conduct_ref, a_ref, b_ref, tops_ref, u_ref, c_ref):
    def finish(l, new):
        tops_ref[l] = new

    evolve(state_ref, conduct_ref, a_ref, b_ref, u_ref, c_ref, 0, 2, finish)


HALF = L // 2
PIECE = 4


def half_body(low, state_ref, conduct_ref, a_ref, b_ref, left_ref, right_ref, out_hbm, done_ref, u_ref, c_ref, own_ref, sems):
    lane = iota((ROWS, COLS), 1)
    copies = []

    def finish(l, new):
        lhs = pltpu.roll(left_ref[...], (COLS - 4 * l) % COLS, 1) if l else left_ref[...]
        turn = (COLS - 4 - 4 * l) % COLS
        rhs = pltpu.roll(right_ref[...], turn, 1) if turn else right_ref[...]
        own_ref[l - low] = jnp.where(lane < 4, lhs, jnp.where(lane >= COLS - 4, rhs, new))
        if (l + 1) % PIECE == 0:
            at = l + 1 - PIECE
            copy = pltpu.make_async_copy(
                own_ref.at[pl.ds(at - low, PIECE)], out_hbm.at[pl.ds(at, PIECE)], sems.at[len(copies)]
            )
            copy.start()
            copies.append(copy)

    evolve(state_ref, conduct_ref, a_ref, b_ref, u_ref, c_ref, low, low + HALF, finish)
    if done_ref is not None:
        done_ref[...] = jnp.zeros(done_ref.shape, F32)
    for copy in copies:
        copy.wait()


def upper_body(state_ref, conduct_ref, a_ref, b_ref, left_ref, right_ref, out_hbm, done_ref, *scratch):
    half_body(0, state_ref, conduct_ref, a_ref, b_ref, left_ref, right_ref, out_hbm, done_ref, *scratch)


def lower_body(state_ref, conduct_ref, a_ref, b_ref, left_ref, right_ref, begun_hbm, out_hbm, *scratch):
    half_body(HALF, state_ref, conduct_ref, a_ref, b_ref, left_ref, right_ref, out_hbm, None, *scratch)


def foot_body(
    returned_ref, placing_ref, after_ref, measured_hbm, weights_ref,
    bright_ref, outgoing_ref, measured_ref, held_ref, cells_ref, seen_ref, misfit_ref, contrib_ref, sems,
):
    parts = 8
    each = OWN // parts
    seen_copy = pltpu.make_async_copy(measured_hbm, measured_ref, sems.at[parts])
    seen_copy.start()
    copies = [
        pltpu.make_async_copy(
            weights_ref.at[pl.ds(p * each, each)], held_ref.at[pl.ds(p * each, each)], sems.at[p]
        )
        for p in range(parts)
    ]
    for copy in copies:
        copy.start()
    placing = placing_ref[...]
    cells_ref[...] = dot(placing, returned_ref[...], 0, 0)
    seen_copy.wait()
    seen = jnp.concatenate([measured_ref[...], jnp.zeros((COLS - OWN, FOOT), F32)], axis=0)
    seen_ref[...] = jnp.transpose(seen)
    misfit_ref[...] = jnp.zeros((FOOT, COLS), F32)
    lane = iota((FOOT, COLS), 1)

    def block(b, carry):
        total = jnp.where(lane == b, -seen_ref[...], 0.0)
        for k in range(TOUCH):
            total = total + held_ref[b, k].astype(F32) * cells_ref[pl.ds(k * OWN + b, 1), :]
        misfit = jnp.sum(total, axis=1, keepdims=True)
        misfit_ref[...] = jnp.where(lane == b, misfit, misfit_ref[...])
        rounded = misfit.astype(BF16).astype(F32)
        for k in range(TOUCH):
            contrib_ref[pl.ds(k * OWN + b, 1), :] = jnp.sum(
                held_ref[b, k].astype(F32) * rounded, axis=0, keepdims=True
            )
        return carry

    for p in range(parts):
        copies[p].wait()
        for b in range(p * each, (p + 1) * each):
            block(b, 0)
    evolved = jnp.transpose(misfit_ref[...] + seen_ref[...])
    bright_ref[...] = evolved[:OWN]
    outgoing_ref[...] = dot(placing, contrib_ref[...].astype(BF16), 1, 0).astype(BF16)


def gradient_body(grads_ref, picker_ref, adjoint_ref, out_ref):
    summed = dot(picker_ref[...], grads_ref[...], 0, 0)[:ROWS]
    common = summed * adjoint_ref[...]
    out_ref[0] = 0.6 * common
    out_ref[1] = 0.4 * common


def swapped(x, axis):
    n = lax.axis_size(axis)
    one = [(i, i ^ 1) for i in range(n)]
    two = [(i, i + 1) for i in range(1, n - 1, 2)] + [(i + 1, i) for i in range(1, n - 1, 2)]
    return lax.ppermute(x[0], axis, one), lax.ppermute(x[1], axis, two)


def exchange(x):
    return lax.all_to_all(
        x.reshape(TILES, CAP, COLS), ("gx", "gy"), split_axis=0, concat_axis=0, tiled=True
    ).reshape(SLOTS, COLS)


def on_device(state, inflow, classes, category, thermal, weights, slots, strips, measured):
    def sds(*shape, dtype=F32):
        return jax.ShapeDtypeStruct(shape, dtype)

    held_state, conduct, edge, warm = call(
        prep_body,
        (sds(L, ROWS, COLS), sds(ROWS, COLS), sds((L + 2) * 8, COLS, dtype=BF16), sds(ROWS, COLS)),
        [SMEM, HBM, HBM, HBM, HBM],
        "prep",
        [pltpu.VMEM((ROWS, COLS), F32), pltpu.VMEM((ROWS, COLS), jnp.int32), pltpu.SemaphoreType.DMA((4,))],
        flops=1_000_000, moved=2_000_000,
    )(classes, far(inflow), far(category), far(state), far(thermal))
    xa, xb = swapped((edge, edge), "gx")
    placing, request = call(
        request_body,
        (sds(SLOTS, REFS, dtype=BF16), sds(SLOTS, COLS, dtype=BF16)),
        [HBM, HBM, ANY],
        "requests",
        [pltpu.VMEM((TOUCH, OWN), jnp.int32), pltpu.VMEM((TOUCH, OWN), jnp.int32), pltpu.SemaphoreType.DMA((2,))],
        flops=20_000_000, moved=500_000,
    )(far(slots.T), far(strips.T), conduct)
    picker = exchange(request)
    own, cond, pa, pb = call(
        pack_body,
        (sds(4, WIDE, COLS), sds(4, WIDE, COLS), sds(2 * WIDE, COLS, dtype=BF16), sds(2 * WIDE, COLS, dtype=BF16)),
        [VMEM] * 4,
        "pack",
        flops=20_000_000_000, moved=1_500_000,
    )(held_state, conduct, xa, xb)
    ya, yb = swapped((pa, pb), "gy")
    tops = call(
        tops_body,
        sds(2, ROWS, COLS),
        [VMEM] * 4,
        "tops",
        [pltpu.VMEM((STEPS + 2, WIDE, COLS), F32), pltpu.VMEM((3, WIDE, COLS), F32)],
        flops=20_000_000_000, moved=1_000_000,
    )(held_state, conduct, xa, xb)
    left, right, adjoint, served = call(
        strip_body,
        (sds(ROWS, COLS), sds(ROWS, COLS), sds(ROWS, COLS), sds(SLOTS, COLS, dtype=BF16)),
        [VMEM] * 7,
        "strips",
        [pltpu.VMEM((6, WIDE, COLS), F32)] * 4,
        flops=20_000_000, moved=1_000_000,
    )(own, cond, ya, yb, tops, warm, picker)
    returned = exchange(served)
    scratch = [
        pltpu.VMEM((HALF + STEPS, WIDE, COLS), F32),
        pltpu.VMEM((3, WIDE, COLS), F32),
        pltpu.VMEM((HALF, ROWS, COLS), F32),
        pltpu.SemaphoreType.DMA((HALF // PIECE,)),
    ]
    begun, done = call(
        upper_body,
        (sds(L, ROWS, COLS), sds(8, COLS)),
        [VMEM] * 6,
        "upper",
        scratch,
        out_specs=(HBM, VMEM),
        flops=500_000_000, moved=3_000_000,
    )(held_state, conduct, xa, xb, left, right)
    brightness, outgoing = call(
        foot_body,
        (sds(OWN, FOOT), sds(SLOTS, COLS, dtype=BF16)),
        [VMEM, VMEM, ANY, HBM, HBM],
        "footprints",
        [
            pltpu.VMEM((OWN, FOOT), F32),
            pltpu.VMEM((OWN, TOUCH, FOOT, COLS), BF16),
            pltpu.VMEM((REFS, COLS), F32),
            pltpu.VMEM((FOOT, COLS), F32),
            pltpu.VMEM((FOOT, COLS), F32),
            pltpu.VMEM((REFS, COLS), F32),
            pltpu.SemaphoreType.DMA((9,)),
        ],
        flops=20_000_000, moved=5_000_000,
    )(returned, placing, done, far(measured), far(weights))
    moisture = call(
        lower_body,
        sds(L, ROWS, COLS),
        [VMEM] * 6 + [HBM],
        "lower",
        scratch,
        out_specs=HBM,
        aliases={6: 0},
        flops=500_000_000, moved=3_000_000,
    )(held_state, conduct, xa, xb, left, right, begun)
    grads = exchange(outgoing)
    grad_top = call(
        gradient_body, sds(2, ROWS, COLS), [VMEM] * 3, "gradient", flops=20_000_000, moved=400_000
    )(grads, picker, adjoint)
    return moisture, brightness, grad_top


def solution(mesh):
    placed = (
        P(None, "gx", "gy"),
        P("gx", "gy"),
        P(),
        P("gx", "gy"),
        P("gx", "gy"),
        P(("gx", "gy"), None, None, None),
        P(("gx", "gy"), None),
        P(("gx", "gy"), None),
        P(("gx", "gy"), None),
    )
    return jax.shard_map(
        on_device,
        mesh=mesh,
        in_specs=placed,
        out_specs=(P(None, "gx", "gy"), P(("gx", "gy"), None), P(None, "gx", "gy")),
        check_vma=False,
    )
```

```python
import jax
import jax.numpy as jnp
from jax import lax
from jax.experimental import pallas as pl
from jax.experimental.pallas import tpu as pltpu
from jax.sharding import PartitionSpec as P

CAP = 4
STEPS = 4
L = 32
ROWS = 64
COLS = 128
WIDE = ROWS + 8
TILES = 128
SLOTS = TILES * CAP
OWN = 32
TOUCH = 4
REFS = OWN * TOUCH
FOOT = 128
F32 = jnp.float32
BF16 = jnp.bfloat16
VMEM = pl.BlockSpec(memory_space=pltpu.VMEM)
SMEM = pl.BlockSpec(memory_space=pltpu.SMEM)
ANY = pl.BlockSpec(memory_space=pl.ANY)
HBM = pl.BlockSpec(memory_space=pltpu.HBM)
LIMIT = 32 * 1024 * 1024


def call(body, outs, in_specs, name, scratch=(), out_specs=None, aliases=None, flops=0, moved=0):
    return pl.pallas_call(
        body,
        out_shape=outs,
        in_specs=in_specs,
        out_specs=out_specs or jax.tree.map(lambda _: VMEM, outs),
        input_output_aliases=aliases or {},
        scratch_shapes=list(scratch),
        name=name,
        compiler_params=pltpu.CompilerParams(vmem_limit_bytes=LIMIT),
        cost_estimate=pl.CostEstimate(flops=flops, bytes_accessed=moved, transcendentals=0),
    )


def iota(shape, dim):
    return lax.broadcasted_iota(jnp.int32, shape, dim)


def far(x):
    return pltpu.with_memory_space_constraint(x, pltpu.HBM)


def dot(a, b, ca, cb):
    return lax.dot_general(a, b, (((ca,), (cb,)), ((), ())), preferred_element_type=F32)


def prep_body(
    classes_hbm, inflow_hbm, category_hbm, state_hbm, thermal_hbm, slot_hbm, strip_hbm, measured_hbm,
    state_ref, conduct_ref, edge_ref, thermal_ref, slot_ref, strip_ref, measured_ref,
    inflow_ref, category_ref, classes_ref, sems,
):
    pairs = (
        (classes_hbm, classes_ref),
        (category_hbm, category_ref),
        (inflow_hbm, inflow_ref),
        (state_hbm, state_ref),
        (slot_hbm, slot_ref),
        (strip_hbm, strip_ref),
        (thermal_hbm, thermal_ref),
        (measured_hbm, measured_ref),
    )
    copies = [pltpu.make_async_copy(a, b, sems.at[i]) for i, (a, b) in enumerate(pairs)]
    for copy in copies:
        copy.start()
    copies[0].wait()
    copies[1].wait()
    category = category_ref[...]
    conduct = jnp.zeros((ROWS, COLS), F32)
    for i in range(classes_ref.shape[0]):
        conduct = jnp.where(category == i, classes_ref[i], conduct)
    conduct_ref[...] = conduct
    copies[2].wait()
    copies[3].wait()
    state_ref[0] = state_ref[0] + inflow_ref[...]
    upper = iota((8, COLS), 0) < 4
    edges = jnp.where(upper[None], state_ref[:, 0:8, :], state_ref[:, ROWS - 8 : ROWS, :])
    ends = jnp.where(upper, conduct[0:8], conduct[ROWS - 8 : ROWS])[None]
    whole = jnp.concatenate([edges, ends, jnp.zeros((1, 8, COLS), F32)], axis=0)
    edge_ref[...] = whole.reshape((L + 2) * 8, COLS).astype(BF16)
    for copy in copies[4:]:
        copy.wait()


def request_body(slot_ref, strip_ref, after_ref, placing_ref, request_ref):
    tile = jnp.concatenate([slot_ref[k : k + 1, :] for k in range(TOUCH)], axis=1)
    row = jnp.concatenate([strip_ref[k : k + 1, :] for k in range(TOUCH)], axis=1)
    sub = iota((TILES, REFS), 0)
    named = (sub == tile).astype(F32)
    before = (sub < iota((REFS, REFS), 1)).astype(F32).astype(BF16)
    rank = jnp.sum(dot(named.astype(BF16), before, 1, 0) * named, axis=0, keepdims=True)
    place = tile * CAP + rank.astype(jnp.int32)
    placing = (iota((SLOTS, REFS), 0) == place).astype(F32).astype(BF16)
    placing_ref[...] = placing
    wanted = (sub == row).astype(F32).astype(BF16)
    request_ref[...] = dot(placing, wanted, 1, 1).astype(BF16)


def row_halo(a_ref, b_ref, levels=L + 1):
    odd = lax.rem(lax.axis_index("gx"), 2)
    a = a_ref[...].astype(F32).reshape(L + 2, 8, COLS)
    b = b_ref[...].astype(F32).reshape(L + 2, 8, COLS)
    half = lax.div(iota((8, COLS), 0), 4)
    return jnp.where((half == odd)[None], a, b)


def halo_rows_inside():
    gx = lax.axis_index("gx")
    sub = iota((8, COLS), 0)
    below = (gx < lax.axis_size("gx") - 1).astype(jnp.int32)
    above = (gx > 0).astype(jnp.int32)
    return jnp.where(sub < 4, below, above) > 0


def held(new, inside):
    return jnp.concatenate([new[:ROWS], jnp.where(inside, new[ROWS:], 0.5)], axis=0)


def rows_change(u, k, cd):
    ud = pltpu.roll(u, WIDE - 1, 0)
    f = (k + cd * ud) * (ud - u)
    return f - pltpu.roll(f, 1, 0)


def lanes_change(u, k, cr, cl):
    ur = pltpu.roll(u, COLS - 1, 1)
    ul = pltpu.roll(u, 1, 1)
    return (k + cr * ur) * (ur - u) - (k + cl * ul) * (u - ul)


def pack_body(state_ref, conduct_ref, a_ref, b_ref, own_ref, cond_ref, pa_ref, pb_ref):
    halo = row_halo(a_ref, b_ref)
    lane64 = iota((ROWS, COLS), 1)
    lane8 = iota((8, COLS), 1)
    shifts = (0, -4, 4, 8)

    def pack(levels_of, lane):
        acc = [jnp.zeros(lane.shape, F32) for _ in range(4)]
        for l in range(L):
            turned = levels_of(l)
            if l:
                turned = pltpu.roll(turned, 4 * l, 1)
            group = lane // 4
            for i, at in enumerate((l, (l + 1) % L, (l - 1) % L, (l - 2) % L)):
                acc[i] = jnp.where(group == at, turned, acc[i])
        return [pltpu.roll(x, s % COLS, 1) if s else x for x, s in zip(acc, shifts)]

    def spread(x, lane):
        out = []
        for s in (0, COLS - 4, 4, 8):
            y = jnp.where(lane < 4, pltpu.roll(x, s, 1) if s else x, 0.0)
            for d in (4, 8, 16, 32, 64):
                y = y + pltpu.roll(y, d, 1)
            out.append(y)
        return out

    main = pack(lambda l: state_ref[l], lane64)
    ends = pack(lambda l: halo[l], lane8)
    cmain = spread(conduct_ref[...], lane64)
    cends = spread(halo[L], lane8)
    packs = [jnp.concatenate([m, e], axis=0) for m, e in zip(main, ends)]
    conds = [jnp.concatenate([m, e], axis=0) for m, e in zip(cmain, cends)]
    for i in range(4):
        own_ref[i] = packs[i]
        cond_ref[i] = conds[i]
    odd = lax.rem(lax.axis_index("gy"), 2)
    left = jnp.concatenate([packs[0], conds[0]], axis=0)
    right = jnp.concatenate([packs[2], conds[2]], axis=0)
    is_odd = (jnp.zeros((2 * WIDE, COLS), jnp.int32) + odd) > 0
    pa_ref[...] = jnp.where(is_odd, left, right).astype(BF16)
    pb_ref[...] = jnp.where(is_odd, right, left).astype(BF16)


def strip_body(
    own_ref, cond_ref, pa_ref, pb_ref, tops_ref, thermal_ref, picker_ref,
    left_ref, right_ref, adjoint_ref, served_ref, u_ref, v_ref, c_ref, cd_ref, cr_ref, cl_ref,
):
    gy = lax.axis_index("gy")
    odd = lax.rem(gy, 2)
    a = pa_ref[...].astype(F32)
    b = pb_ref[...].astype(F32)
    is_odd = (jnp.zeros((2 * WIDE, COLS), jnp.int32) + odd) > 0
    from_right = jnp.where(is_odd, b, a)
    from_left = jnp.where(is_odd, a, b)
    lane = iota((WIDE, COLS), 1)
    last = lax.rem(lane, 4) == 3
    first = lax.rem(lane, 4) == 0
    lowest = lane >= COLS - 4
    highest = lane < 4
    inside = halo_rows_inside()
    in_left = (jnp.zeros((WIDE, COLS), jnp.int32) + gy) > 0
    in_right = (jnp.zeros((WIDE, COLS), jnp.int32) + gy) < lax.axis_size("gy") - 1
    sources = (
        (from_left[:WIDE], from_left[WIDE:]),
        (own_ref[0], cond_ref[0]),
        (own_ref[1], cond_ref[1]),
        (own_ref[3], cond_ref[3]),
        (own_ref[2], cond_ref[2]),
        (from_right[:WIDE], from_right[WIDE:]),
    )
    for i, (s, c) in enumerate(sources):
        u_ref[i] = s + 0.5
        c_ref[i] = 0.5 * c

    def next_of(ref, i):
        x = pltpu.roll(ref[i], COLS - 1, 1)
        return jnp.where(last, pltpu.roll(ref[i + 1], 3, 1), x) if i % 3 < 2 else x

    def prior_of(ref, i):
        x = pltpu.roll(ref[i], 1, 1)
        return jnp.where(first, pltpu.roll(ref[i - 1], COLS - 3, 1), x) if i % 3 else x

    for i in range(6):
        cd_ref[i] = pltpu.roll(c_ref[i], WIDE - 1, 0)
        cr_ref[i] = next_of(c_ref, i)
        cl_ref[i] = prior_of(c_ref, i)

    for step in range(STEPS):
        now, then = (u_ref, v_ref) if step % 2 == 0 else (v_ref, u_ref)
        for i in range(6):
            u, c = now[i], c_ref[i]
            k = c * u
            ur, ul = next_of(now, i), prior_of(now, i)
            uz, ua = pltpu.roll(u, COLS - 4, 1), pltpu.roll(u, 4, 1)
            change = rows_change(u, k, cd_ref[i])
            change = change + ((k + cr_ref[i] * ur) * (ur - u) - (k + cl_ref[i] * ul) * (u - ul))
            down = (k + c * uz) * ((u - uz) + 0.3)
            fall = (c * ua + k) * ((ua - u) + 0.3)
            change = change + (jnp.where(highest, 0.0, fall) - jnp.where(lowest, 0.0, down))
            new = held(u + change, inside)
            if i == 0:
                new = jnp.where(in_left, new, 0.5)
            if i == 5:
                new = jnp.where(in_right, new, 0.5)
            then[i] = new
    left = u_ref[1][:ROWS] - 0.5
    right = u_ref[4][:ROWS] - 0.5
    left_ref[...] = left
    right_ref[...] = right
    lane = iota((ROWS, COLS), 1)

    def joined(l):
        lhs = pltpu.roll(left, COLS - 4 * l, 1) if l else left
        rhs = pltpu.roll(right, COLS - 4 - 4 * l, 1)
        return jnp.where(lane < 4, lhs, jnp.where(lane >= COLS - 4, rhs, tops_ref[l]))

    mix = 0.6 * joined(0) + 0.4 * joined(1)
    thermal = thermal_ref[...]
    bright = (thermal * (1.0 - 0.4 * mix * mix)).astype(BF16)
    adjoint_ref[...] = thermal * (-0.8 * mix)
    bright = jnp.concatenate([bright, jnp.zeros((COLS - ROWS, COLS), BF16)], axis=0)
    served_ref[...] = dot(picker_ref[...], bright, 1, 0).astype(BF16)


def wide_conduct(conduct_ref, halo):
    return 0.5 * jnp.concatenate([conduct_ref[...], halo[L]], axis=0)


NEAR = 12


def evolve(state_ref, conduct_ref, a_ref, b_ref, u_ref, c_ref, low, high, finish):
    halo = row_halo(a_ref, b_ref)
    c = wide_conduct(conduct_ref, halo)
    c_ref[0] = c
    c_ref[1] = pltpu.roll(c, WIDE - 1, 0)
    c_ref[2] = pltpu.roll(c, COLS - 1, 1)
    c_ref[3] = pltpu.roll(c, 1, 1)
    inside = halo_rows_inside()
    start, stop = max(0, low - STEPS), min(L, high + STEPS)
    for l in range(start, stop):
        u_ref[l - start] = jnp.concatenate([state_ref[l], halo[l]], axis=0) + 0.5
    for step in range(STEPS):
        top = max(0, low - (STEPS - 1 - step))
        end = min(L, high + (STEPS - 1 - step))
        above = None
        if top > 0:
            u, uz = u_ref[top - 1 - start], u_ref[top - start]
            above = c_ref[0] * (u + uz) * ((u - uz) + 0.3)
        u = u_ref[top - start]
        k = c_ref[0] * u
        for l in range(top, end):
            change = rows_change(u, k, c_ref[1]) + lanes_change(u, k, c_ref[2], c_ref[3])
            if above is not None:
                change = change + above
            if l < L - 1:
                uz = u_ref[l + 1 - start]
                kz = c_ref[0] * uz
                above = (k + kz) * ((u - uz) + 0.3)
                change = change - above
            new = u + change
            if step < STEPS - 1:
                u_ref[l - start] = held(new, inside)
            else:
                finish(l, new[:ROWS] - 0.5)
            u, k = uz, kz


def tops_body(state_ref, conduct_ref, a_ref, b_ref, tops_ref, u_ref, c_ref):
    def finish(l, new):
        tops_ref[l] = new

    evolve(state_ref, conduct_ref, a_ref, b_ref, u_ref, c_ref, 0, 2, finish)


HALF = L // 2
PIECE = 4


def half_body(low, state_ref, conduct_ref, a_ref, b_ref, left_ref, right_ref, out_hbm, u_ref, c_ref, own_ref, sems):
    lane = iota((ROWS, COLS), 1)
    copies = []

    def finish(l, new):
        lhs = pltpu.roll(left_ref[...], (COLS - 4 * l) % COLS, 1) if l else left_ref[...]
        turn = (COLS - 4 - 4 * l) % COLS
        rhs = pltpu.roll(right_ref[...], turn, 1) if turn else right_ref[...]
        own_ref[l - low] = jnp.where(lane < 4, lhs, jnp.where(lane >= COLS - 4, rhs, new))
        if (l + 1) % PIECE == 0:
            at = l + 1 - PIECE
            copy = pltpu.make_async_copy(
                own_ref.at[pl.ds(at - low, PIECE)], out_hbm.at[pl.ds(at, PIECE)], sems.at[len(copies)]
            )
            copy.start()
            copies.append(copy)

    evolve(state_ref, conduct_ref, a_ref, b_ref, u_ref, c_ref, low, low + HALF, finish)
    for copy in copies:
        copy.wait()


def upper_body(
    state_ref, conduct_ref, a_ref, b_ref, left_ref, right_ref, weights_hbm, out_hbm, weights_ref, *scratch
):
    copy = pltpu.make_async_copy(weights_hbm.at[pl.ds(0, NEAR)], weights_ref, scratch[-1])
    copy.start()
    half_body(0, state_ref, conduct_ref, a_ref, b_ref, left_ref, right_ref, out_hbm, *scratch[:-1])
    copy.wait()


def lower_body(
    state_hbm, conduct_ref, a_ref, b_ref, left_ref, right_ref, begun_hbm, out_hbm, *scratch
):
    state_ref, sem = scratch[-2:]
    span = pl.ds(HALF - STEPS, L - HALF + STEPS)
    copy = pltpu.make_async_copy(state_hbm.at[span], state_ref.at[span], sem)
    copy.start()
    copy.wait()
    half_body(HALF, state_ref, conduct_ref, a_ref, b_ref, left_ref, right_ref, out_hbm, *scratch[:-2])


PART = 4


def foot_body(
    returned_ref, placing_ref, seen_ref, near_ref, weights_hbm,
    bright_ref, outgoing_ref, cells_ref, contrib_ref, weights_ref, sems,
):
    copies = {}
    for start in range(NEAR, OWN, PART):
        span = pl.ds(start, PART)
        copies[start] = pltpu.make_async_copy(
            weights_hbm.at[span], weights_ref.at[span], sems.at[start // PART]
        )
        copies[start].start()
    placing = placing_ref[...]
    cells_ref[...] = dot(placing, returned_ref[...], 0, 0)
    lane = iota((FOOT, COLS), 1)

    def weights(b, k):
        return near_ref[b, k] if b < NEAR else weights_ref[b, k]

    def adjoint(start, misfit):
        for i in range(PART):
            for k in range(TOUCH):
                at = k * OWN + start + i
                contrib_ref[at : at + 1, :] = dot(misfit[i : i + 1], weights(start + i, k), 1, 0)

    misfit = None
    for start in range(0, OWN, PART):
        if start in copies:
            copies[start].wait()
        sums = jnp.zeros((FOOT, COLS), F32)
        for i in range(PART):
            total = None
            for k in range(TOUCH):
                at = k * OWN + start + i
                term = weights(start + i, k).astype(F32) * cells_ref[at : at + 1, :]
                total = term if total is None else total + term
            sums = jnp.where(lane == i, jnp.sum(total, axis=1, keepdims=True), sums)
        if start:
            adjoint(start - PART, misfit)
        evolved = jnp.transpose(sums)[:PART]
        bright_ref[start : start + PART, :] = evolved
        misfit = (evolved - seen_ref[start : start + PART, :]).astype(BF16)
    adjoint(OWN - PART, misfit)
    outgoing_ref[...] = dot(placing, contrib_ref[...].astype(BF16), 1, 0).astype(BF16)


def gradient_body(grads_ref, picker_ref, adjoint_ref, out_ref):
    summed = dot(picker_ref[...], grads_ref[...], 0, 0)[:ROWS]
    common = summed * adjoint_ref[...]
    out_ref[0] = 0.6 * common
    out_ref[1] = 0.4 * common


def swapped(x, axis):
    n = lax.axis_size(axis)
    one = [(i, i ^ 1) for i in range(n)]
    two = [(i, i + 1) for i in range(1, n - 1, 2)] + [(i + 1, i) for i in range(1, n - 1, 2)]
    return lax.ppermute(x[0], axis, one), lax.ppermute(x[1], axis, two)


def exchange(x):
    return lax.all_to_all(
        x.reshape(TILES, CAP, COLS), ("gx", "gy"), split_axis=0, concat_axis=0, tiled=True
    ).reshape(SLOTS, COLS)


def on_device(state, inflow, classes, category, thermal, weights, slots, strips, measured):
    def sds(*shape, dtype=F32):
        return jax.ShapeDtypeStruct(shape, dtype)

    held_state, conduct, edge, warm, slot_ids, strip_ids, seen = call(
        prep_body,
        (
            sds(L, ROWS, COLS), sds(ROWS, COLS), sds((L + 2) * 8, COLS, dtype=BF16), sds(ROWS, COLS),
            sds(TOUCH, OWN, dtype=jnp.int32), sds(TOUCH, OWN, dtype=jnp.int32), sds(OWN, FOOT),
        ),
        [HBM] * 8,
        "prep",
        [
            pltpu.VMEM((ROWS, COLS), F32),
            pltpu.VMEM((ROWS, COLS), jnp.int32),
            pltpu.SMEM(classes.shape, F32),
            pltpu.SemaphoreType.DMA((8,)),
        ],
        flops=1_000_000, moved=2_000_000,
    )(*(far(x) for x in (classes, inflow, category, state, thermal, slots.T, strips.T, measured)))
    xa, xb = swapped((edge, edge), "gx")
    placing, request = call(
        request_body,
        (sds(SLOTS, REFS, dtype=BF16), sds(SLOTS, COLS, dtype=BF16)),
        [VMEM, VMEM, ANY],
        "requests",
        flops=20_000_000, moved=500_000,
    )(slot_ids, strip_ids, conduct)
    picker = exchange(request)
    own, cond, pa, pb = call(
        pack_body,
        (sds(4, WIDE, COLS), sds(4, WIDE, COLS), sds(2 * WIDE, COLS, dtype=BF16), sds(2 * WIDE, COLS, dtype=BF16)),
        [VMEM] * 4,
        "pack",
        flops=20_000_000_000, moved=1_500_000,
    )(held_state, conduct, xa, xb)
    ya, yb = swapped((pa, pb), "gy")
    tops = call(
        tops_body,
        sds(2, ROWS, COLS),
        [VMEM] * 4,
        "tops",
        [pltpu.VMEM((STEPS + 2, WIDE, COLS), F32), pltpu.VMEM((4, WIDE, COLS), F32)],
        flops=20_000_000_000, moved=1_000_000,
    )(held_state, conduct, xa, xb)
    left, right, adjoint, served = call(
        strip_body,
        (sds(ROWS, COLS), sds(ROWS, COLS), sds(ROWS, COLS), sds(SLOTS, COLS, dtype=BF16)),
        [VMEM] * 7,
        "strips",
        [pltpu.VMEM((6, WIDE, COLS), F32)] * 6,
        flops=20_000_000, moved=1_000_000,
    )(own, cond, ya, yb, tops, warm, picker)
    returned = exchange(served)
    scratch = [
        pltpu.VMEM((HALF + STEPS, WIDE, COLS), F32),
        pltpu.VMEM((4, WIDE, COLS), F32),
        pltpu.VMEM((HALF, ROWS, COLS), F32),
        pltpu.SemaphoreType.DMA((HALF // PIECE,)),
    ]
    begun, near = call(
        upper_body,
        (sds(L, ROWS, COLS), sds(NEAR, TOUCH, FOOT, COLS, dtype=BF16)),
        [VMEM] * 6 + [HBM],
        "upper",
        scratch + [pltpu.SemaphoreType.DMA],
        out_specs=(HBM, VMEM),
        flops=500_000_000, moved=3_000_000,
    )(held_state, conduct, xa, xb, left, right, far(weights))
    brightness, outgoing = call(
        foot_body,
        (sds(OWN, FOOT), sds(SLOTS, COLS, dtype=BF16)),
        [VMEM] * 4 + [HBM],
        "footprints",
        [
            pltpu.VMEM((REFS, COLS), F32),
            pltpu.VMEM((REFS, COLS), F32),
            pltpu.VMEM(weights.shape, BF16),
            pltpu.SemaphoreType.DMA((OWN // PART,)),
        ],
        flops=20_000_000, moved=5_000_000,
    )(returned, placing, seen, near, far(weights))
    moisture = call(
        lower_body,
        sds(L, ROWS, COLS),
        [HBM] + [VMEM] * 5 + [HBM],
        "lower",
        scratch + [pltpu.VMEM((L, ROWS, COLS), F32), pltpu.SemaphoreType.DMA],
        out_specs=HBM,
        aliases={6: 0},
        flops=500_000_000, moved=3_000_000,
    )(far(state), conduct, xa, xb, left, right, begun)
    grads = exchange(outgoing)
    grad_top = call(
        gradient_body, sds(2, ROWS, COLS), [VMEM] * 3, "gradient", flops=20_000_000, moved=400_000
    )(grads, picker, adjoint)
    return moisture, brightness, grad_top


def solution(mesh):
    placed = (
        P(None, "gx", "gy"),
        P("gx", "gy"),
        P(),
        P("gx", "gy"),
        P("gx", "gy"),
        P(("gx", "gy"), None, None, None),
        P(("gx", "gy"), None),
        P(("gx", "gy"), None),
        P(("gx", "gy"), None),
    )
    return jax.shard_map(
        on_device,
        mesh=mesh,
        in_specs=placed,
        out_specs=(P(None, "gx", "gy"), P(("gx", "gy"), None), P(None, "gx", "gy")),
        check_vma=False,
    )
```

```python
import jax
import jax.numpy as jnp
from jax import lax
from jax.experimental import pallas as pl
from jax.experimental.pallas import tpu as pltpu
from jax.sharding import PartitionSpec as P

CAP = 4
STEPS = 4
L = 32
ROWS = 64
COLS = 128
WIDE = ROWS + 8
TILES = 128
SLOTS = TILES * CAP
OWN = 32
TOUCH = 4
REFS = OWN * TOUCH
FOOT = 128
F32 = jnp.float32
BF16 = jnp.bfloat16
VMEM = pl.BlockSpec(memory_space=pltpu.VMEM)
SMEM = pl.BlockSpec(memory_space=pltpu.SMEM)
ANY = pl.BlockSpec(memory_space=pl.ANY)
HBM = pl.BlockSpec(memory_space=pltpu.HBM)
LIMIT = 32 * 1024 * 1024


def call(body, outs, in_specs, name, scratch=(), out_specs=None, aliases=None, flops=0, moved=0):
    return pl.pallas_call(
        body,
        out_shape=outs,
        in_specs=in_specs,
        out_specs=out_specs or jax.tree.map(lambda _: VMEM, outs),
        input_output_aliases=aliases or {},
        scratch_shapes=list(scratch),
        name=name,
        compiler_params=pltpu.CompilerParams(vmem_limit_bytes=LIMIT),
        cost_estimate=pl.CostEstimate(flops=flops, bytes_accessed=moved, transcendentals=0),
    )


def iota(shape, dim):
    return lax.broadcasted_iota(jnp.int32, shape, dim)


def far(x):
    return pltpu.with_memory_space_constraint(x, pltpu.HBM)


def dot(a, b, ca, cb):
    return lax.dot_general(a, b, (((ca,), (cb,)), ((), ())), preferred_element_type=F32)


def prep_body(
    classes_hbm, inflow_hbm, category_hbm, state_hbm, thermal_hbm, slot_hbm, strip_hbm, measured_hbm,
    state_ref, conduct_ref, edge_ref, thermal_ref, measured_ref, placing_ref, request_ref,
    inflow_ref, category_ref, classes_ref, slot_ref, strip_ref, sems,
):
    pairs = (
        (slot_hbm, slot_ref),
        (strip_hbm, strip_ref),
        (classes_hbm, classes_ref),
        (category_hbm, category_ref),
        (inflow_hbm, inflow_ref),
        (state_hbm, state_ref),
        (thermal_hbm, thermal_ref),
        (measured_hbm, measured_ref),
    )
    copies = [pltpu.make_async_copy(a, b, sems.at[i]) for i, (a, b) in enumerate(pairs)]
    for copy in copies:
        copy.start()
    copies[0].wait()
    copies[1].wait()
    tile = jnp.concatenate([slot_ref[k : k + 1, :] for k in range(TOUCH)], axis=1)
    row = jnp.concatenate([strip_ref[k : k + 1, :] for k in range(TOUCH)], axis=1)
    sub = iota((TILES, REFS), 0)
    named = (sub == tile).astype(F32)
    before = (sub < iota((REFS, REFS), 1)).astype(F32).astype(BF16)
    rank = jnp.sum(dot(named.astype(BF16), before, 1, 0) * named, axis=0, keepdims=True)
    place = tile * CAP + rank.astype(jnp.int32)
    placing = (iota((SLOTS, REFS), 0) == place).astype(F32).astype(BF16)
    placing_ref[...] = placing
    wanted = (sub == row).astype(F32).astype(BF16)
    request_ref[...] = dot(placing, wanted, 1, 1).astype(BF16)
    copies[2].wait()
    copies[3].wait()
    category = category_ref[...]
    conduct = jnp.zeros((ROWS, COLS), F32)
    for i in range(classes_ref.shape[0]):
        conduct = jnp.where(category == i, classes_ref[i], conduct)
    conduct_ref[...] = conduct
    copies[4].wait()
    copies[5].wait()
    state_ref[0] = state_ref[0] + inflow_ref[...]
    upper = iota((8, COLS), 0) < 4
    edges = jnp.where(upper[None], state_ref[:, 0:8, :], state_ref[:, ROWS - 8 : ROWS, :])
    ends = jnp.where(upper, conduct[0:8], conduct[ROWS - 8 : ROWS])[None]
    whole = jnp.concatenate([edges, ends, jnp.zeros((1, 8, COLS), F32)], axis=0)
    edge_ref[...] = whole.reshape((L + 2) * 8, COLS).astype(BF16)
    for copy in copies[6:]:
        copy.wait()


def row_halo(a_ref, b_ref, levels=L + 1):
    odd = lax.rem(lax.axis_index("gx"), 2)
    a = a_ref[...].astype(F32).reshape(L + 2, 8, COLS)
    b = b_ref[...].astype(F32).reshape(L + 2, 8, COLS)
    half = lax.div(iota((8, COLS), 0), 4)
    return jnp.where((half == odd)[None], a, b)


def halo_rows_inside():
    gx = lax.axis_index("gx")
    sub = iota((8, COLS), 0)
    below = (gx < lax.axis_size("gx") - 1).astype(jnp.int32)
    above = (gx > 0).astype(jnp.int32)
    return jnp.where(sub < 4, below, above) > 0


def held(new, inside):
    return jnp.concatenate([new[:ROWS], jnp.where(inside, new[ROWS:], 0.5)], axis=0)


def rows_change(u, k, cd):
    ud = pltpu.roll(u, WIDE - 1, 0)
    f = (k + cd * ud) * (ud - u)
    return f - pltpu.roll(f, 1, 0)


def lanes_change(u, k, cr, cl):
    ur = pltpu.roll(u, COLS - 1, 1)
    ul = pltpu.roll(u, 1, 1)
    return (k + cr * ur) * (ur - u) - (k + cl * ul) * (u - ul)


def pack_body(state_ref, conduct_ref, a_ref, b_ref, own_ref, cond_ref, pa_ref, pb_ref):
    halo = row_halo(a_ref, b_ref)
    lane64 = iota((ROWS, COLS), 1)
    lane8 = iota((8, COLS), 1)
    shifts = (0, -4, 4, 8)

    def pack(levels_of, lane):
        acc = [jnp.zeros(lane.shape, F32) for _ in range(4)]
        for l in range(L):
            turned = levels_of(l)
            if l:
                turned = pltpu.roll(turned, 4 * l, 1)
            group = lane // 4
            for i, at in enumerate((l, (l + 1) % L, (l - 1) % L, (l - 2) % L)):
                acc[i] = jnp.where(group == at, turned, acc[i])
        return [pltpu.roll(x, s % COLS, 1) if s else x for x, s in zip(acc, shifts)]

    def spread(x, lane):
        out = []
        for s in (0, COLS - 4, 4, 8):
            y = jnp.where(lane < 4, pltpu.roll(x, s, 1) if s else x, 0.0)
            for d in (4, 8, 16, 32, 64):
                y = y + pltpu.roll(y, d, 1)
            out.append(y)
        return out

    main = pack(lambda l: state_ref[l], lane64)
    ends = pack(lambda l: halo[l], lane8)
    cmain = spread(conduct_ref[...], lane64)
    cends = spread(halo[L], lane8)
    packs = [jnp.concatenate([m, e], axis=0) for m, e in zip(main, ends)]
    conds = [jnp.concatenate([m, e], axis=0) for m, e in zip(cmain, cends)]
    for i in range(4):
        own_ref[i] = packs[i]
        cond_ref[i] = conds[i]
    odd = lax.rem(lax.axis_index("gy"), 2)
    left = jnp.concatenate([packs[0], conds[0]], axis=0)
    right = jnp.concatenate([packs[2], conds[2]], axis=0)
    is_odd = (jnp.zeros((2 * WIDE, COLS), jnp.int32) + odd) > 0
    pa_ref[...] = jnp.where(is_odd, left, right).astype(BF16)
    pb_ref[...] = jnp.where(is_odd, right, left).astype(BF16)


def strip_body(
    own_ref, cond_ref, pa_ref, pb_ref, tops_ref, thermal_ref,
    left_ref, right_ref, adjoint_ref, bright_ref, u_ref, v_ref, c_ref, cd_ref, cr_ref, cl_ref, lower_ref, upper_ref,
):
    gy = lax.axis_index("gy")
    odd = lax.rem(gy, 2)
    a = pa_ref[...].astype(F32)
    b = pb_ref[...].astype(F32)
    is_odd = (jnp.zeros((2 * WIDE, COLS), jnp.int32) + odd) > 0
    from_right = jnp.where(is_odd, b, a)
    from_left = jnp.where(is_odd, a, b)
    lane = iota((WIDE, COLS), 1)
    last = lax.rem(lane, 4) == 3
    first = lax.rem(lane, 4) == 0
    lowest = lane >= COLS - 4
    highest = lane < 4
    inside = halo_rows_inside()
    in_left = (jnp.zeros((WIDE, COLS), jnp.int32) + gy) > 0
    in_right = (jnp.zeros((WIDE, COLS), jnp.int32) + gy) < lax.axis_size("gy") - 1
    sources = (
        (from_left[:WIDE], from_left[WIDE:]),
        (own_ref[0], cond_ref[0]),
        (own_ref[1], cond_ref[1]),
        (own_ref[3], cond_ref[3]),
        (own_ref[2], cond_ref[2]),
        (from_right[:WIDE], from_right[WIDE:]),
    )
    for i, (s, c) in enumerate(sources):
        u_ref[i] = s + 0.5
        c_ref[i] = 0.5 * c

    def turn(ref):
        for i in range(6):
            lower_ref[i] = pltpu.roll(ref[i], COLS - 4, 1)
            upper_ref[i] = pltpu.roll(ref[i], 4, 1)

    def next_of(ref, i):
        x = jnp.where(first, upper_ref[i + 1], ref[i]) if i % 3 < 2 else ref[i]
        return pltpu.roll(x, COLS - 1, 1)

    def prior_of(ref, i):
        x = jnp.where(last, lower_ref[i - 1], ref[i]) if i % 3 else ref[i]
        return pltpu.roll(x, 1, 1)

    turn(c_ref)
    for i in range(6):
        cd_ref[i] = pltpu.roll(c_ref[i], WIDE - 1, 0)
        cr_ref[i] = next_of(c_ref, i)
        cl_ref[i] = prior_of(c_ref, i)

    for step in range(STEPS):
        now, then = (u_ref, v_ref) if step % 2 == 0 else (v_ref, u_ref)
        turn(now)
        for i in range(6) if step < STEPS - 1 else (1, 4):
            u, c = now[i], c_ref[i]
            k = c * u
            ur, ul = next_of(now, i), prior_of(now, i)
            uz, ua = lower_ref[i], upper_ref[i]
            change = rows_change(u, k, cd_ref[i])
            change = change + ((k + cr_ref[i] * ur) * (ur - u) - (k + cl_ref[i] * ul) * (u - ul))
            down = (k + c * uz) * ((u - uz) + 0.3)
            fall = (c * ua + k) * ((ua - u) + 0.3)
            change = change + (jnp.where(highest, 0.0, fall) - jnp.where(lowest, 0.0, down))
            new = held(u + change, inside)
            if i == 0:
                new = jnp.where(in_left, new, 0.5)
            if i == 5:
                new = jnp.where(in_right, new, 0.5)
            then[i] = new
    left = u_ref[1][:ROWS] - 0.5
    right = u_ref[4][:ROWS] - 0.5
    left_ref[...] = left
    right_ref[...] = right
    lane = iota((ROWS, COLS), 1)

    def joined(l):
        lhs = pltpu.roll(left, COLS - 4 * l, 1) if l else left
        rhs = pltpu.roll(right, COLS - 4 - 4 * l, 1)
        return jnp.where(lane < 4, lhs, jnp.where(lane >= COLS - 4, rhs, tops_ref[l]))

    mix = 0.6 * joined(0) + 0.4 * joined(1)
    thermal = thermal_ref[...]
    bright = (thermal * (1.0 - 0.4 * mix * mix)).astype(BF16)
    adjoint_ref[...] = thermal * (-0.8 * mix)
    bright_ref[...] = jnp.concatenate([bright, jnp.zeros((COLS - ROWS, COLS), BF16)], axis=0)


def serve_body(picker_ref, bright_ref, served_ref):
    served_ref[...] = dot(picker_ref[...], bright_ref[...], 1, 0).astype(BF16)


def wide_conduct(conduct_ref, halo):
    return 0.5 * jnp.concatenate([conduct_ref[...], halo[L]], axis=0)


NEAR = 12


def evolve(state_ref, conduct_ref, a_ref, b_ref, u_ref, c_ref, low, high, finish):
    halo = row_halo(a_ref, b_ref)
    c = wide_conduct(conduct_ref, halo)
    c_ref[0] = c
    c_ref[1] = pltpu.roll(c, WIDE - 1, 0)
    c_ref[2] = pltpu.roll(c, COLS - 1, 1)
    c_ref[3] = pltpu.roll(c, 1, 1)
    inside = halo_rows_inside()
    start, stop = max(0, low - STEPS), min(L, high + STEPS)
    for l in range(start, stop):
        u_ref[l - start] = jnp.concatenate([state_ref[l], halo[l]], axis=0) + 0.5
    for step in range(STEPS):
        top = max(0, low - (STEPS - 1 - step))
        end = min(L, high + (STEPS - 1 - step))
        above = None
        if top > 0:
            u, uz = u_ref[top - 1 - start], u_ref[top - start]
            above = c_ref[0] * (u + uz) * ((u - uz) + 0.3)
        u = u_ref[top - start]
        k = c_ref[0] * u
        for l in range(top, end):
            change = rows_change(u, k, c_ref[1]) + lanes_change(u, k, c_ref[2], c_ref[3])
            if above is not None:
                change = change + above
            if l < L - 1:
                uz = u_ref[l + 1 - start]
                kz = c_ref[0] * uz
                above = (k + kz) * ((u - uz) + 0.3)
                change = change - above
            new = u + change
            if step < STEPS - 1:
                u_ref[l - start] = held(new, inside)
            else:
                finish(l, new[:ROWS] - 0.5)
            u, k = uz, kz


def tops_body(state_ref, conduct_ref, a_ref, b_ref, tops_ref, u_ref, c_ref):
    def finish(l, new):
        tops_ref[l] = new

    evolve(state_ref, conduct_ref, a_ref, b_ref, u_ref, c_ref, 0, 2, finish)


HALF = L // 2
PIECE = 4


def half_body(low, state_ref, conduct_ref, a_ref, b_ref, left_ref, right_ref, out_hbm, u_ref, c_ref, own_ref, sems):
    lane = iota((ROWS, COLS), 1)
    copies = []

    def finish(l, new):
        lhs = pltpu.roll(left_ref[...], (COLS - 4 * l) % COLS, 1) if l else left_ref[...]
        turn = (COLS - 4 - 4 * l) % COLS
        rhs = pltpu.roll(right_ref[...], turn, 1) if turn else right_ref[...]
        own_ref[l - low] = jnp.where(lane < 4, lhs, jnp.where(lane >= COLS - 4, rhs, new))
        if (l + 1) % PIECE == 0:
            at = l + 1 - PIECE
            copy = pltpu.make_async_copy(
                own_ref.at[pl.ds(at - low, PIECE)], out_hbm.at[pl.ds(at, PIECE)], sems.at[len(copies)]
            )
            copy.start()
            copies.append(copy)

    evolve(state_ref, conduct_ref, a_ref, b_ref, u_ref, c_ref, low, low + HALF, finish)
    for copy in copies:
        copy.wait()


def upper_body(
    state_ref, conduct_ref, a_ref, b_ref, left_ref, right_ref, weights_hbm, out_hbm, weights_ref, *scratch
):
    copy = pltpu.make_async_copy(weights_hbm.at[pl.ds(0, NEAR)], weights_ref, scratch[-1])
    copy.start()
    half_body(0, state_ref, conduct_ref, a_ref, b_ref, left_ref, right_ref, out_hbm, *scratch[:-1])
    copy.wait()


def lower_body(
    state_hbm, conduct_ref, a_ref, b_ref, left_ref, right_ref, begun_hbm, out_hbm, *scratch
):
    state_ref, sem = scratch[-2:]
    span = pl.ds(HALF - STEPS, L - HALF + STEPS)
    copy = pltpu.make_async_copy(state_hbm.at[span], state_ref.at[span], sem)
    copy.start()
    copy.wait()
    half_body(HALF, state_ref, conduct_ref, a_ref, b_ref, left_ref, right_ref, out_hbm, *scratch[:-2])


PART = 4
CHUNKS = (8, 12)


def foot_body(
    returned_ref, placing_ref, seen_ref, near_ref, weights_hbm,
    bright_ref, outgoing_ref, cells_ref, contrib_ref, weights_ref, sems,
):
    copies = {}
    at = NEAR
    for i, count in enumerate(CHUNKS):
        span = pl.ds(at, count)
        copies[at] = pltpu.make_async_copy(weights_hbm.at[span], weights_ref.at[span], sems.at[i])
        copies[at].start()
        at += count
    placing = placing_ref[...]
    cells_ref[...] = dot(placing, returned_ref[...], 0, 0)
    lane = iota((FOOT, COLS), 1)

    def weights(b, k):
        return near_ref[b, k] if b < NEAR else weights_ref[b, k]

    def adjoint(start, misfit):
        for i in range(PART):
            for k in range(TOUCH):
                at = k * OWN + start + i
                contrib_ref[at : at + 1, :] = dot(misfit[i : i + 1], weights(start + i, k), 1, 0)

    misfit = None
    for start in range(0, OWN, PART):
        if start in copies:
            copies[start].wait()
        sums = jnp.zeros((FOOT, COLS), F32)
        for i in range(PART):
            total = None
            for k in range(TOUCH):
                at = k * OWN + start + i
                term = weights(start + i, k).astype(F32) * cells_ref[at : at + 1, :]
                total = term if total is None else total + term
            sums = jnp.where(lane == i, jnp.sum(total, axis=1, keepdims=True), sums)
        if start:
            adjoint(start - PART, misfit)
        evolved = jnp.transpose(sums)[:PART]
        bright_ref[start : start + PART, :] = evolved
        misfit = (evolved - seen_ref[start : start + PART, :]).astype(BF16)
    adjoint(OWN - PART, misfit)
    outgoing_ref[...] = dot(placing, contrib_ref[...].astype(BF16), 1, 0).astype(BF16)


def gradient_body(grads_ref, picker_ref, adjoint_ref, out_ref):
    summed = dot(picker_ref[...], grads_ref[...], 0, 0)[:ROWS]
    common = summed * adjoint_ref[...]
    out_ref[0] = 0.6 * common
    out_ref[1] = 0.4 * common


def swapped(x, axis):
    n = lax.axis_size(axis)
    one = [(i, i ^ 1) for i in range(n)]
    two = [(i, i + 1) for i in range(1, n - 1, 2)] + [(i + 1, i) for i in range(1, n - 1, 2)]
    return lax.ppermute(x[0], axis, one), lax.ppermute(x[1], axis, two)


def exchange(x):
    return lax.all_to_all(
        x.reshape(TILES, CAP, COLS), ("gx", "gy"), split_axis=0, concat_axis=0, tiled=True
    ).reshape(SLOTS, COLS)


def on_device(state, inflow, classes, category, thermal, weights, slots, strips, measured):
    def sds(*shape, dtype=F32):
        return jax.ShapeDtypeStruct(shape, dtype)

    held_state, conduct, edge, warm, seen, placing, request = call(
        prep_body,
        (
            sds(L, ROWS, COLS), sds(ROWS, COLS), sds((L + 2) * 8, COLS, dtype=BF16), sds(ROWS, COLS),
            sds(OWN, FOOT), sds(SLOTS, REFS, dtype=BF16), sds(SLOTS, COLS, dtype=BF16),
        ),
        [HBM] * 8,
        "prep",
        [
            pltpu.VMEM((ROWS, COLS), F32),
            pltpu.VMEM((ROWS, COLS), jnp.int32),
            pltpu.SMEM(classes.shape, F32),
            pltpu.VMEM((TOUCH, OWN), jnp.int32),
            pltpu.VMEM((TOUCH, OWN), jnp.int32),
            pltpu.SemaphoreType.DMA((8,)),
        ],
        flops=20_000_000, moved=2_000_000,
    )(*(far(x) for x in (classes, inflow, category, state, thermal, slots.T, strips.T, measured)))
    xa, xb = swapped((edge, edge), "gx")
    picker = exchange(request)
    own, cond, pa, pb = call(
        pack_body,
        (sds(4, WIDE, COLS), sds(4, WIDE, COLS), sds(2 * WIDE, COLS, dtype=BF16), sds(2 * WIDE, COLS, dtype=BF16)),
        [VMEM] * 4,
        "pack",
        flops=20_000_000_000, moved=1_500_000,
    )(held_state, conduct, xa, xb)
    ya, yb = swapped((pa, pb), "gy")
    tops = call(
        tops_body,
        sds(2, ROWS, COLS),
        [VMEM] * 4,
        "tops",
        [pltpu.VMEM((STEPS + 2, WIDE, COLS), F32), pltpu.VMEM((4, WIDE, COLS), F32)],
        flops=20_000_000_000, moved=1_000_000,
    )(held_state, conduct, xa, xb)
    left, right, adjoint, bright = call(
        strip_body,
        (sds(ROWS, COLS), sds(ROWS, COLS), sds(ROWS, COLS), sds(COLS, COLS, dtype=BF16)),
        [VMEM] * 6,
        "strips",
        [pltpu.VMEM((6, WIDE, COLS), F32)] * 8,
        flops=10_000_000_000, moved=1_000_000,
    )(own, cond, ya, yb, tops, warm)
    served = call(
        serve_body,
        sds(SLOTS, COLS, dtype=BF16),
        [VMEM] * 2,
        "serve",
        flops=20_000_000, moved=300_000,
    )(picker, bright)
    returned = exchange(served)
    scratch = [
        pltpu.VMEM((HALF + STEPS, WIDE, COLS), F32),
        pltpu.VMEM((4, WIDE, COLS), F32),
        pltpu.VMEM((HALF, ROWS, COLS), F32),
        pltpu.SemaphoreType.DMA((HALF // PIECE,)),
    ]
    begun, near = call(
        upper_body,
        (sds(L, ROWS, COLS), sds(NEAR, TOUCH, FOOT, COLS, dtype=BF16)),
        [VMEM] * 6 + [HBM],
        "upper",
        scratch + [pltpu.SemaphoreType.DMA],
        out_specs=(HBM, VMEM),
        flops=500_000_000, moved=3_000_000,
    )(held_state, conduct, xa, xb, left, right, far(weights))
    brightness, outgoing = call(
        foot_body,
        (sds(OWN, FOOT), sds(SLOTS, COLS, dtype=BF16)),
        [VMEM] * 4 + [HBM],
        "footprints",
        [
            pltpu.VMEM((REFS, COLS), F32),
            pltpu.VMEM((REFS, COLS), F32),
            pltpu.VMEM(weights.shape, BF16),
            pltpu.SemaphoreType.DMA((len(CHUNKS),)),
        ],
        flops=20_000_000, moved=5_000_000,
    )(returned, placing, seen, near, far(weights))
    moisture = call(
        lower_body,
        sds(L, ROWS, COLS),
        [HBM] + [VMEM] * 5 + [HBM],
        "lower",
        scratch + [pltpu.VMEM((L, ROWS, COLS), F32), pltpu.SemaphoreType.DMA],
        out_specs=HBM,
        aliases={6: 0},
        flops=500_000_000, moved=3_000_000,
    )(far(state), conduct, xa, xb, left, right, begun)
    grads = exchange(outgoing)
    grad_top = call(
        gradient_body, sds(2, ROWS, COLS), [VMEM] * 3, "gradient", flops=20_000_000, moved=400_000
    )(grads, picker, adjoint)
    return moisture, brightness, grad_top


def solution(mesh):
    placed = (
        P(None, "gx", "gy"),
        P("gx", "gy"),
        P(),
        P("gx", "gy"),
        P("gx", "gy"),
        P(("gx", "gy"), None, None, None),
        P(("gx", "gy"), None),
        P(("gx", "gy"), None),
        P(("gx", "gy"), None),
    )
    return jax.shard_map(
        on_device,
        mesh=mesh,
        in_specs=placed,
        out_specs=(P(None, "gx", "gy"), P(("gx", "gy"), None), P(None, "gx", "gy")),
        check_vma=False,
    )
```

```python
import jax
import jax.numpy as jnp
from jax import lax
from jax.experimental import pallas as pl
from jax.experimental.pallas import tpu as pltpu
from jax.sharding import PartitionSpec as P

CAP = 4
STEPS = 4
L = 32
ROWS = 64
COLS = 128
WIDE = ROWS + 8
TILES = 128
SLOTS = TILES * CAP
OWN = 32
TOUCH = 4
REFS = OWN * TOUCH
FOOT = 128
F32 = jnp.float32
BF16 = jnp.bfloat16
VMEM = pl.BlockSpec(memory_space=pltpu.VMEM)
SMEM = pl.BlockSpec(memory_space=pltpu.SMEM)
ANY = pl.BlockSpec(memory_space=pl.ANY)
HBM = pl.BlockSpec(memory_space=pltpu.HBM)
LIMIT = 32 * 1024 * 1024


def call(body, outs, in_specs, name, scratch=(), out_specs=None, aliases=None, flops=0, moved=0):
    return pl.pallas_call(
        body,
        out_shape=outs,
        in_specs=in_specs,
        out_specs=out_specs or jax.tree.map(lambda _: VMEM, outs),
        input_output_aliases=aliases or {},
        scratch_shapes=list(scratch),
        name=name,
        compiler_params=pltpu.CompilerParams(vmem_limit_bytes=LIMIT),
        cost_estimate=pl.CostEstimate(flops=flops, bytes_accessed=moved, transcendentals=0),
    )


def iota(shape, dim):
    return lax.broadcasted_iota(jnp.int32, shape, dim)


def far(x):
    return pltpu.with_memory_space_constraint(x, pltpu.HBM)


def dot(a, b, ca, cb):
    return lax.dot_general(a, b, (((ca,), (cb,)), ((), ())), preferred_element_type=F32)


def prep_body(
    classes_hbm, inflow_hbm, category_hbm, state_hbm, thermal_hbm, slot_hbm, strip_hbm, measured_hbm,
    state_ref, conduct_ref, edge_ref, thermal_ref, measured_ref, placing_ref, request_ref,
    inflow_ref, category_ref, classes_ref, slot_ref, strip_ref, sems,
):
    pairs = (
        (slot_hbm, slot_ref),
        (strip_hbm, strip_ref),
        (classes_hbm, classes_ref),
        (category_hbm, category_ref),
        (inflow_hbm, inflow_ref),
        (state_hbm, state_ref),
        (thermal_hbm, thermal_ref),
        (measured_hbm, measured_ref),
    )
    copies = [pltpu.make_async_copy(a, b, sems.at[i]) for i, (a, b) in enumerate(pairs)]
    for copy in copies:
        copy.start()
    copies[0].wait()
    copies[1].wait()
    tile = jnp.concatenate([slot_ref[k : k + 1, :] for k in range(TOUCH)], axis=1)
    row = jnp.concatenate([strip_ref[k : k + 1, :] for k in range(TOUCH)], axis=1)
    sub = iota((TILES, REFS), 0)
    named = (sub == tile).astype(F32)
    before = (sub < iota((REFS, REFS), 1)).astype(F32).astype(BF16)
    rank = jnp.sum(dot(named.astype(BF16), before, 1, 0) * named, axis=0, keepdims=True)
    place = tile * CAP + rank.astype(jnp.int32)
    placing = (iota((SLOTS, REFS), 0) == place).astype(F32).astype(BF16)
    placing_ref[...] = placing
    wanted = (sub == row).astype(F32).astype(BF16)
    request_ref[...] = dot(placing, wanted, 1, 1).astype(BF16)
    copies[2].wait()
    copies[3].wait()
    category = category_ref[...]
    conduct = jnp.zeros((ROWS, COLS), F32)
    for i in range(classes_ref.shape[0]):
        conduct = jnp.where(category == i, classes_ref[i], conduct)
    conduct_ref[...] = conduct
    copies[4].wait()
    copies[5].wait()
    state_ref[0] = state_ref[0] + inflow_ref[...]
    upper = iota((8, COLS), 0) < 4
    edges = jnp.where(upper[None], state_ref[:, 0:8, :], state_ref[:, ROWS - 8 : ROWS, :])
    ends = jnp.where(upper, conduct[0:8], conduct[ROWS - 8 : ROWS])[None]
    whole = jnp.concatenate([edges, ends, jnp.zeros((1, 8, COLS), F32)], axis=0)
    edge_ref[...] = whole.reshape((L + 2) * 8, COLS).astype(BF16)
    for copy in copies[6:]:
        copy.wait()


def row_halo(a_ref, b_ref, levels=L + 1):
    odd = lax.rem(lax.axis_index("gx"), 2)
    a = a_ref[...].astype(F32).reshape(L + 2, 8, COLS)
    b = b_ref[...].astype(F32).reshape(L + 2, 8, COLS)
    half = lax.div(iota((8, COLS), 0), 4)
    return jnp.where(halo_rows_inside()[None], jnp.where((half == odd)[None], a, b), 0.0)


def halo_rows_inside():
    gx = lax.axis_index("gx")
    sub = iota((8, COLS), 0)
    below = (gx < lax.axis_size("gx") - 1).astype(jnp.int32)
    above = (gx > 0).astype(jnp.int32)
    return jnp.where(sub < 4, below, above) > 0


def held(new, inside):
    return jnp.concatenate([new[:ROWS], jnp.where(inside, new[ROWS:], 0.5)], axis=0)


def rows_change(u, k, cd):
    ud = pltpu.roll(u, WIDE - 1, 0)
    f = (k + cd * ud) * (ud - u)
    return f - pltpu.roll(f, 1, 0)


def lanes_change(u, k, cr, cl):
    ur = pltpu.roll(u, COLS - 1, 1)
    ul = pltpu.roll(u, 1, 1)
    return (k + cr * ur) * (ur - u) - (k + cl * ul) * (u - ul)


def pack_body(state_ref, conduct_ref, a_ref, b_ref, own_ref, cond_ref, pa_ref, pb_ref):
    halo = row_halo(a_ref, b_ref)
    lane64 = iota((ROWS, COLS), 1)
    lane8 = iota((8, COLS), 1)
    shifts = (0, -4, 4, 8)

    def pack(levels_of, lane):
        acc = [jnp.zeros(lane.shape, F32) for _ in range(4)]
        for l in range(L):
            turned = levels_of(l)
            if l:
                turned = pltpu.roll(turned, 4 * l, 1)
            group = lane // 4
            for i, at in enumerate((l, (l + 1) % L, (l - 1) % L, (l - 2) % L)):
                acc[i] = jnp.where(group == at, turned, acc[i])
        return [pltpu.roll(x, s % COLS, 1) if s else x for x, s in zip(acc, shifts)]

    def spread(x, lane):
        out = []
        for s in (0, COLS - 4, 4, 8):
            y = jnp.where(lane < 4, pltpu.roll(x, s, 1) if s else x, 0.0)
            for d in (4, 8, 16, 32, 64):
                y = y + pltpu.roll(y, d, 1)
            out.append(y)
        return out

    main = pack(lambda l: state_ref[l], lane64)
    ends = pack(lambda l: halo[l], lane8)
    cmain = spread(conduct_ref[...], lane64)
    cends = spread(halo[L], lane8)
    packs = [jnp.concatenate([m, e], axis=0) for m, e in zip(main, ends)]
    conds = [jnp.concatenate([m, e], axis=0) for m, e in zip(cmain, cends)]
    for i in range(4):
        own_ref[i] = packs[i]
        cond_ref[i] = conds[i]
    odd = lax.rem(lax.axis_index("gy"), 2)
    left = jnp.concatenate([packs[0], conds[0]], axis=0)
    right = jnp.concatenate([packs[2], conds[2]], axis=0)
    is_odd = (jnp.zeros((2 * WIDE, COLS), jnp.int32) + odd) > 0
    pa_ref[...] = jnp.where(is_odd, left, right).astype(BF16)
    pb_ref[...] = jnp.where(is_odd, right, left).astype(BF16)


def strip_body(
    own_ref, cond_ref, pa_ref, pb_ref, tops_ref, thermal_ref,
    left_ref, right_ref, adjoint_ref, bright_ref, u_ref, v_ref, c_ref, cd_ref, cr_ref, cl_ref, lower_ref, upper_ref,
):
    gy = lax.axis_index("gy")
    odd = lax.rem(gy, 2)
    a = pa_ref[...].astype(F32)
    b = pb_ref[...].astype(F32)
    is_odd = (jnp.zeros((2 * WIDE, COLS), jnp.int32) + odd) > 0
    at = jnp.zeros((2 * WIDE, COLS), jnp.int32) + gy
    from_right = jnp.where(at < lax.axis_size("gy") - 1, jnp.where(is_odd, b, a), 0.0)
    from_left = jnp.where(at > 0, jnp.where(is_odd, a, b), 0.0)
    lane = iota((WIDE, COLS), 1)
    last = lax.rem(lane, 4) == 3
    first = lax.rem(lane, 4) == 0
    lowest = lane >= COLS - 4
    highest = lane < 4
    inside = halo_rows_inside()
    in_left = (jnp.zeros((WIDE, COLS), jnp.int32) + gy) > 0
    in_right = (jnp.zeros((WIDE, COLS), jnp.int32) + gy) < lax.axis_size("gy") - 1
    sources = (
        (from_left[:WIDE], from_left[WIDE:]),
        (own_ref[0], cond_ref[0]),
        (own_ref[1], cond_ref[1]),
        (own_ref[3], cond_ref[3]),
        (own_ref[2], cond_ref[2]),
        (from_right[:WIDE], from_right[WIDE:]),
    )
    for i, (s, c) in enumerate(sources):
        u_ref[i] = s + 0.5
        c_ref[i] = 0.5 * c

    def turn(ref):
        for i in range(6):
            lower_ref[i] = pltpu.roll(ref[i], COLS - 4, 1)
            upper_ref[i] = pltpu.roll(ref[i], 4, 1)

    def next_of(ref, i):
        x = jnp.where(first, upper_ref[i + 1], ref[i]) if i % 3 < 2 else ref[i]
        return pltpu.roll(x, COLS - 1, 1)

    def prior_of(ref, i):
        x = jnp.where(last, lower_ref[i - 1], ref[i]) if i % 3 else ref[i]
        return pltpu.roll(x, 1, 1)

    turn(c_ref)
    for i in range(6):
        cd_ref[i] = pltpu.roll(c_ref[i], WIDE - 1, 0)
        cr_ref[i] = next_of(c_ref, i)
        cl_ref[i] = prior_of(c_ref, i)

    for step in range(STEPS):
        now, then = (u_ref, v_ref) if step % 2 == 0 else (v_ref, u_ref)
        turn(now)
        for i in range(6) if step < STEPS - 1 else (1, 4):
            u, c = now[i], c_ref[i]
            k = c * u
            ur, ul = next_of(now, i), prior_of(now, i)
            uz, ua = lower_ref[i], upper_ref[i]
            change = rows_change(u, k, cd_ref[i])
            change = change + ((k + cr_ref[i] * ur) * (ur - u) - (k + cl_ref[i] * ul) * (u - ul))
            down = (k + c * uz) * ((u - uz) + 0.3)
            fall = (c * ua + k) * ((ua - u) + 0.3)
            change = change + (jnp.where(highest, 0.0, fall) - jnp.where(lowest, 0.0, down))
            new = held(u + change, inside)
            if i == 0:
                new = jnp.where(in_left, new, 0.5)
            if i == 5:
                new = jnp.where(in_right, new, 0.5)
            then[i] = new
    left = u_ref[1][:ROWS] - 0.5
    right = u_ref[4][:ROWS] - 0.5
    left_ref[...] = left
    right_ref[...] = right
    lane = iota((ROWS, COLS), 1)

    def joined(l):
        lhs = pltpu.roll(left, COLS - 4 * l, 1) if l else left
        rhs = pltpu.roll(right, COLS - 4 - 4 * l, 1)
        return jnp.where(lane < 4, lhs, jnp.where(lane >= COLS - 4, rhs, tops_ref[l]))

    mix = 0.6 * joined(0) + 0.4 * joined(1)
    thermal = thermal_ref[...]
    bright = (thermal * (1.0 - 0.4 * mix * mix)).astype(BF16)
    adjoint_ref[...] = thermal * (-0.8 * mix)
    bright_ref[...] = jnp.concatenate([bright, jnp.zeros((COLS - ROWS, COLS), BF16)], axis=0)


def serve_body(picker_ref, bright_ref, served_ref):
    served_ref[...] = dot(picker_ref[...], bright_ref[...], 1, 0).astype(BF16)


def wide_conduct(conduct_ref, halo):
    return 0.5 * jnp.concatenate([conduct_ref[...], halo[L]], axis=0)


NEAR = 12


def evolve(state_ref, conduct_ref, a_ref, b_ref, u_ref, c_ref, low, high, finish):
    halo = row_halo(a_ref, b_ref)
    c = wide_conduct(conduct_ref, halo)
    c_ref[0] = c
    c_ref[1] = pltpu.roll(c, WIDE - 1, 0)
    c_ref[2] = pltpu.roll(c, COLS - 1, 1)
    c_ref[3] = pltpu.roll(c, 1, 1)
    inside = halo_rows_inside()
    start, stop = max(0, low - STEPS), min(L, high + STEPS)
    for l in range(start, stop):
        u_ref[l - start] = jnp.concatenate([state_ref[l], halo[l]], axis=0) + 0.5
    for step in range(STEPS):
        top = max(0, low - (STEPS - 1 - step))
        end = min(L, high + (STEPS - 1 - step))
        above = None
        if top > 0:
            u, uz = u_ref[top - 1 - start], u_ref[top - start]
            above = c_ref[0] * (u + uz) * ((u - uz) + 0.3)
        u = u_ref[top - start]
        k = c_ref[0] * u
        for l in range(top, end):
            change = rows_change(u, k, c_ref[1]) + lanes_change(u, k, c_ref[2], c_ref[3])
            if above is not None:
                change = change + above
            if l < L - 1:
                uz = u_ref[l + 1 - start]
                kz = c_ref[0] * uz
                above = (k + kz) * ((u - uz) + 0.3)
                change = change - above
            new = u + change
            if step < STEPS - 1:
                u_ref[l - start] = held(new, inside)
            else:
                finish(l, new[:ROWS] - 0.5)
            u, k = uz, kz


def tops_body(state_ref, conduct_ref, a_ref, b_ref, tops_ref, u_ref, c_ref):
    def finish(l, new):
        tops_ref[l] = new

    evolve(state_ref, conduct_ref, a_ref, b_ref, u_ref, c_ref, 0, 2, finish)


HALF = L // 2
PIECE = 4


def half_body(low, state_ref, conduct_ref, a_ref, b_ref, left_ref, right_ref, out_hbm, u_ref, c_ref, own_ref, sems):
    lane = iota((ROWS, COLS), 1)
    copies = []

    def finish(l, new):
        lhs = pltpu.roll(left_ref[...], (COLS - 4 * l) % COLS, 1) if l else left_ref[...]
        turn = (COLS - 4 - 4 * l) % COLS
        rhs = pltpu.roll(right_ref[...], turn, 1) if turn else right_ref[...]
        own_ref[l - low] = jnp.where(lane < 4, lhs, jnp.where(lane >= COLS - 4, rhs, new))
        if (l + 1) % PIECE == 0:
            at = l + 1 - PIECE
            copy = pltpu.make_async_copy(
                own_ref.at[pl.ds(at - low, PIECE)], out_hbm.at[pl.ds(at, PIECE)], sems.at[len(copies)]
            )
            copy.start()
            copies.append(copy)

    evolve(state_ref, conduct_ref, a_ref, b_ref, u_ref, c_ref, low, low + HALF, finish)
    for copy in copies:
        copy.wait()


def upper_body(
    state_ref, conduct_ref, a_ref, b_ref, left_ref, right_ref, weights_hbm, out_hbm, weights_ref, *scratch
):
    copy = pltpu.make_async_copy(weights_hbm.at[pl.ds(0, NEAR)], weights_ref, scratch[-1])
    copy.start()
    half_body(0, state_ref, conduct_ref, a_ref, b_ref, left_ref, right_ref, out_hbm, *scratch[:-1])
    copy.wait()


def lower_body(
    state_hbm, conduct_ref, a_ref, b_ref, left_ref, right_ref, begun_hbm, out_hbm, *scratch
):
    state_ref, sem = scratch[-2:]
    span = pl.ds(HALF - STEPS, L - HALF + STEPS)
    copy = pltpu.make_async_copy(state_hbm.at[span], state_ref.at[span], sem)
    copy.start()
    copy.wait()
    half_body(HALF, state_ref, conduct_ref, a_ref, b_ref, left_ref, right_ref, out_hbm, *scratch[:-2])


PART = 4
CHUNKS = (8, 12)


def foot_body(
    returned_ref, placing_ref, seen_ref, near_ref, weights_hbm,
    bright_ref, outgoing_ref, cells_ref, contrib_ref, weights_ref, sems,
):
    copies = {}
    at = NEAR
    for i, count in enumerate(CHUNKS):
        span = pl.ds(at, count)
        copies[at] = pltpu.make_async_copy(weights_hbm.at[span], weights_ref.at[span], sems.at[i])
        copies[at].start()
        at += count
    placing = placing_ref[...]
    cells_ref[...] = dot(placing, returned_ref[...], 0, 0)
    lane = iota((FOOT, COLS), 1)

    def weights(b, k):
        return near_ref[b, k] if b < NEAR else weights_ref[b, k]

    def adjoint(start, misfit):
        for i in range(PART):
            for k in range(TOUCH):
                at = k * OWN + start + i
                contrib_ref[at : at + 1, :] = dot(misfit[i : i + 1], weights(start + i, k), 1, 0)

    misfit = None
    for start in range(0, OWN, PART):
        if start in copies:
            copies[start].wait()
        sums = jnp.zeros((FOOT, COLS), F32)
        for i in range(PART):
            total = None
            for k in range(TOUCH):
                at = k * OWN + start + i
                term = weights(start + i, k).astype(F32) * cells_ref[at : at + 1, :]
                total = term if total is None else total + term
            sums = jnp.where(lane == i, jnp.sum(total, axis=1, keepdims=True), sums)
        if start:
            adjoint(start - PART, misfit)
        evolved = jnp.transpose(sums)[:PART]
        bright_ref[start : start + PART, :] = evolved
        misfit = (evolved - seen_ref[start : start + PART, :]).astype(BF16)
    adjoint(OWN - PART, misfit)
    outgoing_ref[...] = dot(placing, contrib_ref[...].astype(BF16), 1, 0).astype(BF16)


def gradient_body(grads_ref, picker_ref, adjoint_ref, out_ref):
    summed = dot(picker_ref[...], grads_ref[...], 0, 0)[:ROWS]
    common = summed * adjoint_ref[...]
    out_ref[0] = 0.6 * common
    out_ref[1] = 0.4 * common


def swapped(x, axis):
    n = lax.axis_size(axis)
    one = [(i, i ^ 1) for i in range(n)]
    two = [(i, (i + 1) % n) for i in range(1, n, 2)] + [((i + 1) % n, i) for i in range(1, n, 2)]
    return lax.ppermute(x[0], axis, one), lax.ppermute(x[1], axis, two)


def exchange(x):
    return lax.all_to_all(
        x.reshape(TILES, CAP, COLS), ("gx", "gy"), split_axis=0, concat_axis=0, tiled=True
    ).reshape(SLOTS, COLS)


def on_device(state, inflow, classes, category, thermal, weights, slots, strips, measured):
    def sds(*shape, dtype=F32):
        return jax.ShapeDtypeStruct(shape, dtype)

    held_state, conduct, edge, warm, seen, placing, request = call(
        prep_body,
        (
            sds(L, ROWS, COLS), sds(ROWS, COLS), sds((L + 2) * 8, COLS, dtype=BF16), sds(ROWS, COLS),
            sds(OWN, FOOT), sds(SLOTS, REFS, dtype=BF16), sds(SLOTS, COLS, dtype=BF16),
        ),
        [HBM] * 8,
        "prep",
        [
            pltpu.VMEM((ROWS, COLS), F32),
            pltpu.VMEM((ROWS, COLS), jnp.int32),
            pltpu.SMEM(classes.shape, F32),
            pltpu.VMEM((TOUCH, OWN), jnp.int32),
            pltpu.VMEM((TOUCH, OWN), jnp.int32),
            pltpu.SemaphoreType.DMA((8,)),
        ],
        flops=20_000_000, moved=2_000_000,
    )(*(far(x) for x in (classes, inflow, category, state, thermal, slots.T, strips.T, measured)))
    xa, xb = swapped((edge, edge), "gx")
    picker = exchange(request)
    own, cond, pa, pb = call(
        pack_body,
        (sds(4, WIDE, COLS), sds(4, WIDE, COLS), sds(2 * WIDE, COLS, dtype=BF16), sds(2 * WIDE, COLS, dtype=BF16)),
        [VMEM] * 4,
        "pack",
        flops=20_000_000_000, moved=1_500_000,
    )(held_state, conduct, xa, xb)
    ya, yb = swapped((pa, pb), "gy")
    tops = call(
        tops_body,
        sds(2, ROWS, COLS),
        [VMEM] * 4,
        "tops",
        [pltpu.VMEM((STEPS + 2, WIDE, COLS), F32), pltpu.VMEM((4, WIDE, COLS), F32)],
        flops=20_000_000_000, moved=1_000_000,
    )(held_state, conduct, xa, xb)
    left, right, adjoint, bright = call(
        strip_body,
        (sds(ROWS, COLS), sds(ROWS, COLS), sds(ROWS, COLS), sds(COLS, COLS, dtype=BF16)),
        [VMEM] * 6,
        "strips",
        [pltpu.VMEM((6, WIDE, COLS), F32)] * 8,
        flops=10_000_000_000, moved=1_000_000,
    )(own, cond, ya, yb, tops, warm)
    served = call(
        serve_body,
        sds(SLOTS, COLS, dtype=BF16),
        [VMEM] * 2,
        "serve",
        flops=20_000_000, moved=300_000,
    )(picker, bright)
    returned = exchange(served)
    scratch = [
        pltpu.VMEM((HALF + STEPS, WIDE, COLS), F32),
        pltpu.VMEM((4, WIDE, COLS), F32),
        pltpu.VMEM((HALF, ROWS, COLS), F32),
        pltpu.SemaphoreType.DMA((HALF // PIECE,)),
    ]
    begun, near = call(
        upper_body,
        (sds(L, ROWS, COLS), sds(NEAR, TOUCH, FOOT, COLS, dtype=BF16)),
        [VMEM] * 6 + [HBM],
        "upper",
        scratch + [pltpu.SemaphoreType.DMA],
        out_specs=(HBM, VMEM),
        flops=500_000_000, moved=3_000_000,
    )(held_state, conduct, xa, xb, left, right, far(weights))
    brightness, outgoing = call(
        foot_body,
        (sds(OWN, FOOT), sds(SLOTS, COLS, dtype=BF16)),
        [VMEM] * 4 + [HBM],
        "footprints",
        [
            pltpu.VMEM((REFS, COLS), F32),
            pltpu.VMEM((REFS, COLS), F32),
            pltpu.VMEM(weights.shape, BF16),
            pltpu.SemaphoreType.DMA((len(CHUNKS),)),
        ],
        flops=20_000_000, moved=5_000_000,
    )(returned, placing, seen, near, far(weights))
    moisture = call(
        lower_body,
        sds(L, ROWS, COLS),
        [HBM] + [VMEM] * 5 + [HBM],
        "lower",
        scratch + [pltpu.VMEM((L, ROWS, COLS), F32), pltpu.SemaphoreType.DMA],
        out_specs=HBM,
        aliases={6: 0},
        flops=500_000_000, moved=3_000_000,
    )(far(state), conduct, xa, xb, left, right, begun)
    grads = exchange(outgoing)
    grad_top = call(
        gradient_body, sds(2, ROWS, COLS), [VMEM] * 3, "gradient", flops=20_000_000, moved=400_000
    )(grads, picker, adjoint)
    return moisture, brightness, grad_top


def solution(mesh):
    placed = (
        P(None, "gx", "gy"),
        P("gx", "gy"),
        P(),
        P("gx", "gy"),
        P("gx", "gy"),
        P(("gx", "gy"), None, None, None),
        P(("gx", "gy"), None),
        P(("gx", "gy"), None),
        P(("gx", "gy"), None),
    )
    return jax.shard_map(
        on_device,
        mesh=mesh,
        in_specs=placed,
        out_specs=(P(None, "gx", "gy"), P(("gx", "gy"), None), P(None, "gx", "gy")),
        check_vma=False,
    )
```

```python
import jax
import jax.numpy as jnp
from jax import lax
from jax.experimental import pallas as pl
from jax.experimental.pallas import tpu as pltpu
from jax.sharding import PartitionSpec as P

CAP = 4
STEPS = 4
L = 32
ROWS = 64
COLS = 128
WIDE = ROWS + 8
TILES = 128
SLOTS = TILES * CAP
OWN = 32
TOUCH = 4
REFS = OWN * TOUCH
FOOT = 128
F32 = jnp.float32
BF16 = jnp.bfloat16
VMEM = pl.BlockSpec(memory_space=pltpu.VMEM)
SMEM = pl.BlockSpec(memory_space=pltpu.SMEM)
ANY = pl.BlockSpec(memory_space=pl.ANY)
HBM = pl.BlockSpec(memory_space=pltpu.HBM)
LIMIT = 32 * 1024 * 1024


def call(body, outs, in_specs, name, scratch=(), out_specs=None, aliases=None, flops=0, moved=0):
    return pl.pallas_call(
        body,
        out_shape=outs,
        in_specs=in_specs,
        out_specs=out_specs or jax.tree.map(lambda _: VMEM, outs),
        input_output_aliases=aliases or {},
        scratch_shapes=list(scratch),
        name=name,
        compiler_params=pltpu.CompilerParams(vmem_limit_bytes=LIMIT),
        cost_estimate=pl.CostEstimate(flops=flops, bytes_accessed=moved, transcendentals=0),
    )


def iota(shape, dim):
    return lax.broadcasted_iota(jnp.int32, shape, dim)


def far(x):
    return pltpu.with_memory_space_constraint(x, pltpu.HBM)


def dot(a, b, ca, cb):
    return lax.dot_general(a, b, (((ca,), (cb,)), ((), ())), preferred_element_type=F32)


def prep_body(
    classes_hbm, inflow_hbm, category_hbm, state_hbm, thermal_hbm, slot_hbm, strip_hbm, measured_hbm,
    state_ref, conduct_ref, edge_ref, thermal_ref, measured_ref, placing_ref, request_hbm,
    inflow_ref, category_ref, classes_ref, slot_ref, strip_ref, asked_ref, sems,
):
    pairs = (
        (slot_hbm, slot_ref),
        (strip_hbm, strip_ref),
        (classes_hbm, classes_ref),
        (category_hbm, category_ref),
        (inflow_hbm, inflow_ref),
        (state_hbm, state_ref),
        (thermal_hbm, thermal_ref),
        (measured_hbm, measured_ref),
    )
    copies = [pltpu.make_async_copy(a, b, sems.at[i]) for i, (a, b) in enumerate(pairs)]
    for copy in copies:
        copy.start()
    for copy in copies[:4]:
        copy.wait()
    tile = jnp.concatenate([slot_ref[k : k + 1, :] for k in range(TOUCH)], axis=1)
    row = jnp.concatenate([strip_ref[k : k + 1, :] for k in range(TOUCH)], axis=1)
    sub = iota((TILES, REFS), 0)
    named = (sub == tile).astype(F32)
    before = (sub < iota((REFS, REFS), 1)).astype(F32).astype(BF16)
    rank = jnp.sum(dot(named.astype(BF16), before, 1, 0) * named, axis=0, keepdims=True)
    place = tile * CAP + rank.astype(jnp.int32)
    placing = (iota((SLOTS, REFS), 0) == place).astype(F32).astype(BF16)
    placing_ref[...] = placing
    wanted = (sub == row).astype(F32).astype(BF16)
    asked_ref[...] = dot(placing, wanted, 1, 1).astype(BF16)
    leaving = pltpu.make_async_copy(asked_ref, request_hbm, sems.at[len(pairs)])
    leaving.start()
    category = category_ref[...]
    conduct = jnp.zeros((ROWS, COLS), F32)
    for i in range(classes_ref.shape[0]):
        conduct = jnp.where(category == i, classes_ref[i], conduct)
    conduct_ref[...] = conduct
    copies[4].wait()
    copies[5].wait()
    state_ref[0] = state_ref[0] + inflow_ref[...]
    upper = iota((8, COLS), 0) < 4
    edges = jnp.where(upper[None], state_ref[:, 0:8, :], state_ref[:, ROWS - 8 : ROWS, :])
    ends = jnp.where(upper, conduct[0:8], conduct[ROWS - 8 : ROWS])[None]
    whole = jnp.concatenate([edges, ends, jnp.zeros((1, 8, COLS), F32)], axis=0)
    edge_ref[...] = whole.reshape((L + 2) * 8, COLS).astype(BF16)
    for copy in copies[6:]:
        copy.wait()
    leaving.wait()


def row_halo(a_ref, b_ref, levels=L + 1):
    odd = lax.rem(lax.axis_index("gx"), 2)
    a = a_ref[...].astype(F32).reshape(L + 2, 8, COLS)
    b = b_ref[...].astype(F32).reshape(L + 2, 8, COLS)
    half = lax.div(iota((8, COLS), 0), 4)
    return jnp.where(halo_rows_inside()[None], jnp.where((half == odd)[None], a, b), 0.0)


def halo_rows_inside():
    gx = lax.axis_index("gx")
    sub = iota((8, COLS), 0)
    below = (gx < lax.axis_size("gx") - 1).astype(jnp.int32)
    above = (gx > 0).astype(jnp.int32)
    return jnp.where(sub < 4, below, above) > 0


def held(new, inside):
    return jnp.concatenate([new[:ROWS], jnp.where(inside, new[ROWS:], 0.5)], axis=0)


def rows_change(u, k, cd):
    ud = pltpu.roll(u, WIDE - 1, 0)
    f = (k + cd * ud) * (ud - u)
    return f - pltpu.roll(f, 1, 0)


def lanes_change(u, k, cr, cl):
    ur = pltpu.roll(u, COLS - 1, 1)
    ul = pltpu.roll(u, 1, 1)
    return (k + cr * ur) * (ur - u) - (k + cl * ul) * (u - ul)


def pack_body(state_ref, conduct_ref, a_ref, b_ref, own_ref, cond_ref, pa_ref, pb_ref):
    halo = row_halo(a_ref, b_ref)
    lane64 = iota((ROWS, COLS), 1)
    lane8 = iota((8, COLS), 1)
    shifts = (0, -4, 4, 8)

    def pack(levels_of, lane):
        acc = [jnp.zeros(lane.shape, F32) for _ in range(4)]
        for l in range(L):
            turned = levels_of(l)
            if l:
                turned = pltpu.roll(turned, 4 * l, 1)
            group = lane // 4
            for i, at in enumerate((l, (l + 1) % L, (l - 1) % L, (l - 2) % L)):
                acc[i] = jnp.where(group == at, turned, acc[i])
        return [pltpu.roll(x, s % COLS, 1) if s else x for x, s in zip(acc, shifts)]

    def spread(x, lane):
        out = []
        for s in (0, COLS - 4, 4, 8):
            y = jnp.where(lane < 4, pltpu.roll(x, s, 1) if s else x, 0.0)
            for d in (4, 8, 16, 32, 64):
                y = y + pltpu.roll(y, d, 1)
            out.append(y)
        return out

    main = pack(lambda l: state_ref[l], lane64)
    ends = pack(lambda l: halo[l], lane8)
    cmain = spread(conduct_ref[...], lane64)
    cends = spread(halo[L], lane8)
    packs = [jnp.concatenate([m, e], axis=0) for m, e in zip(main, ends)]
    conds = [jnp.concatenate([m, e], axis=0) for m, e in zip(cmain, cends)]
    for i in range(4):
        own_ref[i] = packs[i]
        cond_ref[i] = conds[i]
    odd = lax.rem(lax.axis_index("gy"), 2)
    left = jnp.concatenate([packs[0], conds[0]], axis=0)
    right = jnp.concatenate([packs[2], conds[2]], axis=0)
    is_odd = (jnp.zeros((2 * WIDE, COLS), jnp.int32) + odd) > 0
    pa_ref[...] = jnp.where(is_odd, left, right).astype(BF16)
    pb_ref[...] = jnp.where(is_odd, right, left).astype(BF16)


def strip_body(
    own_ref, cond_ref, pa_ref, pb_ref, tops_ref, thermal_ref,
    left_ref, right_ref, adjoint_ref, bright_ref, u_ref, v_ref, c_ref, cd_ref, cr_ref, cl_ref, lower_ref, upper_ref,
):
    gy = lax.axis_index("gy")
    odd = lax.rem(gy, 2)
    a = pa_ref[...].astype(F32)
    b = pb_ref[...].astype(F32)
    is_odd = (jnp.zeros((2 * WIDE, COLS), jnp.int32) + odd) > 0
    at = jnp.zeros((2 * WIDE, COLS), jnp.int32) + gy
    from_right = jnp.where(at < lax.axis_size("gy") - 1, jnp.where(is_odd, b, a), 0.0)
    from_left = jnp.where(at > 0, jnp.where(is_odd, a, b), 0.0)
    lane = iota((WIDE, COLS), 1)
    last = lax.rem(lane, 4) == 3
    first = lax.rem(lane, 4) == 0
    lowest = lane >= COLS - 4
    highest = lane < 4
    inside = halo_rows_inside()
    in_left = (jnp.zeros((WIDE, COLS), jnp.int32) + gy) > 0
    in_right = (jnp.zeros((WIDE, COLS), jnp.int32) + gy) < lax.axis_size("gy") - 1
    sources = (
        (from_left[:WIDE], from_left[WIDE:]),
        (own_ref[0], cond_ref[0]),
        (own_ref[1], cond_ref[1]),
        (own_ref[3], cond_ref[3]),
        (own_ref[2], cond_ref[2]),
        (from_right[:WIDE], from_right[WIDE:]),
    )
    for i, (s, c) in enumerate(sources):
        u_ref[i] = s + 0.5
        c_ref[i] = 0.5 * c

    def turn(ref):
        for i in range(6):
            lower_ref[i] = pltpu.roll(ref[i], COLS - 4, 1)
            upper_ref[i] = pltpu.roll(ref[i], 4, 1)

    def next_of(ref, i):
        x = jnp.where(first, upper_ref[i + 1], ref[i]) if i % 3 < 2 else ref[i]
        return pltpu.roll(x, COLS - 1, 1)

    def prior_of(ref, i):
        x = jnp.where(last, lower_ref[i - 1], ref[i]) if i % 3 else ref[i]
        return pltpu.roll(x, 1, 1)

    turn(c_ref)
    for i in range(6):
        cd_ref[i] = pltpu.roll(c_ref[i], WIDE - 1, 0)
        cr_ref[i] = next_of(c_ref, i)
        cl_ref[i] = prior_of(c_ref, i)

    for step in range(STEPS):
        now, then = (u_ref, v_ref) if step % 2 == 0 else (v_ref, u_ref)
        turn(now)
        for i in range(6) if step < STEPS - 1 else (1, 4):
            u, c = now[i], c_ref[i]
            k = c * u
            ur, ul = next_of(now, i), prior_of(now, i)
            uz, ua = lower_ref[i], upper_ref[i]
            change = rows_change(u, k, cd_ref[i])
            change = change + ((k + cr_ref[i] * ur) * (ur - u) - (k + cl_ref[i] * ul) * (u - ul))
            down = (k + c * uz) * ((u - uz) + 0.3)
            fall = (c * ua + k) * ((ua - u) + 0.3)
            change = change + (jnp.where(highest, 0.0, fall) - jnp.where(lowest, 0.0, down))
            new = held(u + change, inside)
            if i == 0:
                new = jnp.where(in_left, new, 0.5)
            if i == 5:
                new = jnp.where(in_right, new, 0.5)
            then[i] = new
    left = u_ref[1][:ROWS] - 0.5
    right = u_ref[4][:ROWS] - 0.5
    left_ref[...] = left
    right_ref[...] = right
    lane = iota((ROWS, COLS), 1)

    def joined(l):
        lhs = pltpu.roll(left, COLS - 4 * l, 1) if l else left
        rhs = pltpu.roll(right, COLS - 4 - 4 * l, 1)
        return jnp.where(lane < 4, lhs, jnp.where(lane >= COLS - 4, rhs, tops_ref[l]))

    mix = 0.6 * joined(0) + 0.4 * joined(1)
    thermal = thermal_ref[...]
    bright = (thermal * (1.0 - 0.4 * mix * mix)).astype(BF16)
    adjoint_ref[...] = thermal * (-0.8 * mix)
    bright_ref[...] = jnp.concatenate([bright, jnp.zeros((COLS - ROWS, COLS), BF16)], axis=0)


def serve_body(picker_ref, bright_ref, served_ref):
    served_ref[...] = dot(picker_ref[...], bright_ref[...], 1, 0).astype(BF16)


def wide_conduct(conduct_ref, halo):
    return 0.5 * jnp.concatenate([conduct_ref[...], halo[L]], axis=0)


NEAR = 12


def evolve(state_ref, conduct_ref, a_ref, b_ref, u_ref, c_ref, low, high, finish):
    halo = row_halo(a_ref, b_ref)
    c = wide_conduct(conduct_ref, halo)
    c_ref[0] = c
    c_ref[1] = pltpu.roll(c, WIDE - 1, 0)
    c_ref[2] = pltpu.roll(c, COLS - 1, 1)
    c_ref[3] = pltpu.roll(c, 1, 1)
    inside = halo_rows_inside()
    start, stop = max(0, low - STEPS), min(L, high + STEPS)
    for l in range(start, stop):
        u_ref[l - start] = jnp.concatenate([state_ref[l], halo[l]], axis=0) + 0.5
    for step in range(STEPS):
        top = max(0, low - (STEPS - 1 - step))
        end = min(L, high + (STEPS - 1 - step))
        above = None
        if top > 0:
            u, uz = u_ref[top - 1 - start], u_ref[top - start]
            above = c_ref[0] * (u + uz) * ((u - uz) + 0.3)
        u = u_ref[top - start]
        k = c_ref[0] * u
        for l in range(top, end):
            change = rows_change(u, k, c_ref[1]) + lanes_change(u, k, c_ref[2], c_ref[3])
            if above is not None:
                change = change + above
            if l < L - 1:
                uz = u_ref[l + 1 - start]
                kz = c_ref[0] * uz
                above = (k + kz) * ((u - uz) + 0.3)
                change = change - above
            new = u + change
            if step < STEPS - 1:
                u_ref[l - start] = held(new, inside)
            else:
                finish(l, new[:ROWS] - 0.5)
            u, k = uz, kz


def turned(ref):
    parts = [
        jnp.transpose(ref[i : i + COLS, :].astype(F32)).astype(BF16) for i in range(0, SLOTS, COLS)
    ]
    return jnp.concatenate(parts, axis=1)


def tops_body(state_ref, conduct_ref, a_ref, b_ref, tops_ref, u_ref, c_ref):
    def finish(l, new):
        tops_ref[l] = new

    evolve(state_ref, conduct_ref, a_ref, b_ref, u_ref, c_ref, 0, 2, finish)


HALF = L // 2
PIECE = 4


def half_body(low, state_ref, conduct_ref, a_ref, b_ref, left_ref, right_ref, out_hbm, u_ref, c_ref, own_ref, sems):
    lane = iota((ROWS, COLS), 1)
    copies = []

    def finish(l, new):
        lhs = pltpu.roll(left_ref[...], (COLS - 4 * l) % COLS, 1) if l else left_ref[...]
        turn = (COLS - 4 - 4 * l) % COLS
        rhs = pltpu.roll(right_ref[...], turn, 1) if turn else right_ref[...]
        own_ref[l - low] = jnp.where(lane < 4, lhs, jnp.where(lane >= COLS - 4, rhs, new))
        if (l + 1) % PIECE == 0:
            at = l + 1 - PIECE
            copy = pltpu.make_async_copy(
                own_ref.at[pl.ds(at - low, PIECE)], out_hbm.at[pl.ds(at, PIECE)], sems.at[len(copies)]
            )
            copy.start()
            copies.append(copy)

    evolve(state_ref, conduct_ref, a_ref, b_ref, u_ref, c_ref, low, low + HALF, finish)
    for copy in copies:
        copy.wait()


def upper_body(
    state_ref, conduct_ref, a_ref, b_ref, left_ref, right_ref, picker_ref, weights_hbm,
    out_hbm, weights_ref, across_ref, *scratch,
):
    copy = pltpu.make_async_copy(weights_hbm.at[pl.ds(0, NEAR)], weights_ref, scratch[-1])
    copy.start()
    across_ref[...] = turned(picker_ref)
    half_body(0, state_ref, conduct_ref, a_ref, b_ref, left_ref, right_ref, out_hbm, *scratch[:-1])
    copy.wait()


def lower_body(
    state_hbm, conduct_ref, a_ref, b_ref, left_ref, right_ref, begun_hbm, out_hbm, *scratch
):
    state_ref, sem = scratch[-2:]
    span = pl.ds(HALF - STEPS, L - HALF + STEPS)
    copy = pltpu.make_async_copy(state_hbm.at[span], state_ref.at[span], sem)
    copy.start()
    copy.wait()
    half_body(HALF, state_ref, conduct_ref, a_ref, b_ref, left_ref, right_ref, out_hbm, *scratch[:-2])


PART = 4
CHUNKS = (8, 12)


def foot_body(
    returned_ref, placing_ref, seen_ref, near_ref, weights_hbm,
    bright_ref, outgoing_ref, cells_ref, contrib_ref, weights_ref, sems,
):
    copies = {}
    at = NEAR
    for i, count in enumerate(CHUNKS):
        span = pl.ds(at, count)
        copies[at] = pltpu.make_async_copy(weights_hbm.at[span], weights_ref.at[span], sems.at[i])
        copies[at].start()
        at += count
    placing = placing_ref[...]
    cells_ref[...] = dot(placing, returned_ref[...], 0, 0)
    lane = iota((FOOT, COLS), 1)

    def weights(b, k):
        return near_ref[b, k] if b < NEAR else weights_ref[b, k]

    def adjoint(start, misfit):
        for i in range(PART):
            for k in range(TOUCH):
                at = k * OWN + start + i
                contrib_ref[at : at + 1, :] = dot(misfit[i : i + 1], weights(start + i, k), 1, 0)

    misfit = None
    for start in range(0, OWN, PART):
        if start in copies:
            copies[start].wait()
        sums = jnp.zeros((FOOT, COLS), F32)
        for i in range(PART):
            total = None
            for k in range(TOUCH):
                at = k * OWN + start + i
                term = weights(start + i, k).astype(F32) * cells_ref[at : at + 1, :]
                total = term if total is None else total + term
            sums = jnp.where(lane == i, jnp.sum(total, axis=1, keepdims=True), sums)
        if start:
            adjoint(start - PART, misfit)
        evolved = jnp.transpose(sums)[:PART]
        bright_ref[start : start + PART, :] = evolved
        misfit = (evolved - seen_ref[start : start + PART, :]).astype(BF16)
    adjoint(OWN - PART, misfit)
    outgoing_ref[...] = dot(placing, contrib_ref[...].astype(BF16), 1, 0).astype(BF16)


def gradient_body(grads_ref, across_ref, adjoint_ref, out_ref):
    summed = dot(across_ref[0:ROWS, :], grads_ref[...], 1, 0)
    common = summed * adjoint_ref[...]
    out_ref[0] = 0.6 * common
    out_ref[1] = 0.4 * common


def swapped(x, axis):
    n, m = lax.axis_size(axis), lax.axis_size("gy" if axis == "gx" else "gx")

    def place(along, across):
        return along * m + across if axis == "gx" else across * n + along

    one = [(i, i ^ 1) for i in range(n)]
    two = []
    for j in range(m):
        two += [(place(i, j), place(i, j ^ 1)) for i in (0, n - 1)]
        for i in range(1, n - 1, 2):
            two += [(place(i, j), place(i + 1, j)), (place(i + 1, j), place(i, j))]
    return lax.ppermute(x[0], axis, one), lax.ppermute(x[1], ("gx", "gy"), two)


def exchange(x):
    return lax.all_to_all(
        x.reshape(TILES, CAP, COLS), ("gx", "gy"), split_axis=0, concat_axis=0, tiled=True
    ).reshape(SLOTS, COLS)


def on_device(state, inflow, classes, category, thermal, weights, slots, strips, measured):
    def sds(*shape, dtype=F32):
        return jax.ShapeDtypeStruct(shape, dtype)

    held_state, conduct, edge, warm, seen, placing, request = call(
        prep_body,
        (
            sds(L, ROWS, COLS), sds(ROWS, COLS), sds((L + 2) * 8, COLS, dtype=BF16), sds(ROWS, COLS),
            sds(OWN, FOOT), sds(SLOTS, REFS, dtype=BF16), sds(SLOTS, COLS, dtype=BF16),
        ),
        [HBM] * 8,
        "prep",
        [
            pltpu.VMEM((ROWS, COLS), F32),
            pltpu.VMEM((ROWS, COLS), jnp.int32),
            pltpu.SMEM(classes.shape, F32),
            pltpu.VMEM((TOUCH, OWN), jnp.int32),
            pltpu.VMEM((TOUCH, OWN), jnp.int32),
            pltpu.VMEM((SLOTS, COLS), BF16),
            pltpu.SemaphoreType.DMA((9,)),
        ],
        out_specs=(VMEM,) * 6 + (HBM,),
        flops=20_000_000, moved=2_000_000,
    )(*(far(x) for x in (classes, inflow, category, state, thermal, slots.T, strips.T, measured)))
    xa, xb = swapped((edge, edge), "gx")
    picker = exchange(request)
    own, cond, pa, pb = call(
        pack_body,
        (sds(4, WIDE, COLS), sds(4, WIDE, COLS), sds(2 * WIDE, COLS, dtype=BF16), sds(2 * WIDE, COLS, dtype=BF16)),
        [VMEM] * 4,
        "pack",
        flops=20_000_000_000, moved=1_500_000,
    )(held_state, conduct, xa, xb)
    ya, yb = swapped((pa, pb), "gy")
    tops = call(
        tops_body,
        sds(2, ROWS, COLS),
        [VMEM] * 4,
        "tops",
        [pltpu.VMEM((STEPS + 2, WIDE, COLS), F32), pltpu.VMEM((4, WIDE, COLS), F32)],
        flops=20_000_000_000, moved=1_000_000,
    )(held_state, conduct, xa, xb)
    left, right, adjoint, bright = call(
        strip_body,
        (sds(ROWS, COLS), sds(ROWS, COLS), sds(ROWS, COLS), sds(COLS, COLS, dtype=BF16)),
        [VMEM] * 6,
        "strips",
        [pltpu.VMEM((6, WIDE, COLS), F32)] * 8,
        flops=10_000_000_000, moved=1_000_000,
    )(own, cond, ya, yb, tops, warm)
    served = call(
        serve_body,
        sds(SLOTS, COLS, dtype=BF16),
        [VMEM] * 2,
        "serve",
        flops=20_000_000, moved=300_000,
    )(picker, bright)
    returned = exchange(served)
    scratch = [
        pltpu.VMEM((HALF + STEPS, WIDE, COLS), F32),
        pltpu.VMEM((4, WIDE, COLS), F32),
        pltpu.VMEM((HALF, ROWS, COLS), F32),
        pltpu.SemaphoreType.DMA((HALF // PIECE,)),
    ]
    begun, near, picker_across = call(
        upper_body,
        (
            sds(L, ROWS, COLS), sds(NEAR, TOUCH, FOOT, COLS, dtype=BF16), sds(COLS, SLOTS, dtype=BF16)
        ),
        [VMEM] * 7 + [HBM],
        "upper",
        scratch + [pltpu.SemaphoreType.DMA],
        out_specs=(HBM, VMEM, VMEM),
        flops=500_000_000, moved=3_000_000,
    )(held_state, conduct, xa, xb, left, right, picker, far(weights))
    brightness, outgoing = call(
        foot_body,
        (sds(OWN, FOOT), sds(SLOTS, COLS, dtype=BF16)),
        [VMEM] * 4 + [HBM],
        "footprints",
        [
            pltpu.VMEM((REFS, COLS), F32),
            pltpu.VMEM((REFS, COLS), F32),
            pltpu.VMEM(weights.shape, BF16),
            pltpu.SemaphoreType.DMA((len(CHUNKS),)),
        ],
        flops=20_000_000, moved=5_000_000,
    )(returned, placing, seen, near, far(weights))
    moisture = call(
        lower_body,
        sds(L, ROWS, COLS),
        [HBM] + [VMEM] * 5 + [HBM],
        "lower",
        scratch + [pltpu.VMEM((L, ROWS, COLS), F32), pltpu.SemaphoreType.DMA],
        out_specs=HBM,
        aliases={6: 0},
        flops=500_000_000, moved=3_000_000,
    )(far(state), conduct, xa, xb, left, right, begun)
    grads = exchange(outgoing)
    grad_top = call(
        gradient_body, sds(2, ROWS, COLS), [VMEM] * 3, "gradient", flops=20_000_000, moved=400_000
    )(grads, picker_across, adjoint)
    return moisture, brightness, grad_top


def solution(mesh):
    placed = (
        P(None, "gx", "gy"),
        P("gx", "gy"),
        P(),
        P("gx", "gy"),
        P("gx", "gy"),
        P(("gx", "gy"), None, None, None),
        P(("gx", "gy"), None),
        P(("gx", "gy"), None),
        P(("gx", "gy"), None),
    )
    return jax.shard_map(
        on_device,
        mesh=mesh,
        in_specs=placed,
        out_specs=(P(None, "gx", "gy"), P(("gx", "gy"), None), P(None, "gx", "gy")),
        check_vma=False,
    )
```

```python
import jax
import jax.numpy as jnp
from jax import lax
from jax.experimental import pallas as pl
from jax.experimental.pallas import tpu as pltpu
from jax.sharding import PartitionSpec as P

CAP = 4
STEPS = 4
L = 32
ROWS = 64
COLS = 128
WIDE = ROWS + 8
TILES = 128
SLOTS = TILES * CAP
OWN = 32
TOUCH = 4
REFS = OWN * TOUCH
FOOT = 128
F32 = jnp.float32
BF16 = jnp.bfloat16
VMEM = pl.BlockSpec(memory_space=pltpu.VMEM)
SMEM = pl.BlockSpec(memory_space=pltpu.SMEM)
ANY = pl.BlockSpec(memory_space=pl.ANY)
HBM = pl.BlockSpec(memory_space=pltpu.HBM)
LIMIT = 32 * 1024 * 1024


def call(body, outs, in_specs, name, scratch=(), out_specs=None, aliases=None, flops=0, moved=0):
    return pl.pallas_call(
        body,
        out_shape=outs,
        in_specs=in_specs,
        out_specs=out_specs or jax.tree.map(lambda _: VMEM, outs),
        input_output_aliases=aliases or {},
        scratch_shapes=list(scratch),
        name=name,
        compiler_params=pltpu.CompilerParams(vmem_limit_bytes=LIMIT),
        cost_estimate=pl.CostEstimate(flops=flops, bytes_accessed=moved, transcendentals=0),
    )


def iota(shape, dim):
    return lax.broadcasted_iota(jnp.int32, shape, dim)


def far(x):
    return pltpu.with_memory_space_constraint(x, pltpu.HBM)


def dot(a, b, ca, cb):
    return lax.dot_general(a, b, (((ca,), (cb,)), ((), ())), preferred_element_type=F32)


def prep_body(
    classes_hbm, inflow_hbm, category_hbm, state_hbm, thermal_hbm, slot_hbm, strip_hbm, measured_hbm,
    state_ref, conduct_ref, edge_ref, thermal_ref, measured_ref, placing_ref, request_hbm,
    inflow_ref, category_ref, classes_ref, slot_ref, strip_ref, asked_ref, sems,
):
    pairs = (
        (slot_hbm, slot_ref),
        (strip_hbm, strip_ref),
        (classes_hbm, classes_ref),
        (category_hbm, category_ref),
        (inflow_hbm, inflow_ref),
        (state_hbm, state_ref),
        (thermal_hbm, thermal_ref),
        (measured_hbm, measured_ref),
    )
    copies = [pltpu.make_async_copy(a, b, sems.at[i]) for i, (a, b) in enumerate(pairs)]
    for copy in copies:
        copy.start()
    for copy in copies[:4]:
        copy.wait()
    tile = jnp.concatenate([slot_ref[k : k + 1, :] for k in range(TOUCH)], axis=1)
    row = jnp.concatenate([strip_ref[k : k + 1, :] for k in range(TOUCH)], axis=1)
    sub = iota((TILES, REFS), 0)
    named = (sub == tile).astype(F32)
    before = (sub < iota((REFS, REFS), 1)).astype(F32).astype(BF16)
    rank = jnp.sum(dot(named.astype(BF16), before, 1, 0) * named, axis=0, keepdims=True)
    place = tile * CAP + rank.astype(jnp.int32)
    placing = (iota((SLOTS, REFS), 0) == place).astype(F32).astype(BF16)
    placing_ref[...] = placing
    wanted = (sub == row).astype(F32).astype(BF16)
    asked_ref[...] = dot(placing, wanted, 1, 1).astype(BF16)
    leaving = pltpu.make_async_copy(asked_ref, request_hbm, sems.at[len(pairs)])
    leaving.start()
    category = category_ref[...]
    conduct = jnp.zeros((ROWS, COLS), F32)
    for i in range(classes_ref.shape[0]):
        conduct = jnp.where(category == i, classes_ref[i], conduct)
    conduct_ref[...] = conduct
    copies[4].wait()
    copies[5].wait()
    state_ref[0] = state_ref[0] + inflow_ref[...]
    upper = iota((8, COLS), 0) < 4
    edges = jnp.where(upper[None], state_ref[:, 0:8, :], state_ref[:, ROWS - 8 : ROWS, :])
    ends = jnp.where(upper, conduct[0:8], conduct[ROWS - 8 : ROWS])[None]
    whole = jnp.concatenate([edges, ends, jnp.zeros((1, 8, COLS), F32)], axis=0)
    edge_ref[...] = whole.reshape((L + 2) * 8, COLS).astype(BF16)
    for copy in copies[6:]:
        copy.wait()
    leaving.wait()


def row_halo(a_ref, b_ref, levels=L + 1):
    odd = lax.rem(lax.axis_index("gx"), 2)
    a = a_ref[...].astype(F32).reshape(L + 2, 8, COLS)
    b = b_ref[...].astype(F32).reshape(L + 2, 8, COLS)
    half = lax.div(iota((8, COLS), 0), 4)
    return jnp.where(halo_rows_inside()[None], jnp.where((half == odd)[None], a, b), 0.0)


def halo_rows_inside():
    gx = lax.axis_index("gx")
    sub = iota((8, COLS), 0)
    below = (gx < lax.axis_size("gx") - 1).astype(jnp.int32)
    above = (gx > 0).astype(jnp.int32)
    return jnp.where(sub < 4, below, above) > 0


def held(new, inside):
    return jnp.concatenate([new[:ROWS], jnp.where(inside, new[ROWS:], 0.5)], axis=0)


def rows_change(u, k, cd):
    ud = pltpu.roll(u, WIDE - 1, 0)
    f = (k + cd * ud) * (ud - u)
    return f - pltpu.roll(f, 1, 0)


def lanes_change(u, k, cr, cl):
    ur = pltpu.roll(u, COLS - 1, 1)
    ul = pltpu.roll(u, 1, 1)
    return (k + cr * ur) * (ur - u) - (k + cl * ul) * (u - ul)


def packed(state_ref, conduct_ref, halo, sides):
    ahead = (0, 1, -1, -2)

    def pack(level_of, lane):
        acc = [jnp.zeros(lane.shape, F32) for _ in sides]
        group = lane // 4
        for l in range(L):
            x = pltpu.roll(level_of(l), 4 * l, 1) if l else level_of(l)
            for i, side in enumerate(sides):
                acc[i] = jnp.where(group == (l + ahead[side]) % L, x, acc[i])
        turns = [-4 * ahead[side] % COLS for side in sides]
        return [pltpu.roll(x, t, 1) if t else x for x, t in zip(acc, turns)]

    def spread(x, lane):
        out = []
        for side in sides:
            t = -4 * ahead[side] % COLS
            y = jnp.where(lane < 4, pltpu.roll(x, t, 1) if t else x, 0.0)
            for d in (4, 8, 16, 32, 64):
                y = y + pltpu.roll(y, d, 1)
            out.append(y)
        return out

    lane64, lane8 = iota((ROWS, COLS), 1), iota((8, COLS), 1)
    main, ends = pack(lambda l: state_ref[l], lane64), pack(lambda l: halo[l], lane8)
    cmain, cends = spread(conduct_ref[...], lane64), spread(halo[L], lane8)
    states = [jnp.concatenate([m, e], axis=0) for m, e in zip(main, ends)]
    conds = [jnp.concatenate([m, e], axis=0) for m, e in zip(cmain, cends)]
    return states, conds


def pack_body(state_ref, conduct_ref, a_ref, b_ref, own_ref, cond_ref, pa_ref, pb_ref):
    states, conds = packed(state_ref, conduct_ref, row_halo(a_ref, b_ref), (0, 2))
    for i in range(2):
        own_ref[i] = states[i]
        cond_ref[i] = conds[i]
    odd = lax.rem(lax.axis_index("gy"), 2)
    left = jnp.concatenate([states[0], conds[0]], axis=0)
    right = jnp.concatenate([states[1], conds[1]], axis=0)
    is_odd = (jnp.zeros((2 * WIDE, COLS), jnp.int32) + odd) > 0
    pa_ref[...] = jnp.where(is_odd, left, right).astype(BF16)
    pb_ref[...] = jnp.where(is_odd, right, left).astype(BF16)


def strip_body(
    own_ref, cond_ref, inner_ref, inner_cond_ref, pa_ref, pb_ref, tops_ref, thermal_ref,
    left_ref, right_ref, adjoint_ref, bright_ref, u_ref, v_ref, c_ref, cd_ref, cr_ref, cl_ref, lower_ref, upper_ref,
):
    gy = lax.axis_index("gy")
    odd = lax.rem(gy, 2)
    a = pa_ref[...].astype(F32)
    b = pb_ref[...].astype(F32)
    is_odd = (jnp.zeros((2 * WIDE, COLS), jnp.int32) + odd) > 0
    at = jnp.zeros((2 * WIDE, COLS), jnp.int32) + gy
    from_right = jnp.where(at < lax.axis_size("gy") - 1, jnp.where(is_odd, b, a), 0.0)
    from_left = jnp.where(at > 0, jnp.where(is_odd, a, b), 0.0)
    lane = iota((WIDE, COLS), 1)
    last = lax.rem(lane, 4) == 3
    first = lax.rem(lane, 4) == 0
    lowest = lane >= COLS - 4
    highest = lane < 4
    inside = halo_rows_inside()
    in_left = (jnp.zeros((WIDE, COLS), jnp.int32) + gy) > 0
    in_right = (jnp.zeros((WIDE, COLS), jnp.int32) + gy) < lax.axis_size("gy") - 1
    sources = (
        (from_left[:WIDE], from_left[WIDE:]),
        (own_ref[0], cond_ref[0]),
        (inner_ref[0], inner_cond_ref[0]),
        (inner_ref[1], inner_cond_ref[1]),
        (own_ref[1], cond_ref[1]),
        (from_right[:WIDE], from_right[WIDE:]),
    )
    for i, (s, c) in enumerate(sources):
        u_ref[i] = s + 0.5
        c_ref[i] = 0.5 * c

    def turn(ref):
        for i in range(6):
            lower_ref[i] = pltpu.roll(ref[i], COLS - 4, 1)
            upper_ref[i] = pltpu.roll(ref[i], 4, 1)

    def next_of(ref, i):
        x = jnp.where(first, upper_ref[i + 1], ref[i]) if i % 3 < 2 else ref[i]
        return pltpu.roll(x, COLS - 1, 1)

    def prior_of(ref, i):
        x = jnp.where(last, lower_ref[i - 1], ref[i]) if i % 3 else ref[i]
        return pltpu.roll(x, 1, 1)

    turn(c_ref)
    for i in range(6):
        cd_ref[i] = pltpu.roll(c_ref[i], WIDE - 1, 0)
        cr_ref[i] = next_of(c_ref, i)
        cl_ref[i] = prior_of(c_ref, i)

    for step in range(STEPS):
        now, then = (u_ref, v_ref) if step % 2 == 0 else (v_ref, u_ref)
        turn(now)
        for i in range(6) if step < STEPS - 1 else (1, 4):
            u, c = now[i], c_ref[i]
            k = c * u
            ur, ul = next_of(now, i), prior_of(now, i)
            uz, ua = lower_ref[i], upper_ref[i]
            change = rows_change(u, k, cd_ref[i])
            change = change + ((k + cr_ref[i] * ur) * (ur - u) - (k + cl_ref[i] * ul) * (u - ul))
            down = (k + c * uz) * ((u - uz) + 0.3)
            fall = (c * ua + k) * ((ua - u) + 0.3)
            change = change + (jnp.where(highest, 0.0, fall) - jnp.where(lowest, 0.0, down))
            new = held(u + change, inside)
            if i == 0:
                new = jnp.where(in_left, new, 0.5)
            if i == 5:
                new = jnp.where(in_right, new, 0.5)
            then[i] = new
    left = u_ref[1][:ROWS] - 0.5
    right = u_ref[4][:ROWS] - 0.5
    left_ref[...] = left
    right_ref[...] = right
    lane = iota((ROWS, COLS), 1)

    def joined(l):
        lhs = pltpu.roll(left, COLS - 4 * l, 1) if l else left
        rhs = pltpu.roll(right, COLS - 4 - 4 * l, 1)
        return jnp.where(lane < 4, lhs, jnp.where(lane >= COLS - 4, rhs, tops_ref[l]))

    mix = 0.6 * joined(0) + 0.4 * joined(1)
    thermal = thermal_ref[...]
    bright = (thermal * (1.0 - 0.4 * mix * mix)).astype(BF16)
    adjoint_ref[...] = thermal * (-0.8 * mix)
    bright_ref[...] = jnp.concatenate([bright, jnp.zeros((COLS - ROWS, COLS), BF16)], axis=0)


def serve_body(picker_ref, bright_ref, served_ref):
    served_ref[...] = dot(picker_ref[...], bright_ref[...], 1, 0).astype(BF16)


def wide_conduct(conduct_ref, halo):
    return 0.5 * jnp.concatenate([conduct_ref[...], halo[L]], axis=0)


NEAR = 12


def evolve(state_ref, conduct_ref, a_ref, b_ref, u_ref, c_ref, low, high, finish):
    halo = row_halo(a_ref, b_ref)
    c = wide_conduct(conduct_ref, halo)
    c_ref[0] = c
    c_ref[1] = pltpu.roll(c, WIDE - 1, 0)
    c_ref[2] = pltpu.roll(c, COLS - 1, 1)
    c_ref[3] = pltpu.roll(c, 1, 1)
    inside = halo_rows_inside()
    start, stop = max(0, low - STEPS), min(L, high + STEPS)
    for l in range(start, stop):
        u_ref[l - start] = jnp.concatenate([state_ref[l], halo[l]], axis=0) + 0.5
    for step in range(STEPS):
        top = max(0, low - (STEPS - 1 - step))
        end = min(L, high + (STEPS - 1 - step))
        above = None
        if top > 0:
            u, uz = u_ref[top - 1 - start], u_ref[top - start]
            above = c_ref[0] * (u + uz) * ((u - uz) + 0.3)
        u = u_ref[top - start]
        k = c_ref[0] * u
        for l in range(top, end):
            change = rows_change(u, k, c_ref[1]) + lanes_change(u, k, c_ref[2], c_ref[3])
            if above is not None:
                change = change + above
            if l < L - 1:
                uz = u_ref[l + 1 - start]
                kz = c_ref[0] * uz
                above = (k + kz) * ((u - uz) + 0.3)
                change = change - above
            new = u + change
            if step < STEPS - 1:
                u_ref[l - start] = held(new, inside)
            else:
                finish(l, new[:ROWS] - 0.5)
            u, k = uz, kz


def turned(ref):
    parts = [
        jnp.transpose(ref[i : i + COLS, :].astype(F32)).astype(BF16) for i in range(0, SLOTS, COLS)
    ]
    return jnp.concatenate(parts, axis=1)


def tops_body(
    state_ref, conduct_ref, a_ref, b_ref, tops_ref, inner_ref, inner_cond_ref, u_ref, c_ref
):
    states, conds = packed(state_ref, conduct_ref, row_halo(a_ref, b_ref), (1, 3))
    for i in range(2):
        inner_ref[i] = states[i]
        inner_cond_ref[i] = conds[i]

    def finish(l, new):
        tops_ref[l] = new

    evolve(state_ref, conduct_ref, a_ref, b_ref, u_ref, c_ref, 0, 2, finish)


HALF = L // 2
PIECE = 4


def half_body(low, state_ref, conduct_ref, a_ref, b_ref, left_ref, right_ref, out_hbm, u_ref, c_ref, own_ref, sems):
    lane = iota((ROWS, COLS), 1)
    copies = []

    def finish(l, new):
        lhs = pltpu.roll(left_ref[...], (COLS - 4 * l) % COLS, 1) if l else left_ref[...]
        turn = (COLS - 4 - 4 * l) % COLS
        rhs = pltpu.roll(right_ref[...], turn, 1) if turn else right_ref[...]
        own_ref[l - low] = jnp.where(lane < 4, lhs, jnp.where(lane >= COLS - 4, rhs, new))
        if (l + 1) % PIECE == 0:
            at = l + 1 - PIECE
            copy = pltpu.make_async_copy(
                own_ref.at[pl.ds(at - low, PIECE)], out_hbm.at[pl.ds(at, PIECE)], sems.at[len(copies)]
            )
            copy.start()
            copies.append(copy)

    evolve(state_ref, conduct_ref, a_ref, b_ref, u_ref, c_ref, low, low + HALF, finish)
    for copy in copies:
        copy.wait()


def upper_body(
    state_ref, conduct_ref, a_ref, b_ref, left_ref, right_ref, picker_ref, weights_hbm,
    out_hbm, weights_ref, across_ref, *scratch,
):
    copy = pltpu.make_async_copy(weights_hbm.at[pl.ds(0, NEAR)], weights_ref, scratch[-1])
    copy.start()
    across_ref[...] = turned(picker_ref)
    half_body(0, state_ref, conduct_ref, a_ref, b_ref, left_ref, right_ref, out_hbm, *scratch[:-1])
    copy.wait()


def lower_body(
    state_hbm, conduct_ref, a_ref, b_ref, left_ref, right_ref, begun_hbm, out_hbm, *scratch
):
    state_ref, sem = scratch[-2:]
    span = pl.ds(HALF - STEPS, L - HALF + STEPS)
    copy = pltpu.make_async_copy(state_hbm.at[span], state_ref.at[span], sem)
    copy.start()
    copy.wait()
    half_body(HALF, state_ref, conduct_ref, a_ref, b_ref, left_ref, right_ref, out_hbm, *scratch[:-2])


PART = 4
CHUNKS = (8, 12)


def foot_body(
    returned_ref, placing_ref, seen_ref, near_ref, weights_hbm,
    bright_ref, outgoing_ref, cells_ref, contrib_ref, weights_ref, sems,
):
    copies = {}
    at = NEAR
    for i, count in enumerate(CHUNKS):
        span = pl.ds(at, count)
        copies[at] = pltpu.make_async_copy(weights_hbm.at[span], weights_ref.at[span], sems.at[i])
        copies[at].start()
        at += count
    placing = placing_ref[...]
    cells_ref[...] = dot(placing, returned_ref[...], 0, 0)
    lane = iota((FOOT, COLS), 1)

    def weights(b, k):
        return near_ref[b, k] if b < NEAR else weights_ref[b, k]

    def adjoint(start, misfit):
        for i in range(PART):
            for k in range(TOUCH):
                at = k * OWN + start + i
                contrib_ref[at : at + 1, :] = dot(misfit[i : i + 1], weights(start + i, k), 1, 0)

    misfit = None
    for start in range(0, OWN, PART):
        if start in copies:
            copies[start].wait()
        sums = jnp.zeros((FOOT, COLS), F32)
        for i in range(PART):
            total = None
            for k in range(TOUCH):
                at = k * OWN + start + i
                term = weights(start + i, k).astype(F32) * cells_ref[at : at + 1, :]
                total = term if total is None else total + term
            sums = jnp.where(lane == i, jnp.sum(total, axis=1, keepdims=True), sums)
        if start:
            adjoint(start - PART, misfit)
        evolved = jnp.transpose(sums)[:PART]
        bright_ref[start : start + PART, :] = evolved
        misfit = (evolved - seen_ref[start : start + PART, :]).astype(BF16)
    adjoint(OWN - PART, misfit)
    outgoing_ref[...] = dot(placing, contrib_ref[...].astype(BF16), 1, 0).astype(BF16)


def gradient_body(grads_ref, across_ref, adjoint_ref, out_ref):
    summed = dot(across_ref[0:ROWS, :], grads_ref[...], 1, 0)
    common = summed * adjoint_ref[...]
    out_ref[0] = 0.6 * common
    out_ref[1] = 0.4 * common


def swapped(x, axis):
    n, m = lax.axis_size(axis), lax.axis_size("gy" if axis == "gx" else "gx")

    def place(along, across):
        return along * m + across if axis == "gx" else across * n + along

    one = [(i, i ^ 1) for i in range(n)]
    two = []
    for j in range(m):
        two += [(place(i, j), place(i, j ^ 1)) for i in (0, n - 1)]
        for i in range(1, n - 1, 2):
            two += [(place(i, j), place(i + 1, j)), (place(i + 1, j), place(i, j))]
    return lax.ppermute(x[0], axis, one), lax.ppermute(x[1], ("gx", "gy"), two)


def exchange(x):
    return lax.all_to_all(
        x.reshape(TILES, CAP, COLS), ("gx", "gy"), split_axis=0, concat_axis=0, tiled=True
    ).reshape(SLOTS, COLS)


def on_device(state, inflow, classes, category, thermal, weights, slots, strips, measured):
    def sds(*shape, dtype=F32):
        return jax.ShapeDtypeStruct(shape, dtype)

    held_state, conduct, edge, warm, seen, placing, request = call(
        prep_body,
        (
            sds(L, ROWS, COLS), sds(ROWS, COLS), sds((L + 2) * 8, COLS, dtype=BF16), sds(ROWS, COLS),
            sds(OWN, FOOT), sds(SLOTS, REFS, dtype=BF16), sds(SLOTS, COLS, dtype=BF16),
        ),
        [HBM] * 8,
        "prep",
        [
            pltpu.VMEM((ROWS, COLS), F32),
            pltpu.VMEM((ROWS, COLS), jnp.int32),
            pltpu.SMEM(classes.shape, F32),
            pltpu.VMEM((TOUCH, OWN), jnp.int32),
            pltpu.VMEM((TOUCH, OWN), jnp.int32),
            pltpu.VMEM((SLOTS, COLS), BF16),
            pltpu.SemaphoreType.DMA((9,)),
        ],
        out_specs=(VMEM,) * 6 + (HBM,),
        flops=20_000_000, moved=2_000_000,
    )(*(far(x) for x in (classes, inflow, category, state, thermal, slots.T, strips.T, measured)))
    xa, xb = swapped((edge, edge), "gx")
    picker = exchange(request)
    own, cond, pa, pb = call(
        pack_body,
        (sds(2, WIDE, COLS), sds(2, WIDE, COLS), sds(2 * WIDE, COLS, dtype=BF16), sds(2 * WIDE, COLS, dtype=BF16)),
        [VMEM] * 4,
        "pack",
        flops=20_000_000_000, moved=1_500_000,
    )(held_state, conduct, xa, xb)
    ya, yb = swapped((pa, pb), "gy")
    tops, inner, inner_cond = call(
        tops_body,
        (sds(2, ROWS, COLS), sds(2, WIDE, COLS), sds(2, WIDE, COLS)),
        [VMEM] * 4,
        "tops",
        [pltpu.VMEM((STEPS + 2, WIDE, COLS), F32), pltpu.VMEM((4, WIDE, COLS), F32)],
        flops=20_000_000_000, moved=1_000_000,
    )(held_state, conduct, xa, xb)
    left, right, adjoint, bright = call(
        strip_body,
        (sds(ROWS, COLS), sds(ROWS, COLS), sds(ROWS, COLS), sds(COLS, COLS, dtype=BF16)),
        [VMEM] * 8,
        "strips",
        [pltpu.VMEM((6, WIDE, COLS), F32)] * 8,
        flops=10_000_000_000, moved=1_000_000,
    )(own, cond, inner, inner_cond, ya, yb, tops, warm)
    served = call(
        serve_body,
        sds(SLOTS, COLS, dtype=BF16),
        [VMEM] * 2,
        "serve",
        flops=20_000_000, moved=300_000,
    )(picker, bright)
    returned = exchange(served)
    scratch = [
        pltpu.VMEM((HALF + STEPS, WIDE, COLS), F32),
        pltpu.VMEM((4, WIDE, COLS), F32),
        pltpu.VMEM((HALF, ROWS, COLS), F32),
        pltpu.SemaphoreType.DMA((HALF // PIECE,)),
    ]
    begun, near, picker_across = call(
        upper_body,
        (
            sds(L, ROWS, COLS), sds(NEAR, TOUCH, FOOT, COLS, dtype=BF16), sds(COLS, SLOTS, dtype=BF16)
        ),
        [VMEM] * 7 + [HBM],
        "upper",
        scratch + [pltpu.SemaphoreType.DMA],
        out_specs=(HBM, VMEM, VMEM),
        flops=500_000_000, moved=3_000_000,
    )(held_state, conduct, xa, xb, left, right, picker, far(weights))
    brightness, outgoing = call(
        foot_body,
        (sds(OWN, FOOT), sds(SLOTS, COLS, dtype=BF16)),
        [VMEM] * 4 + [HBM],
        "footprints",
        [
            pltpu.VMEM((REFS, COLS), F32),
            pltpu.VMEM((REFS, COLS), F32),
            pltpu.VMEM(weights.shape, BF16),
            pltpu.SemaphoreType.DMA((len(CHUNKS),)),
        ],
        flops=20_000_000, moved=5_000_000,
    )(returned, placing, seen, near, far(weights))
    moisture = call(
        lower_body,
        sds(L, ROWS, COLS),
        [HBM] + [VMEM] * 5 + [HBM],
        "lower",
        scratch + [pltpu.VMEM((L, ROWS, COLS), F32), pltpu.SemaphoreType.DMA],
        out_specs=HBM,
        aliases={6: 0},
        flops=500_000_000, moved=3_000_000,
    )(far(state), conduct, xa, xb, left, right, begun)
    grads = exchange(outgoing)
    grad_top = call(
        gradient_body, sds(2, ROWS, COLS), [VMEM] * 3, "gradient", flops=20_000_000, moved=400_000
    )(grads, picker_across, adjoint)
    return moisture, brightness, grad_top


def solution(mesh):
    placed = (
        P(None, "gx", "gy"),
        P("gx", "gy"),
        P(),
        P("gx", "gy"),
        P("gx", "gy"),
        P(("gx", "gy"), None, None, None),
        P(("gx", "gy"), None),
        P(("gx", "gy"), None),
        P(("gx", "gy"), None),
    )
    return jax.shard_map(
        on_device,
        mesh=mesh,
        in_specs=placed,
        out_specs=(P(None, "gx", "gy"), P(("gx", "gy"), None), P(None, "gx", "gy")),
        check_vma=False,
    )
```

```python
import jax
import jax.numpy as jnp
from jax import lax
from jax.experimental import pallas as pl
from jax.experimental.pallas import tpu as pltpu
from jax.sharding import PartitionSpec as P

CAP = 4
STEPS = 4
L = 32
ROWS = 64
COLS = 128
WIDE = ROWS + 8
TILES = 128
SLOTS = TILES * CAP
OWN = 32
TOUCH = 4
REFS = OWN * TOUCH
FOOT = 128
F32 = jnp.float32
BF16 = jnp.bfloat16
VMEM = pl.BlockSpec(memory_space=pltpu.VMEM)
SMEM = pl.BlockSpec(memory_space=pltpu.SMEM)
ANY = pl.BlockSpec(memory_space=pl.ANY)
HBM = pl.BlockSpec(memory_space=pltpu.HBM)
LIMIT = 32 * 1024 * 1024


def call(body, outs, in_specs, name, scratch=(), out_specs=None, aliases=None, flops=0, moved=0):
    return pl.pallas_call(
        body,
        out_shape=outs,
        in_specs=in_specs,
        out_specs=out_specs or jax.tree.map(lambda _: VMEM, outs),
        input_output_aliases=aliases or {},
        scratch_shapes=list(scratch),
        name=name,
        compiler_params=pltpu.CompilerParams(vmem_limit_bytes=LIMIT),
        cost_estimate=pl.CostEstimate(flops=flops, bytes_accessed=moved, transcendentals=0),
    )


def iota(shape, dim):
    return lax.broadcasted_iota(jnp.int32, shape, dim)


def far(x):
    return pltpu.with_memory_space_constraint(x, pltpu.HBM)


def dot(a, b, ca, cb):
    return lax.dot_general(a, b, (((ca,), (cb,)), ((), ())), preferred_element_type=F32)


def prep_body(
    classes_hbm, inflow_hbm, category_hbm, state_hbm, thermal_hbm, slot_hbm, strip_hbm, measured_hbm,
    state_ref, conduct_ref, edge_ref, thermal_ref, measured_ref, placing_ref, request_hbm,
    inflow_ref, category_ref, classes_ref, slot_ref, strip_ref, asked_ref, sems,
):
    pairs = (
        (slot_hbm, slot_ref),
        (strip_hbm, strip_ref),
        (classes_hbm, classes_ref),
        (category_hbm, category_ref),
        (inflow_hbm, inflow_ref),
        (state_hbm, state_ref),
        (thermal_hbm, thermal_ref),
        (measured_hbm, measured_ref),
    )
    copies = [pltpu.make_async_copy(a, b, sems.at[i]) for i, (a, b) in enumerate(pairs)]
    for copy in copies:
        copy.start()
    for copy in copies[:4]:
        copy.wait()
    tile = jnp.concatenate([slot_ref[k : k + 1, :] for k in range(TOUCH)], axis=1)
    row = jnp.concatenate([strip_ref[k : k + 1, :] for k in range(TOUCH)], axis=1)
    sub = iota((TILES, REFS), 0)
    named = (sub == tile).astype(F32)
    before = (sub < iota((REFS, REFS), 1)).astype(F32).astype(BF16)
    rank = jnp.sum(dot(named.astype(BF16), before, 1, 0) * named, axis=0, keepdims=True)
    place = tile * CAP + rank.astype(jnp.int32)
    placing = (iota((SLOTS, REFS), 0) == place).astype(F32).astype(BF16)
    placing_ref[...] = placing
    wanted = (sub == row).astype(F32).astype(BF16)
    asked_ref[...] = dot(placing, wanted, 1, 1).astype(BF16)
    leaving = pltpu.make_async_copy(asked_ref, request_hbm, sems.at[len(pairs)])
    leaving.start()
    category = category_ref[...]
    conduct = jnp.zeros((ROWS, COLS), F32)
    for i in range(classes_ref.shape[0]):
        conduct = jnp.where(category == i, classes_ref[i], conduct)
    conduct_ref[...] = conduct
    copies[4].wait()
    copies[5].wait()
    state_ref[0] = state_ref[0] + inflow_ref[...]
    upper = iota((8, COLS), 0) < 4
    edges = jnp.where(upper[None], state_ref[:, 0:8, :], state_ref[:, ROWS - 8 : ROWS, :])
    ends = jnp.where(upper, conduct[0:8], conduct[ROWS - 8 : ROWS])[None]
    whole = jnp.concatenate([edges, ends, jnp.zeros((1, 8, COLS), F32)], axis=0)
    edge_ref[...] = whole.reshape((L + 2) * 8, COLS).astype(BF16)
    for copy in copies[6:]:
        copy.wait()
    leaving.wait()


def row_halo(a_ref, b_ref, levels=L + 1):
    odd = lax.rem(lax.axis_index("gx"), 2)
    a = a_ref[...].astype(F32).reshape(L + 2, 8, COLS)
    b = b_ref[...].astype(F32).reshape(L + 2, 8, COLS)
    half = lax.div(iota((8, COLS), 0), 4)
    return jnp.where(halo_rows_inside()[None], jnp.where((half == odd)[None], a, b), 0.0)


def halo_rows_inside():
    gx = lax.axis_index("gx")
    sub = iota((8, COLS), 0)
    below = (gx < lax.axis_size("gx") - 1).astype(jnp.int32)
    above = (gx > 0).astype(jnp.int32)
    return jnp.where(sub < 4, below, above) > 0


def held(new, inside):
    return jnp.concatenate([new[:ROWS], jnp.where(inside, new[ROWS:], 0.5)], axis=0)


def rows_change(u, k, cd):
    ud = pltpu.roll(u, WIDE - 1, 0)
    f = (k + cd * ud) * (ud - u)
    return f - pltpu.roll(f, 1, 0)


def lanes_change(u, k, cr, cl):
    ur = pltpu.roll(u, COLS - 1, 1)
    ul = pltpu.roll(u, 1, 1)
    return (k + cr * ur) * (ur - u) - (k + cl * ul) * (u - ul)


def packed(state_ref, conduct_ref, halo, sides):
    ahead = (0, 1, -1, -2)

    def pack(level_of, lane):
        acc = [jnp.zeros(lane.shape, F32) for _ in sides]
        group = lane // 4
        for l in range(L):
            x = pltpu.roll(level_of(l), 4 * l, 1) if l else level_of(l)
            for i, side in enumerate(sides):
                acc[i] = jnp.where(group == (l + ahead[side]) % L, x, acc[i])
        turns = [-4 * ahead[side] % COLS for side in sides]
        return [pltpu.roll(x, t, 1) if t else x for x, t in zip(acc, turns)]

    def spread(x, lane):
        out = []
        for side in sides:
            t = -4 * ahead[side] % COLS
            y = jnp.where(lane < 4, pltpu.roll(x, t, 1) if t else x, 0.0)
            for d in (4, 8, 16, 32, 64):
                y = y + pltpu.roll(y, d, 1)
            out.append(y)
        return out

    lane64, lane8 = iota((ROWS, COLS), 1), iota((8, COLS), 1)
    main, ends = pack(lambda l: state_ref[l], lane64), pack(lambda l: halo[l], lane8)
    cmain, cends = spread(conduct_ref[...], lane64), spread(halo[L], lane8)
    states = [jnp.concatenate([m, e], axis=0) for m, e in zip(main, ends)]
    conds = [jnp.concatenate([m, e], axis=0) for m, e in zip(cmain, cends)]
    return states, conds


def pack_body(state_ref, conduct_ref, a_ref, b_ref, own_ref, cond_ref, pa_ref, pb_ref):
    states, conds = packed(state_ref, conduct_ref, row_halo(a_ref, b_ref), (0, 2))
    for i in range(2):
        own_ref[i] = states[i]
        cond_ref[i] = conds[i]
    odd = lax.rem(lax.axis_index("gy"), 2)
    left = jnp.concatenate([states[0], conds[0]], axis=0)
    right = jnp.concatenate([states[1], conds[1]], axis=0)
    is_odd = (jnp.zeros((2 * WIDE, COLS), jnp.int32) + odd) > 0
    pa_ref[...] = jnp.where(is_odd, left, right).astype(BF16)
    pb_ref[...] = jnp.where(is_odd, right, left).astype(BF16)


def strip_body(
    own_ref, cond_ref, inner_ref, inner_cond_ref, pa_ref, pb_ref, tops_ref, thermal_ref,
    left_ref, right_ref, adjoint_ref, bright_ref, u_ref, v_ref, c_ref, cd_ref, cr_ref, cl_ref, lower_ref, upper_ref,
):
    gy = lax.axis_index("gy")
    odd = lax.rem(gy, 2)
    a = pa_ref[...].astype(F32)
    b = pb_ref[...].astype(F32)
    is_odd = (jnp.zeros((2 * WIDE, COLS), jnp.int32) + odd) > 0
    at = jnp.zeros((2 * WIDE, COLS), jnp.int32) + gy
    from_right = jnp.where(at < lax.axis_size("gy") - 1, jnp.where(is_odd, b, a), 0.0)
    from_left = jnp.where(at > 0, jnp.where(is_odd, a, b), 0.0)
    lane = iota((WIDE, COLS), 1)
    last = lax.rem(lane, 4) == 3
    first = lax.rem(lane, 4) == 0
    lowest = lane >= COLS - 4
    highest = lane < 4
    inside = halo_rows_inside()
    in_left = (jnp.zeros((WIDE, COLS), jnp.int32) + gy) > 0
    in_right = (jnp.zeros((WIDE, COLS), jnp.int32) + gy) < lax.axis_size("gy") - 1
    sources = (
        (from_left[:WIDE], from_left[WIDE:]),
        (own_ref[0], cond_ref[0]),
        (inner_ref[0], inner_cond_ref[0]),
        (inner_ref[1], inner_cond_ref[1]),
        (own_ref[1], cond_ref[1]),
        (from_right[:WIDE], from_right[WIDE:]),
    )
    for i, (s, c) in enumerate(sources):
        u_ref[i] = s + 0.5
        c_ref[i] = 0.5 * c

    def turn(ref):
        for i in range(6):
            lower_ref[i] = pltpu.roll(ref[i], COLS - 4, 1)
            upper_ref[i] = pltpu.roll(ref[i], 4, 1)

    def next_of(ref, i):
        x = jnp.where(first, upper_ref[i + 1], ref[i]) if i % 3 < 2 else ref[i]
        return pltpu.roll(x, COLS - 1, 1)

    def prior_of(ref, i):
        x = jnp.where(last, lower_ref[i - 1], ref[i]) if i % 3 else ref[i]
        return pltpu.roll(x, 1, 1)

    turn(c_ref)
    for i in range(6):
        cd_ref[i] = pltpu.roll(c_ref[i], WIDE - 1, 0)
        cr_ref[i] = next_of(c_ref, i)
        cl_ref[i] = prior_of(c_ref, i)

    for step in range(STEPS):
        now, then = (u_ref, v_ref) if step % 2 == 0 else (v_ref, u_ref)
        turn(now)
        for i in range(6) if step < STEPS - 1 else (1, 4):
            u, c = now[i], c_ref[i]
            k = c * u
            ur, ul = next_of(now, i), prior_of(now, i)
            uz, ua = lower_ref[i], upper_ref[i]
            change = rows_change(u, k, cd_ref[i])
            change = change + ((k + cr_ref[i] * ur) * (ur - u) - (k + cl_ref[i] * ul) * (u - ul))
            down = (k + c * uz) * ((u - uz) + 0.3)
            fall = (c * ua + k) * ((ua - u) + 0.3)
            change = change + (jnp.where(highest, 0.0, fall) - jnp.where(lowest, 0.0, down))
            new = held(u + change, inside)
            if i == 0:
                new = jnp.where(in_left, new, 0.5)
            if i == 5:
                new = jnp.where(in_right, new, 0.5)
            then[i] = new
    left = u_ref[1][:ROWS] - 0.5
    right = u_ref[4][:ROWS] - 0.5
    left_ref[...] = left
    right_ref[...] = right
    lane = iota((ROWS, COLS), 1)

    def joined(l):
        lhs = pltpu.roll(left, COLS - 4 * l, 1) if l else left
        rhs = pltpu.roll(right, COLS - 4 - 4 * l, 1)
        return jnp.where(lane < 4, lhs, jnp.where(lane >= COLS - 4, rhs, tops_ref[l]))

    mix = 0.6 * joined(0) + 0.4 * joined(1)
    thermal = thermal_ref[...]
    bright = (thermal * (1.0 - 0.4 * mix * mix)).astype(BF16)
    adjoint_ref[...] = thermal * (-0.8 * mix)
    bright_ref[...] = jnp.concatenate([bright, jnp.zeros((COLS - ROWS, COLS), BF16)], axis=0)


def sent(left_ref, right, out_hbm, held_ref, sems):
    half = SLOTS // 2
    copies = []
    for i in range(2):
        span = pl.ds(i * half, half)
        held_ref[span, :] = dot(left_ref[span, :], right, 1, 0).astype(BF16)
        copies.append(pltpu.make_async_copy(held_ref.at[span], out_hbm.at[span], sems.at[i]))
        copies[i].start()
    for copy in copies:
        copy.wait()


def serve_body(picker_ref, bright_ref, served_hbm, held_ref, sems):
    sent(picker_ref, bright_ref[...], served_hbm, held_ref, sems)


def wide_conduct(conduct_ref, halo):
    return 0.5 * jnp.concatenate([conduct_ref[...], halo[L]], axis=0)


NEAR = 12


def evolve(state_ref, conduct_ref, a_ref, b_ref, u_ref, c_ref, low, high, finish):
    halo = row_halo(a_ref, b_ref)
    c = wide_conduct(conduct_ref, halo)
    c_ref[0] = c
    c_ref[1] = pltpu.roll(c, WIDE - 1, 0)
    c_ref[2] = pltpu.roll(c, COLS - 1, 1)
    c_ref[3] = pltpu.roll(c, 1, 1)
    inside = halo_rows_inside()
    start, stop = max(0, low - STEPS), min(L, high + STEPS)
    for l in range(start, stop):
        u_ref[l - start] = jnp.concatenate([state_ref[l], halo[l]], axis=0) + 0.5
    for step in range(STEPS):
        top = max(0, low - (STEPS - 1 - step))
        end = min(L, high + (STEPS - 1 - step))
        above = None
        if top > 0:
            u, uz = u_ref[top - 1 - start], u_ref[top - start]
            above = c_ref[0] * (u + uz) * ((u - uz) + 0.3)
        u = u_ref[top - start]
        k = c_ref[0] * u
        for l in range(top, end):
            change = rows_change(u, k, c_ref[1]) + lanes_change(u, k, c_ref[2], c_ref[3])
            if above is not None:
                change = change + above
            if l < L - 1:
                uz = u_ref[l + 1 - start]
                kz = c_ref[0] * uz
                above = (k + kz) * ((u - uz) + 0.3)
                change = change - above
            new = u + change
            if step < STEPS - 1:
                u_ref[l - start] = held(new, inside)
            else:
                finish(l, new[:ROWS] - 0.5)
            u, k = uz, kz


def turned(ref):
    parts = [
        jnp.transpose(ref[i : i + COLS, :].astype(F32)).astype(BF16) for i in range(0, SLOTS, COLS)
    ]
    return jnp.concatenate(parts, axis=1)


def tops_body(
    state_ref, conduct_ref, a_ref, b_ref, tops_ref, inner_ref, inner_cond_ref, u_ref, c_ref
):
    states, conds = packed(state_ref, conduct_ref, row_halo(a_ref, b_ref), (1, 3))
    for i in range(2):
        inner_ref[i] = states[i]
        inner_cond_ref[i] = conds[i]

    def finish(l, new):
        tops_ref[l] = new

    evolve(state_ref, conduct_ref, a_ref, b_ref, u_ref, c_ref, 0, 2, finish)


HALF = L // 2
PIECE = 4


def half_body(low, state_ref, conduct_ref, a_ref, b_ref, left_ref, right_ref, out_hbm, u_ref, c_ref, own_ref, sems):
    lane = iota((ROWS, COLS), 1)
    copies = []

    def finish(l, new):
        lhs = pltpu.roll(left_ref[...], (COLS - 4 * l) % COLS, 1) if l else left_ref[...]
        turn = (COLS - 4 - 4 * l) % COLS
        rhs = pltpu.roll(right_ref[...], turn, 1) if turn else right_ref[...]
        own_ref[l - low] = jnp.where(lane < 4, lhs, jnp.where(lane >= COLS - 4, rhs, new))
        if (l + 1) % PIECE == 0:
            at = l + 1 - PIECE
            copy = pltpu.make_async_copy(
                own_ref.at[pl.ds(at - low, PIECE)], out_hbm.at[pl.ds(at, PIECE)], sems.at[len(copies)]
            )
            copy.start()
            copies.append(copy)

    evolve(state_ref, conduct_ref, a_ref, b_ref, u_ref, c_ref, low, low + HALF, finish)
    for copy in copies:
        copy.wait()


def upper_body(
    state_ref, conduct_ref, a_ref, b_ref, left_ref, right_ref, picker_ref, weights_hbm,
    out_hbm, weights_ref, across_ref, *scratch,
):
    copy = pltpu.make_async_copy(weights_hbm.at[pl.ds(0, NEAR)], weights_ref, scratch[-1])
    copy.start()
    across_ref[...] = turned(picker_ref)
    half_body(0, state_ref, conduct_ref, a_ref, b_ref, left_ref, right_ref, out_hbm, *scratch[:-1])
    copy.wait()


def lower_body(
    state_hbm, conduct_ref, a_ref, b_ref, left_ref, right_ref, begun_hbm, out_hbm, *scratch
):
    state_ref, sem = scratch[-2:]
    span = pl.ds(HALF - STEPS, L - HALF + STEPS)
    copy = pltpu.make_async_copy(state_hbm.at[span], state_ref.at[span], sem)
    copy.start()
    copy.wait()
    half_body(HALF, state_ref, conduct_ref, a_ref, b_ref, left_ref, right_ref, out_hbm, *scratch[:-2])


PART = 4
CHUNKS = (8, 12)


def foot_body(
    returned_ref, placing_ref, seen_ref, near_ref, weights_hbm,
    bright_ref, outgoing_hbm, cells_ref, contrib_ref, weights_ref, sems, leaving_ref, leaving_sems,
):
    copies = {}
    at = NEAR
    for i, count in enumerate(CHUNKS):
        span = pl.ds(at, count)
        copies[at] = pltpu.make_async_copy(weights_hbm.at[span], weights_ref.at[span], sems.at[i])
        copies[at].start()
        at += count
    placing = placing_ref[...]
    cells_ref[...] = dot(placing, returned_ref[...], 0, 0)
    lane = iota((FOOT, COLS), 1)

    def weights(b, k):
        return near_ref[b, k] if b < NEAR else weights_ref[b, k]

    def adjoint(start, misfit):
        for i in range(PART):
            for k in range(TOUCH):
                at = k * OWN + start + i
                contrib_ref[at : at + 1, :] = dot(misfit[i : i + 1], weights(start + i, k), 1, 0)

    misfit = None
    for start in range(0, OWN, PART):
        if start in copies:
            copies[start].wait()
        sums = jnp.zeros((FOOT, COLS), F32)
        for i in range(PART):
            total = None
            for k in range(TOUCH):
                at = k * OWN + start + i
                term = weights(start + i, k).astype(F32) * cells_ref[at : at + 1, :]
                total = term if total is None else total + term
            sums = jnp.where(lane == i, jnp.sum(total, axis=1, keepdims=True), sums)
        if start:
            adjoint(start - PART, misfit)
        evolved = jnp.transpose(sums)[:PART]
        bright_ref[start : start + PART, :] = evolved
        misfit = (evolved - seen_ref[start : start + PART, :]).astype(BF16)
    adjoint(OWN - PART, misfit)
    sent(placing_ref, contrib_ref[...].astype(BF16), outgoing_hbm, leaving_ref, leaving_sems)


def gradient_body(grads_ref, across_ref, adjoint_ref, out_ref):
    summed = dot(across_ref[0:ROWS, :], grads_ref[...], 1, 0)
    common = summed * adjoint_ref[...]
    out_ref[0] = 0.6 * common
    out_ref[1] = 0.4 * common


def swapped(x, axis):
    n, m = lax.axis_size(axis), lax.axis_size("gy" if axis == "gx" else "gx")

    def place(along, across):
        return along * m + across if axis == "gx" else across * n + along

    one = [(i, i ^ 1) for i in range(n)]
    two = []
    for j in range(m):
        two += [(place(i, j), place(i, j ^ 1)) for i in (0, n - 1)]
        for i in range(1, n - 1, 2):
            two += [(place(i, j), place(i + 1, j)), (place(i + 1, j), place(i, j))]
    return lax.ppermute(x[0], axis, one), lax.ppermute(x[1], ("gx", "gy"), two)


def exchange(x):
    return lax.all_to_all(
        x.reshape(TILES, CAP, COLS), ("gx", "gy"), split_axis=0, concat_axis=0, tiled=True
    ).reshape(SLOTS, COLS)


def on_device(state, inflow, classes, category, thermal, weights, slots, strips, measured):
    def sds(*shape, dtype=F32):
        return jax.ShapeDtypeStruct(shape, dtype)

    held_state, conduct, edge, warm, seen, placing, request = call(
        prep_body,
        (
            sds(L, ROWS, COLS), sds(ROWS, COLS), sds((L + 2) * 8, COLS, dtype=BF16), sds(ROWS, COLS),
            sds(OWN, FOOT), sds(SLOTS, REFS, dtype=BF16), sds(SLOTS, COLS, dtype=BF16),
        ),
        [HBM] * 8,
        "prep",
        [
            pltpu.VMEM((ROWS, COLS), F32),
            pltpu.VMEM((ROWS, COLS), jnp.int32),
            pltpu.SMEM(classes.shape, F32),
            pltpu.VMEM((TOUCH, OWN), jnp.int32),
            pltpu.VMEM((TOUCH, OWN), jnp.int32),
            pltpu.VMEM((SLOTS, COLS), BF16),
            pltpu.SemaphoreType.DMA((9,)),
        ],
        out_specs=(VMEM,) * 6 + (HBM,),
        flops=20_000_000, moved=2_000_000,
    )(*(far(x) for x in (classes, inflow, category, state, thermal, slots.T, strips.T, measured)))
    xa, xb = swapped((edge, edge), "gx")
    picker = exchange(request)
    own, cond, pa, pb = call(
        pack_body,
        (sds(2, WIDE, COLS), sds(2, WIDE, COLS), sds(2 * WIDE, COLS, dtype=BF16), sds(2 * WIDE, COLS, dtype=BF16)),
        [VMEM] * 4,
        "pack",
        flops=20_000_000_000, moved=1_500_000,
    )(held_state, conduct, xa, xb)
    ya, yb = swapped((pa, pb), "gy")
    tops, inner, inner_cond = call(
        tops_body,
        (sds(2, ROWS, COLS), sds(2, WIDE, COLS), sds(2, WIDE, COLS)),
        [VMEM] * 4,
        "tops",
        [pltpu.VMEM((STEPS + 2, WIDE, COLS), F32), pltpu.VMEM((4, WIDE, COLS), F32)],
        flops=20_000_000_000, moved=1_000_000,
    )(held_state, conduct, xa, xb)
    left, right, adjoint, bright = call(
        strip_body,
        (sds(ROWS, COLS), sds(ROWS, COLS), sds(ROWS, COLS), sds(COLS, COLS, dtype=BF16)),
        [VMEM] * 8,
        "strips",
        [pltpu.VMEM((6, WIDE, COLS), F32)] * 8,
        flops=10_000_000_000, moved=1_000_000,
    )(own, cond, inner, inner_cond, ya, yb, tops, warm)
    served = call(
        serve_body,
        sds(SLOTS, COLS, dtype=BF16),
        [VMEM] * 2,
        "serve",
        [pltpu.VMEM((SLOTS, COLS), BF16), pltpu.SemaphoreType.DMA((2,))],
        out_specs=HBM,
        flops=20_000_000, moved=300_000,
    )(picker, bright)
    returned = exchange(served)
    scratch = [
        pltpu.VMEM((HALF + STEPS, WIDE, COLS), F32),
        pltpu.VMEM((4, WIDE, COLS), F32),
        pltpu.VMEM((HALF, ROWS, COLS), F32),
        pltpu.SemaphoreType.DMA((HALF // PIECE,)),
    ]
    begun, near, picker_across = call(
        upper_body,
        (
            sds(L, ROWS, COLS), sds(NEAR, TOUCH, FOOT, COLS, dtype=BF16), sds(COLS, SLOTS, dtype=BF16)
        ),
        [VMEM] * 7 + [HBM],
        "upper",
        scratch + [pltpu.SemaphoreType.DMA],
        out_specs=(HBM, VMEM, VMEM),
        flops=500_000_000, moved=3_000_000,
    )(held_state, conduct, xa, xb, left, right, picker, far(weights))
    brightness, outgoing = call(
        foot_body,
        (sds(OWN, FOOT), sds(SLOTS, COLS, dtype=BF16)),
        [VMEM] * 4 + [HBM],
        "footprints",
        [
            pltpu.VMEM((REFS, COLS), F32),
            pltpu.VMEM((REFS, COLS), F32),
            pltpu.VMEM(weights.shape, BF16),
            pltpu.SemaphoreType.DMA((len(CHUNKS),)),
            pltpu.VMEM((SLOTS, COLS), BF16),
            pltpu.SemaphoreType.DMA((2,)),
        ],
        out_specs=(VMEM, HBM),
        flops=20_000_000, moved=5_000_000,
    )(returned, placing, seen, near, far(weights))
    moisture = call(
        lower_body,
        sds(L, ROWS, COLS),
        [HBM] + [VMEM] * 5 + [HBM],
        "lower",
        scratch + [pltpu.VMEM((L, ROWS, COLS), F32), pltpu.SemaphoreType.DMA],
        out_specs=HBM,
        aliases={6: 0},
        flops=500_000_000, moved=3_000_000,
    )(far(state), conduct, xa, xb, left, right, begun)
    grads = exchange(outgoing)
    grad_top = call(
        gradient_body, sds(2, ROWS, COLS), [VMEM] * 3, "gradient", flops=20_000_000, moved=400_000
    )(grads, picker_across, adjoint)
    return moisture, brightness, grad_top


def solution(mesh):
    placed = (
        P(None, "gx", "gy"),
        P("gx", "gy"),
        P(),
        P("gx", "gy"),
        P("gx", "gy"),
        P(("gx", "gy"), None, None, None),
        P(("gx", "gy"), None),
        P(("gx", "gy"), None),
        P(("gx", "gy"), None),
    )
    return jax.shard_map(
        on_device,
        mesh=mesh,
        in_specs=placed,
        out_specs=(P(None, "gx", "gy"), P(("gx", "gy"), None), P(None, "gx", "gy")),
        check_vma=False,
    )
```
